128 devices in a mesh: wide: 32 (over x, z_hi, y), narrow: 4 (over z_lo, core).
Axes of the slice: x: 4, y: 4, z: 4 (z_hi: 2, z_lo: 2; z = z_hi * 2 + z_lo), core: 2. Of those that a mesh axis runs over, the one named last changes fastest.
Arguments:
- cube: bfloat16 [16384, 4, 6144], P(('wide', 'narrow')), may hold values from -70 to 70, as said below
- flags: int32 [1024], P(('wide', 'narrow')), may hold values 0 or 1
- line_gain: float32 [8193], replicated, may hold values from 0 to 1
- beam_width: float32 [16384], P(('wide', 'narrow')), may hold values from 1 to 3
Outputs:
- restored: bfloat16 [16384, 4, 6144], P(('wide', 'narrow'))
- continuum: float32 [6, 24576], P(None, ('wide', 'narrow'))
The draws below stay inside these ranges and needn't reach their ends.
Inputs may be any that keep to these rules, and one draw needn't show every extreme that they name: `cube`: continuum polynomial plus noise per pixel.
All inputs are finite; a program needn't handle non-finite values. No bound on the sum of `flags` on one device may be relied on, other than what follows from the above.
Results may differ from the reference program's by a relative error of at most 0.0049.
Values may be sent and summed in bfloat16 or wider, within the bound.
A program may use at most 192 MiB of HBM per device.

```python
import math
import jax
import jax.numpy as jnp
from jax import lax

NCHAN = 16384
NPIX = 6144
ROWS = 4
NBASIS = 6
HALF = 8
FLAGBLK = 16
NFLAG = 1024
NBIN = 8193


def draw_cube(key, part):
    key = jax.random.fold_in(key, 11)
    key_amps, key_noise = jax.random.split(key, 2)
    x = (2.0 * jnp.arange(NCHAN, dtype=jnp.float32) + 1.0) / NCHAN - 1.0
    terms = [jnp.ones_like(x), x]
    for k in range(1, NBASIS - 1):
        terms.append(((2 * k + 1) * x * terms[k] - k * terms[k - 1]) / (k + 1))
    levels = jnp.array([2.0, 1.0, 0.8, 0.6, 0.5, 0.4], jnp.float32)[:NBASIS]
    amps = jnp.clip(jax.random.normal(key_amps, (NBASIS, ROWS, NPIX), jnp.float32), -3.0, 3.0) * levels[:, None, None]
    noise = jnp.clip(jax.random.normal(key_noise, (NCHAN, ROWS, NPIX), jnp.float32), -5.0, 5.0)
    total = noise
    for k in range(NBASIS):
        total = total + terms[k][:, None, None] * amps[k][None, :, :]
    return total.astype(jnp.bfloat16)


def touch_ends(values, key, least, high):
    shape = values.shape
    spot = [jax.random.randint(jax.random.fold_in(key, axis), (), 0, shape[axis]) for axis in range(len(shape))]
    values = values.at[tuple(spot)].set(least)
    longest = shape.index(max(shape))
    spot[longest] = (spot[longest] + 1) % shape[longest]
    return values.at[tuple(spot)].set(high)


def shard_levels(own_key, shape, cuts, least, high):
    def one(position, parts):
        heights = jax.random.uniform(jax.random.fold_in(jax.random.fold_in(own_key, 6), position), (parts,), jnp.float32, least / len(cuts), high / len(cuts))
        return jnp.repeat(jnp.exp(heights), shape[position] // parts).reshape((-1,) + (1,) * (len(shape) - position - 1))

    loudness = one(*cuts[0])
    for cut in cuts[1:]:
        loudness = loudness * one(*cut)
    return loudness


def setup_inputs(seed: int = 0) -> dict:
    key_of = jax.random.split(jax.random.key(seed), 5)
    cube = draw_cube(jax.random.fold_in(key_of[4], 71), 0)
    flags = touch_ends((jax.random.randint(key_of[1], (NFLAG,), 0, 8) < 1).astype(jnp.int32), jax.random.fold_in(key_of[1], 1), 0, 1)
    line_gain = jnp.clip(jax.random.uniform(key_of[2], (NBIN,), jnp.float32, 0.0, 1.0), 0.0, 1.0)
    beam_width = jnp.clip(jnp.exp(math.log(3.0) - 1.0986123 * jax.random.uniform(key_of[3], (NCHAN,), jnp.float32) ** shard_levels(key_of[3], (NCHAN,), ((0, 128),), -0.2, 0.2)), 1.0, 3.0)
    return {"cube": cube, "flags": flags, "line_gain": line_gain, "beam_width": beam_width}


def legendre(count):
    x = (2.0 * jnp.arange(count, dtype=jnp.float32) + 1.0) / count - 1.0
    terms = [jnp.ones_like(x), x]
    for k in range(1, NBASIS - 1):
        terms.append(((2 * k + 1) * x * terms[k] - k * terms[k - 1]) / (k + 1))
    return jnp.stack(terms[:NBASIS])

def make_taps(widths):
    offsets = jnp.arange(2 * HALF + 1, dtype=jnp.float32) - HALF
    raw = jnp.exp(-offsets[None, :] ** 2 / (2.0 * widths[:, None] ** 2))
    return raw / jnp.sum(raw, axis=1, keepdims=True)

def small_solve(factor, moments):
    count = factor.shape[0]
    inner = []
    for i in range(count):
        value = moments[i]
        for j in range(i):
            value = value - factor[i, j] * inner[j]
        inner.append(value / factor[i, i])
    result = [None] * count
    for i in reversed(range(count)):
        value = inner[i]
        for j in range(i + 1, count):
            value = value - factor[j, i] * result[j]
        result[i] = value / factor[i, i]
    return jnp.stack(result)

def reference(cube, flags, line_gain, beam_width):
    basis = legendre(NCHAN)
    weight = 1.0 - jnp.repeat(flags, FLAGBLK).astype(jnp.float32)
    wbasis = basis * weight[None, :]
    gram = jnp.dot(wbasis, basis.T, precision=lax.Precision.HIGHEST)
    factor = jnp.linalg.cholesky(gram)
    taps = make_taps(beam_width)

    def one_row(row):
        y_data = row.astype(jnp.float32)
        moments = jnp.dot(wbasis, y_data, precision=lax.Precision.HIGHEST)
        coeffs = small_solve(factor, moments)
        smooth = jnp.dot(basis.T, coeffs, precision=lax.Precision.HIGHEST)
        residual = weight[:, None] * (y_data - smooth)
        spectrum = jnp.fft.rfft(residual, axis=0) * line_gain[:, None]
        filtered = jnp.fft.irfft(spectrum, n=NCHAN, axis=0).astype(jnp.bfloat16)
        padded = jnp.pad(filtered, ((0, 0), (HALF, HALF)))
        total = jnp.zeros((NCHAN, NPIX), jnp.float32)
        for j in range(2 * HALF + 1):
            total = total + taps[:, j:j + 1] * padded[:, j:j + NPIX]
        return (total.astype(jnp.bfloat16), coeffs)
    restored, coeffs = lax.map(one_row, jnp.moveaxis(cube, 1, 0))
    continuum = jnp.transpose(coeffs, (1, 0, 2)).reshape(NBASIS, ROWS * NPIX)
    return (jnp.moveaxis(restored, 0, 1), continuum)
```

```python
import functools
import math

import jax
import jax.numpy as jnp
import numpy as np
from jax import lax
from jax.experimental import pallas as pl
from jax.experimental.pallas import tpu as pltpu
from jax.sharding import PartitionSpec as P

NDEV = 128
NBASIS = 6
HALF = 8
FLAGBLK = 16
ROWS = 4
NPIX = 6144
NCHAN = 16384
SIDE = 128
HROWS = 72
OWN = NPIX // NDEV
GROUP = 16
FLAGGED = 128.0
LIMIT = 100.0
BF = jnp.bfloat16
F32 = jnp.float32
VMEM_BYTES = 56 * 1024 * 1024
AXES = ("wide", "narrow")


def split3(x):
    hi = x.astype(BF)
    rest = x - hi.astype(np.float64)
    lo = rest.astype(BF)
    return hi, lo, (rest - lo.astype(np.float64)).astype(BF)


def legendre64(x):
    terms = [np.ones_like(x), x]
    for k in range(1, NBASIS - 1):
        terms.append(((2 * k + 1) * x * terms[k] - k * terms[k - 1]) / (k + 1))
    return np.stack(terms[:NBASIS])


@functools.cache
def tables():
    idx = np.arange(SIDE)
    turn = 2.0 * np.pi / SIDE
    half = SIDE // 2 + 1
    cos = np.cos(turn * (np.outer(idx, idx) % SIDE))
    sin = np.sin(turn * (np.outer(idx, idx) % SIDE))
    first = np.zeros((2 * HROWS, SIDE))
    first[:half] = cos[:half]
    first[HROWS : HROWS + half] = -sin[:half]
    plain = first.astype(np.float32)
    slow = legendre64((2.0 * idx + 1.0) / SIDE - 1.0)
    first[half : half + NBASIS] = slow
    fa_hi, fa_lo, fa_rest = split3(first)
    fa_hi = fa_hi.copy()
    fa_hi[HROWS + half : HROWS + half + NBASIS] = fa_rest[half : half + NBASIS]
    chan = np.arange(NCHAN)
    full = legendre64((2.0 * chan + 1.0) / NCHAN - 1.0).reshape(NBASIS, SIDE, SIDE)
    fit = np.linalg.pinv(slow.T)
    mix = np.einsum("ma,kab->kmb", fit, full)
    mix = np.where(np.arange(NBASIS)[None, :, None] <= np.arange(NBASIS)[:, None, None], mix, 0.0)
    w2 = np.block([[cos, -sin], [sin, cos]])
    v2 = np.block([[cos, sin], [-sin, cos]])
    times = np.full((half,), 2.0)
    times[0] = times[-1] = 1.0
    last = np.zeros((SIDE, 2 * HROWS))
    last[:, :half] = cos[:, :half] * times
    last[:, HROWS : HROWS + half] = -sin[:, :half] * times
    tc = np.zeros((HROWS, SIDE))
    ts = np.zeros((HROWS, SIDE))
    tc[:half] = np.cos(2.0 * np.pi / NCHAN * np.outer(idx[:half], idx))
    ts[:half] = np.sin(2.0 * np.pi / NCHAN * np.outer(idx[:half], idx))
    w_hi, w_lo, _ = split3(w2)
    v_hi, v_lo, _ = split3(v2)
    l_hi, l_lo, _ = split3(last)
    f = np.float32
    return dict(
        fa=np.stack([fa_hi, fa_lo]), plain=plain, full=full.astype(f), mix=mix.astype(f),
        w2=np.stack([w_hi, w_lo]), v2=np.stack([v_hi, v_lo]), last=np.stack([l_hi, l_lo]),
        tc=tc.astype(f), ts=ts.astype(f),
    )


def dot(a, b):
    return jnp.dot(a, b, preferred_element_type=F32)


def halves(x):
    hi = x.astype(BF)
    return hi, (x - hi.astype(F32)).astype(BF)


def dot_right(x, table):
    hi, lo = halves(x)
    return dot(hi, table[0]) + dot(lo, table[0]) + dot(hi, table[1])


def dot_left(table, x):
    hi, lo = halves(x)
    return dot(table[0], hi) + dot(table[0], lo) + dot(table[1], hi)


def unpack_group(src, start, xs):
    @pl.loop(0, SIDE // 8)
    def _(i):
        block = src[pl.ds(i * 8, 8), pl.ds(start, GROUP), :].astype(F32)
        xs[pl.ds(pl.multiple_of(i * 8 * GROUP, 128), 8 * GROUP), :] = block.reshape(8 * GROUP, SIDE)


def pack_group(dst, start, xs):
    @pl.loop(0, SIDE // 8)
    def _(i):
        block = xs[pl.ds(pl.multiple_of(i * 8 * GROUP, 128), 8 * GROUP), :]
        dst[pl.ds(i * 8, 8), pl.ds(start, GROUP), :] = block.reshape(8, GROUP, SIDE).astype(BF)


def fit_setup(xs, full, plain, fw, chol):
    weight = jnp.where(xs[pl.ds(0, SIDE, stride=GROUP), :] > LIMIT, 0.0, 1.0)
    gram = {}
    for i in range(NBASIS):
        weighted = full[i] * weight
        fw[i] = jnp.dot(plain[...], weighted, preferred_element_type=F32, precision=lax.Precision.HIGHEST)
        for j in range(i + 1):
            total = jnp.sum(jnp.sum(weighted * full[j], axis=0, keepdims=True), axis=1, keepdims=True)
            gram[i, j] = jnp.broadcast_to(total, (8, SIDE))
    factor = {}
    for j in range(NBASIS):
        value = gram[j, j]
        for k in range(j):
            value = value - factor[j, k] * factor[j, k]
        factor[j, j] = jnp.sqrt(value)
        for i in range(j + 1, NBASIS):
            value = gram[i, j]
            for k in range(j):
                value = value - factor[i, k] * factor[j, k]
            factor[i, j] = value / factor[j, j]
    for (i, j), value in factor.items():
        chol[i * NBASIS + j] = value


def fit_group(z, tt, mix, chol, cs):
    @pl.loop(0, GROUP)
    def _(p):
        tt[pl.ds(pl.multiple_of(p * 8, 8), 8), :] = z[p, 64:72, :] + z[p, 136:144, :]

    parts = [tt[pl.ds(m + 1, GROUP, stride=8), :] for m in range(NBASIS)]

    def entry(i, j):
        return jnp.broadcast_to(chol[i * NBASIS + j, 0:1, :], (GROUP, SIDE))

    inner = []
    for k in range(NBASIS):
        total = parts[0] * mix[k, 0:1, :]
        for m in range(1, k + 1):
            total = total + parts[m] * mix[k, m : m + 1, :]
        value = jnp.broadcast_to(jnp.sum(total, axis=1, keepdims=True), (GROUP, SIDE))
        for j in range(k):
            value = value - entry(k, j) * inner[j]
        inner.append(value / entry(k, k))
    result = [None] * NBASIS
    for i in reversed(range(NBASIS)):
        value = inner[i]
        for j in range(i + 1, NBASIS):
            value = value - entry(j, i) * result[j]
        result[i] = value / entry(i, i)
    lane = lax.broadcasted_iota(jnp.int32, (GROUP, SIDE), 1)
    shown = jnp.zeros((GROUP, SIDE), F32)
    for k in range(NBASIS):
        cs[k] = result[k]
        shown = jnp.where(lane == k, result[k], shown)
    return shown


def filter_group(xs, z, tt, cs, fa, w2, v2, last, tc, ts, gain, mix, fw, chol):
    @pl.loop(0, GROUP // 2)
    def _(i):
        both = [xs[pl.ds(2 * i + q, SIDE, stride=GROUP), :] for q in range(2)]
        x = jnp.concatenate([jnp.where(v > LIMIT, 0.0, v) for v in both], axis=1).astype(BF)
        res = dot(fa[0], x) + dot(fa[1], x)
        z[2 * i] = res[:, :SIDE]
        z[2 * i + 1] = res[:, SIDE:]

    shown = fit_group(z, tt, mix, chol, cs)
    quad = 4

    @pl.loop(0, GROUP // quad)
    def _(i):
        real, imag = [], []
        for q in range(quad):
            p = i * quad + q
            zr, zi = z[p, :HROWS, :], z[p, HROWS:, :]
            for k in range(NBASIS):
                coef = cs[k, pl.ds(p, 1), :]
                zr = zr - coef * fw[k, :HROWS, :]
                zi = zi - coef * fw[k, HROWS:, :]
            real.append(zr * tc[...] + zi * ts[...])
            imag.append(zi * tc[...] - zr * ts[...])
        u = jnp.concatenate([jnp.concatenate(real, axis=0), jnp.concatenate(imag, axis=0)], axis=1)
        x = dot_right(u, w2)
        g = jnp.concatenate([gain[...]] * quad, axis=0)
        x = x * jnp.concatenate([g, g], axis=1)
        v = dot_right(x, v2)
        cols = []
        for q in range(quad):
            vr, vi = v[q * HROWS : (q + 1) * HROWS, :SIDE], v[q * HROWS : (q + 1) * HROWS, SIDE:]
            cols.append(jnp.concatenate([vr * tc[...] - vi * ts[...], vi * tc[...] + vr * ts[...]], axis=0))
        out = dot_left(last, jnp.concatenate(cols, axis=1))
        for q in range(quad):
            xs[pl.ds(i * quad + q, SIDE, stride=GROUP), :] = out[:, q * SIDE : (q + 1) * SIDE]

    return shown


LANES = 512
PARTS = NPIX // LANES
TILES = NPIX // SIDE
TURN = 37


def place():
    wide, narrow = lax.axis_index("wide"), lax.axis_index("narrow")
    return wide, narrow, wide * 4 + narrow


def partner(i):
    wide, narrow, _ = place()
    s = i * TURN % NDEV
    x = (wide // 8 + s % 4) % 4
    y = (wide % 4 + s // 4 % 4) % 4
    z = (wide // 4 % 2 * 2 + narrow // 2 + s // 16 % 4) % 4
    core = (narrow % 2 + s // 64) % 2
    return (x * 2 + z // 2) * 4 + y, z % 2 * 2 + core


def columns(ref, row, device):
    return ref.at[row, pl.ds(pl.multiple_of(device * OWN, 16), OWN)]


def exchange(row, source, target, send_sem, recv_sem):
    @pl.loop(1, NDEV)
    def _(i):
        wide, narrow = partner(i)
        pltpu.make_async_remote_copy(
            src_ref=source(wide * 4 + narrow),
            dst_ref=target,
            send_sem=send_sem.at[row],
            recv_sem=recv_sem.at[row],
            device_id=(wide, narrow),
            device_id_type=pl.DeviceIdType.MESH,
        ).start()


def wait_all(row, buffer, sem):
    block = buffer.at[row, pl.ds(0, NDEV - 1)]
    pltpu.make_async_copy(block, block, sem.at[row]).wait()


def wait_rows(row, buffer, sem):
    block = buffer.at[row, pl.ds(0, (NDEV - 1) * OWN)]
    pltpu.make_async_copy(block, block, sem.at[row]).wait()


def relayout_in(cube_v, work, part):
    lanes = pl.ds(pl.multiple_of(part * LANES, LANES), LANES)
    for c in range(0, SIDE, 16):
        block = cube_v[pl.ds(c, 16), :, lanes].astype(F32).reshape(16 * ROWS, LANES)
        for q in range(LANES // SIDE):
            work[part * (LANES // SIDE) + q, pl.ds(c * ROWS, 16 * ROWS), :] = block[:, q * SIDE : (q + 1) * SIDE]


def relayout_out(cube_v, work, part):
    lanes = pl.ds(pl.multiple_of(part * LANES, LANES), LANES)
    for c in range(0, SIDE, 16):
        parts = [work[part * (LANES // SIDE) + q, pl.ds(c * ROWS, 16 * ROWS), :] for q in range(LANES // SIDE)]
        cube_v[pl.ds(c, 16), :, lanes] = jnp.concatenate(parts, axis=1).reshape(16, ROWS, LANES).astype(BF)


def turn_in(row, tile, work, marks, sent):
    block = work[tile, pl.ds(row, SIDE, stride=ROWS), :]
    turned = jnp.where(marks[...] > 0, FLAGGED, block.T)
    sent[row, pl.ds(pl.multiple_of(tile * SIDE, SIDE), SIDE), :] = turned.astype(BF)


def beam_start(row, back, padded):
    padded[0:HALF, :] = jnp.zeros((HALF, SIDE), F32)
    padded[HALF + NPIX : NPIX + 2 * HALF, :] = jnp.zeros((HALF, SIDE), F32)

    @pl.loop(0, TILES)
    def _(i):
        at = pl.multiple_of(i * SIDE, SIDE)
        padded[pl.ds(at + HALF, SIDE), :] = back[row, pl.ds(at, SIDE), :].astype(F32)


def beam_tile(row, tile, padded, taps, flat, work):
    at = tile * SIDE
    run = SIDE // 8
    values = [padded[pl.ds(at + t, 8, stride=run), :] for t in range(run + 2 * HALF)]
    for t in range(run):
        total = values[t + HALF] * taps[HALF]
        for j in range(HALF):
            total = total + (values[t + j] + values[t + 2 * HALF - j]) * taps[j]
        flat[pl.ds(t, 8, stride=run), :] = total
    work[tile, pl.ds(row, SIDE, stride=ROWS), :] = flat[...].T


def strip_kernel(
    cube, marks, gain, taps, fa, w2, v2, last, tc, ts, mix, full, plain, restored, continuum,
    cube_v, work, sent, got, back, padded, flat, xs, z, tt, cs, fw, chol, shown, gathered,
    in_sem, out_sem, go_send, go_recv, home_send, home_recv, own_sem, fit_send, fit_recv,
):
    my_wide, my_narrow, me = place()

    def cube_part(part):
        lanes = pl.ds(pl.multiple_of(part * LANES, LANES), LANES)
        return pltpu.make_async_copy(cube.at[:, :, lanes], cube_v.at[:, :, lanes], in_sem.at[part])

    def out_part(part):
        lanes = pl.ds(pl.multiple_of(part * LANES, LANES), LANES)
        return pltpu.make_async_copy(cube_v.at[:, :, lanes], restored.at[:, :, lanes], out_sem.at[part])

    def own_go(row):
        return pltpu.make_async_copy(columns(sent, row, me), got.at[row, me], own_sem.at[row])

    def own_home(row):
        return pltpu.make_async_copy(got.at[row, me], columns(back, row, me), own_sem.at[ROWS + row])

    @pl.loop(0, PARTS)
    def _(part):
        cube_part(part).start()

    @pl.loop(0, PARTS)
    def _(part):
        cube_part(part).wait()
        relayout_in(cube_v, work, part)
        for q in range(LANES // SIDE):
            turn_in(0, part * (LANES // SIDE) + q, work, marks, sent)

    for row in range(ROWS):
        if row > 0:
            @pl.loop(0, TILES, step=2)
            def _(tile):
                turn_in(row, tile, work, marks, sent)
                turn_in(row, tile + 1, work, marks, sent)

        own_go(row).start()
        exchange(row, lambda d: columns(sent, row, d), got.at[row, me], go_send, go_recv)

    def fit_target(row):
        return row * (NDEV // ROWS) + me // ROWS

    def fit_remote(row):
        dest = fit_target(row)
        return pltpu.make_async_remote_copy(
            src_ref=shown.at[row],
            dst_ref=gathered.at[me % ROWS],
            send_sem=fit_send.at[row],
            recv_sem=fit_recv.at[me % ROWS],
            device_id=(dest // 4, dest % 4),
            device_id_type=pl.DeviceIdType.MESH,
        )

    def fit_local(row):
        return pltpu.make_async_copy(shown.at[row], gathered.at[me % ROWS], fit_send.at[row])

    for row in range(ROWS):
        own_go(row).wait()
        wait_all(row, got, go_recv)
        rows = got.at[row]
        if row == 0:
            unpack_group(rows, 0, xs)
            fit_setup(xs, full, plain, fw, chol)

        @pl.loop(0, OWN // GROUP)
        def _(g):
            start = pl.multiple_of(g * GROUP, GROUP)
            unpack_group(rows, start, xs)
            shown[row, pl.ds(start, GROUP), :] = filter_group(
                xs, z, tt, cs, fa, w2, v2, last, tc, ts, gain, mix, fw, chol
            )
            pack_group(rows, start, xs)

        own_home(row).start()
        exchange(row, lambda d: got.at[row, d], columns(back, row, me), home_send, home_recv)
        dest = fit_target(row)

        @pl.when(dest != me)
        def _():
            fit_remote(row).start()

        @pl.when(dest == me)
        def _():
            fit_local(row).start()

    for row in range(ROWS):
        own_home(row).wait()
        wait_rows(row, back, home_recv)
        beam_start(row, back, padded)
        if row < ROWS - 1:
            @pl.loop(0, TILES)
            def _(tile):
                beam_tile(row, tile, padded, taps, flat, work)
        else:
            @pl.loop(0, PARTS)
            def _(part):
                for q in range(LANES // SIDE):
                    beam_tile(row, part * (LANES // SIDE) + q, padded, taps, flat, work)
                relayout_out(cube_v, work, part)
                out_part(part).start()

    for row in range(ROWS):
        dest = fit_target(row)

        @pl.when(dest != me)
        def _():
            fit_remote(row).wait_send()

        @pl.when(dest == me)
        def _():
            fit_local(row).wait()

    for slot in range(ROWS):
        source = me % (NDEV // ROWS) * ROWS + slot

        @pl.when(source != me)
        def _():
            block = gathered.at[slot]
            pltpu.make_async_copy(block, block, fit_recv.at[slot]).wait()

    for slot in range(ROWS):
        continuum[slot] = gathered[slot]
    for row in range(ROWS):
        wait_rows(row, sent, go_send)
        wait_all(row, got, home_send)

    @pl.loop(0, PARTS)
    def _(part):
        out_part(part).wait()


def params():
    return pltpu.CompilerParams(vmem_limit_bytes=VMEM_BYTES)


def whole(array):
    return pl.BlockSpec(array.shape, lambda *_: (0,) * array.ndim)


def make_taps(widths):
    offsets = jnp.arange(2 * HALF + 1, dtype=F32) - HALF
    raw = jnp.exp(-offsets[:, None] ** 2 / (2.0 * widths[None, :] ** 2))
    return raw / jnp.sum(raw, axis=0, keepdims=True)


def gain_table(line_gain):
    both = jnp.concatenate([line_gain, line_gain[1:-1][::-1]]) / NCHAN
    return both.reshape(SIDE, SIDE).T[:HROWS]


def body(cube, flags, line_gain, beam_width):
    tab = {k: jnp.asarray(v) for k, v in tables().items()}
    gain = gain_table(line_gain)
    taps = jnp.broadcast_to(make_taps(beam_width)[: HALF + 1, None, :], (HALF + 1, 8, SIDE))
    marks = jnp.repeat(flags, FLAGBLK)[None, :]
    names = ("fa", "w2", "v2", "last", "tc", "ts", "mix", "full", "plain")
    ins = [marks, gain, taps] + [tab[n] for n in names]
    dma = pltpu.SemaphoreType.DMA
    restored, coefs = pl.pallas_call(
        strip_kernel,
        in_specs=[pl.BlockSpec(memory_space=pl.ANY)] + [pl.BlockSpec(memory_space=pltpu.VMEM)] * len(ins),
        out_specs=[pl.BlockSpec(memory_space=pl.ANY), pl.BlockSpec(memory_space=pltpu.VMEM)],
        out_shape=[
            jax.ShapeDtypeStruct((SIDE, ROWS, NPIX), BF),
            jax.ShapeDtypeStruct((ROWS, OWN, SIDE), F32),
        ],
        scratch_shapes=[
            pltpu.VMEM((SIDE, ROWS, NPIX), BF),
            pltpu.VMEM((TILES, SIDE * ROWS, SIDE), F32),
            pltpu.VMEM((ROWS, NPIX, SIDE), BF),
            pltpu.VMEM((ROWS, NDEV, OWN, SIDE), BF),
            pltpu.VMEM((ROWS, NPIX, SIDE), BF),
            pltpu.VMEM((NPIX + 2 * HALF, SIDE), F32),
            pltpu.VMEM((SIDE, SIDE), F32),
            pltpu.VMEM((SIDE * GROUP, SIDE), F32),
            pltpu.VMEM((GROUP, 2 * HROWS, SIDE), F32),
            pltpu.VMEM((GROUP * 8, SIDE), F32),
            pltpu.VMEM((NBASIS, GROUP, SIDE), F32),
            pltpu.VMEM((NBASIS, 2 * HROWS, SIDE), F32),
            pltpu.VMEM((NBASIS * NBASIS, 8, SIDE), F32),
            pltpu.VMEM((ROWS, OWN, SIDE), F32),
            pltpu.VMEM((ROWS, OWN, SIDE), F32),
            dma((PARTS,)),
            dma((PARTS,)),
            dma((ROWS,)),
            dma((ROWS,)),
            dma((ROWS,)),
            dma((ROWS,)),
            dma((2 * ROWS,)),
            dma((ROWS,)),
            dma((ROWS,)),
        ],
        compiler_params=pltpu.CompilerParams(vmem_limit_bytes=VMEM_BYTES, has_side_effects=True),
    )(cube, *ins)
    continuum = coefs.reshape(ROWS * OWN, SIDE)[:, :NBASIS].T
    return (restored, continuum)


def solution(mesh):
    placed = (P(AXES, None, None), P(AXES), P(), P(AXES))
    return jax.shard_map(
        body,
        mesh=mesh,
        in_specs=placed,
        out_specs=(P(AXES, None, None), P(None, AXES)),
        check_vma=False,
    )
```

```python
import functools
import math

import jax
import jax.numpy as jnp
import numpy as np
from jax import lax
from jax.experimental import pallas as pl
from jax.experimental.pallas import tpu as pltpu
from jax.sharding import PartitionSpec as P

NDEV = 128
NBASIS = 6
HALF = 8
FLAGBLK = 16
ROWS = 4
NPIX = 6144
NCHAN = 16384
SIDE = 128
HROWS = 72
OWN = NPIX // NDEV
GROUP = 16
FLAGGED = 128.0
LIMIT = 100.0
BF = jnp.bfloat16
F32 = jnp.float32
VMEM_BYTES = 56 * 1024 * 1024
AXES = ("wide", "narrow")


def split3(x):
    hi = x.astype(BF)
    rest = x - hi.astype(np.float64)
    lo = rest.astype(BF)
    return hi, lo, (rest - lo.astype(np.float64)).astype(BF)


def legendre64(x):
    terms = [np.ones_like(x), x]
    for k in range(1, NBASIS - 1):
        terms.append(((2 * k + 1) * x * terms[k] - k * terms[k - 1]) / (k + 1))
    return np.stack(terms[:NBASIS])


@functools.cache
def tables():
    idx = np.arange(SIDE)
    turn = 2.0 * np.pi / SIDE
    half = SIDE // 2 + 1
    cos = np.cos(turn * (np.outer(idx, idx) % SIDE))
    sin = np.sin(turn * (np.outer(idx, idx) % SIDE))
    first = np.zeros((2 * HROWS, SIDE))
    first[:half] = cos[:half]
    first[HROWS : HROWS + half] = -sin[:half]
    plain = first.astype(np.float32)
    slow = legendre64((2.0 * idx + 1.0) / SIDE - 1.0)
    first[half : half + NBASIS] = slow
    fa_hi, fa_lo, fa_rest = split3(first)
    fa_hi = fa_hi.copy()
    fa_hi[HROWS + half : HROWS + half + NBASIS] = fa_rest[half : half + NBASIS]
    chan = np.arange(NCHAN)
    full = legendre64((2.0 * chan + 1.0) / NCHAN - 1.0).reshape(NBASIS, SIDE, SIDE)
    fit = np.linalg.pinv(slow.T)
    mix = np.einsum("ma,kab->kmb", fit, full)
    mix = np.where(np.arange(NBASIS)[None, :, None] <= np.arange(NBASIS)[:, None, None], mix, 0.0)
    w2 = np.block([[cos, -sin], [sin, cos]])
    v2 = np.block([[cos, sin], [-sin, cos]])
    times = np.full((half,), 2.0)
    times[0] = times[-1] = 1.0
    last = np.zeros((SIDE, 2 * HROWS))
    last[:, :half] = cos[:, :half] * times
    last[:, HROWS : HROWS + half] = -sin[:, :half] * times
    tc = np.zeros((HROWS, SIDE))
    ts = np.zeros((HROWS, SIDE))
    tc[:half] = np.cos(2.0 * np.pi / NCHAN * np.outer(idx[:half], idx))
    ts[:half] = np.sin(2.0 * np.pi / NCHAN * np.outer(idx[:half], idx))
    w_hi, w_lo, _ = split3(w2)
    v_hi, v_lo, _ = split3(v2)
    l_hi, l_lo, _ = split3(last)
    f = np.float32
    return dict(
        fa=np.concatenate([fa_hi, fa_lo], axis=1), plain=plain, full=full.astype(f), mix=mix.astype(f),
        w2=np.stack([w_hi, w_lo]), v2=np.stack([v_hi, v_lo]), last=np.concatenate([l_hi, l_lo, l_hi], axis=1),
        tc=tc.astype(f), ts=ts.astype(f),
    )


def dot(a, b):
    return jnp.dot(a, b, preferred_element_type=F32)


def halves(x):
    hi = x.astype(BF)
    return hi, (x - hi.astype(F32)).astype(BF)


def dot_right(x, table):
    hi, lo = halves(x)
    return dot(hi, table[0]) + dot(lo, table[0]) + dot(hi, table[1])


def dot_left(table, x):
    hi, lo = halves(x)
    return dot(table[...], jnp.concatenate([hi, hi, lo], axis=0))


def unpack_group(src, start, xs):
    @pl.loop(0, SIDE // 8)
    def _(i):
        block = src[pl.ds(i * 8, 8), pl.ds(start, GROUP), :].astype(F32)
        xs[pl.ds(pl.multiple_of(i * 8 * GROUP, 128), 8 * GROUP), :] = block.reshape(8 * GROUP, SIDE)


def pack_group(dst, start, xs):
    @pl.loop(0, SIDE // 8)
    def _(i):
        block = xs[pl.ds(pl.multiple_of(i * 8 * GROUP, 128), 8 * GROUP), :]
        dst[pl.ds(i * 8, 8), pl.ds(start, GROUP), :] = block.reshape(8, GROUP, SIDE).astype(BF)


def fit_setup(xs, full, plain, fw, chol):
    weight = jnp.where(xs[pl.ds(0, SIDE, stride=GROUP), :] > LIMIT, 0.0, 1.0)
    gram = {}
    for i in range(NBASIS):
        weighted = full[i] * weight
        fw[i] = jnp.dot(plain[...], weighted, preferred_element_type=F32, precision=lax.Precision.HIGHEST)
        for j in range(i + 1):
            total = jnp.sum(jnp.sum(weighted * full[j], axis=0, keepdims=True), axis=1, keepdims=True)
            gram[i, j] = jnp.broadcast_to(total, (8, SIDE))
    factor = {}
    for j in range(NBASIS):
        value = gram[j, j]
        for k in range(j):
            value = value - factor[j, k] * factor[j, k]
        factor[j, j] = jnp.sqrt(value)
        for i in range(j + 1, NBASIS):
            value = gram[i, j]
            for k in range(j):
                value = value - factor[i, k] * factor[j, k]
            factor[i, j] = value / factor[j, j]
    for (i, j), value in factor.items():
        chol[i * NBASIS + j] = value


def fit_group(z, tt, mix, chol, cs):
    @pl.loop(0, GROUP)
    def _(p):
        tt[pl.ds(pl.multiple_of(p * 8, 8), 8), :] = z[p, 64:72, :] + z[p, 136:144, :]

    parts = [tt[pl.ds(m + 1, GROUP, stride=8), :] for m in range(NBASIS)]

    def entry(i, j):
        return jnp.broadcast_to(chol[i * NBASIS + j, 0:1, :], (GROUP, SIDE))

    inner = []
    for k in range(NBASIS):
        total = parts[0] * mix[k, 0:1, :]
        for m in range(1, k + 1):
            total = total + parts[m] * mix[k, m : m + 1, :]
        value = jnp.broadcast_to(jnp.sum(total, axis=1, keepdims=True), (GROUP, SIDE))
        for j in range(k):
            value = value - entry(k, j) * inner[j]
        inner.append(value / entry(k, k))
    result = [None] * NBASIS
    for i in reversed(range(NBASIS)):
        value = inner[i]
        for j in range(i + 1, NBASIS):
            value = value - entry(j, i) * result[j]
        result[i] = value / entry(i, i)
    lane = lax.broadcasted_iota(jnp.int32, (GROUP, SIDE), 1)
    shown = jnp.zeros((GROUP, SIDE), F32)
    for k in range(NBASIS):
        cs[k] = result[k]
        shown = jnp.where(lane == k, result[k], shown)
    return shown


def filter_group(xs, z, tt, cs, fa, w2, v2, last, tc, ts, gain, mix, fw, chol):
    @pl.loop(0, GROUP // 2)
    def _(i):
        both = [xs[pl.ds(2 * i + q, SIDE, stride=GROUP), :] for q in range(2)]
        x = jnp.concatenate([jnp.where(v > LIMIT, 0.0, v) for v in both], axis=1).astype(BF)
        res = dot(fa[...], jnp.concatenate([x, x], axis=0))
        z[2 * i] = res[:, :SIDE]
        z[2 * i + 1] = res[:, SIDE:]

    shown = fit_group(z, tt, mix, chol, cs)
    quad = 4

    @pl.loop(0, GROUP // quad)
    def _(i):
        real, imag = [], []
        for q in range(quad):
            p = i * quad + q
            zr, zi = z[p, :HROWS, :], z[p, HROWS:, :]
            for k in range(NBASIS):
                coef = cs[k, pl.ds(p, 1), :]
                zr = zr - coef * fw[k, :HROWS, :]
                zi = zi - coef * fw[k, HROWS:, :]
            real.append(zr * tc[...] + zi * ts[...])
            imag.append(zi * tc[...] - zr * ts[...])
        u = jnp.concatenate([jnp.concatenate(real, axis=0), jnp.concatenate(imag, axis=0)], axis=1)
        x = dot_right(u, w2)
        g = jnp.concatenate([gain[...]] * quad, axis=0)
        x = x * jnp.concatenate([g, g], axis=1)
        v = dot_right(x, v2)
        cols = []
        for q in range(quad):
            vr, vi = v[q * HROWS : (q + 1) * HROWS, :SIDE], v[q * HROWS : (q + 1) * HROWS, SIDE:]
            cols.append(jnp.concatenate([vr * tc[...] - vi * ts[...], vi * tc[...] + vr * ts[...]], axis=0))
        out = dot_left(last, jnp.concatenate(cols, axis=1))
        for q in range(quad):
            xs[pl.ds(i * quad + q, SIDE, stride=GROUP), :] = out[:, q * SIDE : (q + 1) * SIDE]

    return shown


LANES = 512
PARTS = NPIX // LANES
TILES = NPIX // SIDE
SLOTS = 4
PER = LANES // SIDE


def place():
    wide, narrow = lax.axis_index("wide"), lax.axis_index("narrow")
    return wide, narrow, wide * 4 + narrow


def partner(i, j):
    wide, narrow, _ = place()
    x, y = lax.div(wide, 8), lax.rem(wide, 4)
    z = lax.rem(lax.div(wide, 4), 2) * 2 + lax.div(narrow, 2)
    x = lax.rem(x + i + j, 4)
    y = lax.rem(y + i // 4 + j // 2 if isinstance(i, int) else y + lax.div(i, 4) + j // 2, 4)
    z = lax.rem(z + j % 4, 4)
    core = lax.rem(lax.rem(narrow, 2) + j // 4, 2)
    return (x * 2 + lax.div(z, 2)) * 4 + y, lax.rem(z, 2) * 2 + core


def columns(ref, row, device):
    return ref.at[row, pl.ds(pl.multiple_of(device * OWN, 16), OWN)]


def exchange(row, source, target, send_sem, recv_sem):
    def send(i, j):
        wide, narrow = partner(i, j)
        pltpu.make_async_remote_copy(
            src_ref=source(wide * 4 + narrow),
            dst_ref=target,
            send_sem=send_sem.at[row],
            recv_sem=recv_sem.at[row],
            device_id=(wide, narrow),
            device_id_type=pl.DeviceIdType.MESH,
        ).start()

    @pl.loop(1, 16)
    def _(i):
        for j in range(8):
            send(i, j)

    for j in range(1, 8):
        send(0, j)


def wait_all(row, buffer, sem):
    block = buffer.at[row, pl.ds(0, NDEV - 1)]
    pltpu.make_async_copy(block, block, sem.at[row]).wait()


def wait_rows(row, buffer, sem):
    block = buffer.at[row, pl.ds(0, (NDEV - 1) * OWN)]
    pltpu.make_async_copy(block, block, sem.at[row]).wait()


def relayout_in(cube_v, slot, work, part):
    for c in range(0, SIDE, 16):
        block = cube_v[slot, pl.ds(c, 16), :, :].astype(F32).reshape(16 * ROWS, LANES)
        for q in range(PER):
            work[part * PER + q, pl.ds(c * ROWS, 16 * ROWS), :] = block[:, q * SIDE : (q + 1) * SIDE]


def turn_in(row, tile, work, marks, sent):
    block = work[tile, pl.ds(row, SIDE, stride=ROWS), :]
    turned = jnp.where(marks[0:1, :] > 0.0, FLAGGED, block.T)
    sent[row, pl.ds(pl.multiple_of(tile * SIDE, SIDE), SIDE), :] = turned.astype(BF)


def make_marks(flags, marks):
    lane = lax.broadcasted_iota(jnp.int32, (8, SIDE), 1)
    value = jnp.zeros((8, SIDE), F32)
    for f in range(SIDE // FLAGBLK):
        inside = (lane >= f * FLAGBLK) & (lane < (f + 1) * FLAGBLK)
        value = jnp.where(inside, flags[f].astype(F32), value)
    marks[...] = value


def make_taps(width, taps):
    w = jnp.broadcast_to(width[...], (8, SIDE))
    raw = [jnp.exp(-float((HALF - j) ** 2) / (2.0 * w * w)) for j in range(HALF + 1)]
    total = raw[HALF]
    for j in range(HALF):
        total = total + 2.0 * raw[j]
    for j in range(HALF + 1):
        taps[j] = raw[j] / total


def make_gain(line, gain):
    half = SIDE // 2

    def exact(a, b):
        return jnp.dot(a, b, preferred_element_type=F32, precision=lax.Precision.HIGHEST)

    low = line[...]
    row = lax.broadcasted_iota(jnp.int32, (half, HROWS), 0)
    col = lax.broadcasted_iota(jnp.int32, (half, HROWS), 1)
    first = lax.broadcasted_iota(jnp.int32, (SIDE, SIDE), 0)
    second = lax.broadcasted_iota(jnp.int32, (SIDE, SIDE), 1)
    turned = exact(jnp.where(row + col == half - 1, 1.0, 0.0), low)
    mirror = exact(turned, jnp.where(first + second == SIDE, 1.0, 0.0))
    edge = exact(jnp.where(row + col == half, 1.0, 0.0), low)
    lane = lax.broadcasted_iota(jnp.int32, (half, SIDE), 1)
    high = jnp.where(lane == 0, edge, mirror)
    gain[...] = jnp.concatenate([low[:half], high], axis=0).T[:HROWS] * (1.0 / NCHAN)


def beam_start(row, back, padded):
    padded[0:HALF, :] = jnp.zeros((HALF, SIDE), F32)
    padded[HALF + NPIX : NPIX + 2 * HALF, :] = jnp.zeros((HALF, SIDE), F32)

    @pl.loop(0, TILES)
    def _(i):
        at = pl.multiple_of(i * SIDE, SIDE)
        padded[pl.ds(at + HALF, SIDE), :] = back[row, pl.ds(at, SIDE), :].astype(F32)


def beam_tile(row, tile, padded, taps, flat, work):
    at = tile * SIDE
    run = SIDE // 8
    values = [padded[pl.ds(at + t, 8, stride=run), :] for t in range(run + 2 * HALF)]
    for t in range(run):
        total = values[t + HALF] * taps[HALF]
        for j in range(HALF):
            total = total + (values[t + j] + values[t + 2 * HALF - j]) * taps[j]
        flat[pl.ds(t, 8, stride=run), :] = total
    work[tile, pl.ds(row, SIDE, stride=ROWS), :] = flat[...].T


def strip_kernel(
    cube, flags, line, width, fa, w2, v2, last, tc, ts, mix, full, plain, tiles, continuum,
    cube_v, work, sent, got, back, padded, flat, leave, marks, taps, gain, xs, z, tt, cs, fw, chol, shown, gathered,
    in_sem, out_sem, go_send, go_recv, home_send, home_recv, own_sem, fit_send, fit_recv,
):
    my_wide, my_narrow, me = place()

    def cube_part(part):
        lanes = pl.ds(pl.multiple_of(part * LANES, LANES), LANES)
        slot = lax.rem(part, SLOTS)
        return pltpu.make_async_copy(cube.at[:, :, lanes], cube_v.at[slot], in_sem.at[slot])

    def out_part(part):
        slot = lax.rem(part, 2)
        target = tiles.at[pl.ds(part * PER, PER)]
        return pltpu.make_async_copy(leave.at[slot], target, out_sem.at[slot])

    def own_go(row):
        return pltpu.make_async_copy(columns(sent, row, me), got.at[row, me], own_sem.at[row])

    def own_home(row):
        return pltpu.make_async_copy(got.at[row, me], columns(back, row, me), own_sem.at[ROWS + row])

    @pl.loop(0, SLOTS)
    def _(part):
        cube_part(part).start()

    make_marks(flags, marks)

    @pl.loop(0, PARTS)
    def _(part):
        cube_part(part).wait()
        relayout_in(cube_v, lax.rem(part, SLOTS), work, part)

        @pl.when(part + SLOTS < PARTS)
        def _():
            cube_part(part + SLOTS).start()

        for q in range(PER):
            turn_in(0, part * PER + q, work, marks, sent)

    for row in range(ROWS):
        if row > 0:
            @pl.loop(0, TILES, step=2)
            def _(tile):
                turn_in(row, tile, work, marks, sent)
                turn_in(row, tile + 1, work, marks, sent)

        own_go(row).start()
        exchange(row, lambda d: columns(sent, row, d), got.at[row, me], go_send, go_recv)

    make_gain(line, gain)
    make_taps(width, taps)

    def fit_target(row):
        return row * (NDEV // ROWS) + me // ROWS

    def fit_remote(row):
        dest = fit_target(row)
        return pltpu.make_async_remote_copy(
            src_ref=shown.at[row],
            dst_ref=gathered.at[me % ROWS],
            send_sem=fit_send.at[row],
            recv_sem=fit_recv.at[me % ROWS],
            device_id=(dest // 4, dest % 4),
            device_id_type=pl.DeviceIdType.MESH,
        )

    def fit_local(row):
        return pltpu.make_async_copy(shown.at[row], gathered.at[me % ROWS], fit_send.at[row])

    for row in range(ROWS):
        own_go(row).wait()
        wait_all(row, got, go_recv)
        rows = got.at[row]
        if row == 0:
            unpack_group(rows, 0, xs)
            fit_setup(xs, full, plain, fw, chol)

        @pl.loop(0, OWN // GROUP)
        def _(g):
            start = pl.multiple_of(g * GROUP, GROUP)
            unpack_group(rows, start, xs)
            shown[row, pl.ds(start, GROUP), :] = filter_group(
                xs, z, tt, cs, fa, w2, v2, last, tc, ts, gain, mix, fw, chol
            )
            pack_group(rows, start, xs)

        own_home(row).start()
        exchange(row, lambda d: got.at[row, d], columns(back, row, me), home_send, home_recv)
        dest = fit_target(row)

        @pl.when(dest != me)
        def _():
            fit_remote(row).start()

        @pl.when(dest == me)
        def _():
            fit_local(row).start()

    for row in range(ROWS):
        own_home(row).wait()
        wait_rows(row, back, home_recv)
        beam_start(row, back, padded)
        if row < ROWS - 1:
            @pl.loop(0, TILES)
            def _(tile):
                beam_tile(row, tile, padded, taps, flat, work)
        else:
            @pl.loop(0, PARTS)
            def _(part):
                for q in range(PER):
                    beam_tile(row, part * PER + q, padded, taps, flat, work)

                @pl.when(part >= 2)
                def _():
                    out_part(part - 2).wait()

                for q in range(PER):
                    leave[lax.rem(part, 2), q] = work[part * PER + q].astype(BF)
                out_part(part).start()

    for row in range(ROWS):
        dest = fit_target(row)

        @pl.when(dest != me)
        def _():
            fit_remote(row).wait_send()

        @pl.when(dest == me)
        def _():
            fit_local(row).wait()

    for slot in range(ROWS):
        source = me % (NDEV // ROWS) * ROWS + slot

        @pl.when(source != me)
        def _():
            block = gathered.at[slot]
            pltpu.make_async_copy(block, block, fit_recv.at[slot]).wait()

    for slot in range(ROWS):
        continuum[slot * OWN : (slot + 1) * OWN, :] = gathered[slot]
    continuum[ROWS * OWN :, :] = jnp.zeros((2 * SIDE - ROWS * OWN, SIDE), F32)
    for row in range(ROWS):
        wait_rows(row, sent, go_send)
        wait_all(row, got, home_send)

    for part in (PARTS - 2, PARTS - 1):
        out_part(part).wait()


def leave_kernel(tiles, coefs, restored, continuum):
    for c in range(0, SIDE, 16):
        parts = [tiles[q, pl.ds(c * ROWS, 16 * ROWS), :].astype(F32) for q in range(PER)]
        restored[pl.ds(c, 16), :, :] = jnp.concatenate(parts, axis=1).reshape(16, ROWS, LANES).astype(BF)
    continuum[...] = coefs[...].T[:NBASIS, : ROWS * OWN]


def params(**more):
    return pltpu.CompilerParams(vmem_limit_bytes=VMEM_BYTES, **more)


def body(cube, flags, line_gain, beam_width):
    tab = {k: jnp.asarray(v) for k, v in tables().items()}
    line = jnp.pad(line_gain, (0, HROWS * SIDE - line_gain.shape[0])).reshape(HROWS, SIDE)
    names = ("fa", "w2", "v2", "last", "tc", "ts", "mix", "full", "plain")
    ins = [line, beam_width[None, :]] + [tab[n] for n in names]
    dma = pltpu.SemaphoreType.DMA
    vmem = pltpu.VMEM
    tiles, coefs = pl.pallas_call(
        strip_kernel,
        in_specs=[pl.BlockSpec(memory_space=pl.ANY), pl.BlockSpec(memory_space=pltpu.SMEM)]
        + [pl.BlockSpec(memory_space=vmem)] * len(ins),
        out_specs=[pl.BlockSpec(memory_space=pl.ANY), pl.BlockSpec(memory_space=vmem)],
        out_shape=[
            jax.ShapeDtypeStruct((TILES, SIDE * ROWS, SIDE), BF),
            jax.ShapeDtypeStruct((2 * SIDE, SIDE), F32),
        ],
        scratch_shapes=[
            vmem((SLOTS, SIDE, ROWS, LANES), BF),
            vmem((TILES, SIDE * ROWS, SIDE), F32),
            vmem((ROWS, NPIX, SIDE), BF),
            vmem((ROWS, NDEV, OWN, SIDE), BF),
            vmem((ROWS, NPIX, SIDE), BF),
            vmem((NPIX + 2 * HALF, SIDE), F32),
            vmem((SIDE, SIDE), F32),
            vmem((2, PER, SIDE * ROWS, SIDE), BF),
            vmem((8, SIDE), F32),
            vmem((HALF + 1, 8, SIDE), F32),
            vmem((HROWS, SIDE), F32),
            vmem((SIDE * GROUP, SIDE), F32),
            vmem((GROUP, 2 * HROWS, SIDE), F32),
            vmem((GROUP * 8, SIDE), F32),
            vmem((NBASIS, GROUP, SIDE), F32),
            vmem((NBASIS, 2 * HROWS, SIDE), F32),
            vmem((NBASIS * NBASIS, 8, SIDE), F32),
            vmem((ROWS, OWN, SIDE), F32),
            vmem((ROWS, OWN, SIDE), F32),
            dma((SLOTS,)),
            dma((2,)),
            dma((ROWS,)),
            dma((ROWS,)),
            dma((ROWS,)),
            dma((ROWS,)),
            dma((2 * ROWS,)),
            dma((ROWS,)),
            dma((ROWS,)),
        ],
        compiler_params=params(has_side_effects=True),
    )(cube, flags, *ins)
    restored, continuum = pl.pallas_call(
        leave_kernel,
        grid=(PARTS,),
        in_specs=[
            pl.BlockSpec((PER, SIDE * ROWS, SIDE), lambda i: (i, 0, 0)),
            pl.BlockSpec((2 * SIDE, SIDE), lambda i: (0, 0)),
        ],
        out_specs=[
            pl.BlockSpec((SIDE, ROWS, LANES), lambda i: (0, 0, i)),
            pl.BlockSpec((NBASIS, ROWS * OWN), lambda i: (0, 0)),
        ],
        out_shape=[
            jax.ShapeDtypeStruct((SIDE, ROWS, NPIX), BF),
            jax.ShapeDtypeStruct((NBASIS, ROWS * OWN), F32),
        ],
        compiler_params=params(),
    )(tiles, coefs)
    return (restored, continuum)


def solution(mesh):
    placed = (P(AXES, None, None), P(AXES), P(), P(AXES))
    return jax.shard_map(
        body,
        mesh=mesh,
        in_specs=placed,
        out_specs=(P(AXES, None, None), P(None, AXES)),
        check_vma=False,
    )
```

```python
import functools
import math

import jax
import jax.numpy as jnp
import numpy as np
from jax import lax
from jax.experimental import pallas as pl
from jax.experimental.pallas import tpu as pltpu
from jax.sharding import PartitionSpec as P

NDEV = 128
NBASIS = 6
HALF = 8
FLAGBLK = 16
ROWS = 4
NPIX = 6144
NCHAN = 16384
SIDE = 128
HROWS = 72
OWN = NPIX // NDEV
GROUP = 16
STEP = GROUP + 1
FLAGGED = 128.0
LIMIT = 100.0
BF = jnp.bfloat16
F32 = jnp.float32
VMEM_BYTES = 56 * 1024 * 1024
AXES = ("wide", "narrow")


def split3(x):
    hi = x.astype(BF)
    rest = x - hi.astype(np.float64)
    lo = rest.astype(BF)
    return hi, lo, (rest - lo.astype(np.float64)).astype(BF)


def legendre64(x):
    terms = [np.ones_like(x), x]
    for k in range(1, NBASIS - 1):
        terms.append(((2 * k + 1) * x * terms[k] - k * terms[k - 1]) / (k + 1))
    return np.stack(terms[:NBASIS])


@functools.cache
def tables():
    idx = np.arange(SIDE)
    turn = 2.0 * np.pi / SIDE
    half = SIDE // 2 + 1
    cos = np.cos(turn * (np.outer(idx, idx) % SIDE))
    sin = np.sin(turn * (np.outer(idx, idx) % SIDE))
    first = np.zeros((2 * HROWS, SIDE))
    first[:half] = cos[:half]
    first[HROWS : HROWS + half] = -sin[:half]
    plain = first.astype(np.float32)
    slow = legendre64((2.0 * idx + 1.0) / SIDE - 1.0)
    first[half : half + NBASIS] = slow
    fa_hi, fa_lo, fa_rest = split3(first)
    fa_hi = fa_hi.copy()
    fa_hi[HROWS + half : HROWS + half + NBASIS] = fa_rest[half : half + NBASIS]
    chan = np.arange(NCHAN)
    full = legendre64((2.0 * chan + 1.0) / NCHAN - 1.0).reshape(NBASIS, SIDE, SIDE)
    fit = np.linalg.pinv(slow.T)
    mix = np.einsum("ma,kab->kmb", fit, full)
    mix = np.where(np.arange(NBASIS)[None, :, None] <= np.arange(NBASIS)[:, None, None], mix, 0.0)
    w2 = np.block([[cos, -sin], [sin, cos]])
    v2 = np.block([[cos, sin], [-sin, cos]])
    times = np.full((half,), 2.0)
    times[0] = times[-1] = 1.0
    last = np.zeros((SIDE, 2 * HROWS))
    last[:, :half] = cos[:, :half] * times
    last[:, HROWS : HROWS + half] = -sin[:, :half] * times
    tc = np.zeros((HROWS, SIDE))
    ts = np.zeros((HROWS, SIDE))
    tc[:half] = np.cos(2.0 * np.pi / NCHAN * np.outer(idx[:half], idx))
    ts[:half] = np.sin(2.0 * np.pi / NCHAN * np.outer(idx[:half], idx))
    w_hi, w_lo, _ = split3(w2)
    v_hi, v_lo, _ = split3(v2)
    l_hi, l_lo, _ = split3(last)
    f = np.float32
    return dict(
        fa=np.concatenate([fa_hi, fa_lo], axis=1), plain=plain, full=full.astype(f), mix=mix.astype(f),
        w2=np.stack([w_hi, w_lo]), v2=np.stack([v_hi, v_lo]), last=np.concatenate([l_hi, l_lo, l_hi], axis=1),
        tc=tc.astype(f), ts=ts.astype(f),
    )


def dot(a, b):
    return jnp.dot(a, b, preferred_element_type=F32)


def halves(x):
    hi = x.astype(BF)
    return hi, (x - hi.astype(F32)).astype(BF)


def dot_right(x, table):
    hi, lo = halves(x)
    return dot(hi, table[0]) + dot(lo, table[0]) + dot(hi, table[1])


def dot_left(table, x):
    hi, lo = halves(x)
    return dot(table[...], jnp.concatenate([hi, hi, lo], axis=0))


def unpack_group(src, start, xs):
    @pl.loop(0, SIDE // 8)
    def _(i):
        base = pl.multiple_of(i * 8 * STEP, 8)
        for k in range(8):
            xs[pl.ds(base + k * STEP, GROUP), :] = src[i * 8 + k, pl.ds(start, GROUP), :].astype(F32)


def pack_group(dst, start, xs):
    @pl.loop(0, SIDE // 8)
    def _(i):
        base = pl.multiple_of(i * 8 * STEP, 8)
        for k in range(8):
            dst[i * 8 + k, pl.ds(start, GROUP), :] = xs[pl.ds(base + k * STEP, GROUP), :].astype(BF)


def fit_setup(xs, full, plain, fw, chol):
    weight = jnp.where(xs[pl.ds(0, SIDE, stride=STEP), :] > LIMIT, 0.0, 1.0)
    gram = {}
    for i in range(NBASIS):
        weighted = full[i] * weight
        fw[i] = jnp.dot(plain[...], weighted, preferred_element_type=F32, precision=lax.Precision.HIGHEST)
        for j in range(i + 1):
            total = jnp.sum(jnp.sum(weighted * full[j], axis=0, keepdims=True), axis=1, keepdims=True)
            gram[i, j] = jnp.broadcast_to(total, (8, SIDE))
    factor = {}
    for j in range(NBASIS):
        value = gram[j, j]
        for k in range(j):
            value = value - factor[j, k] * factor[j, k]
        factor[j, j] = jnp.sqrt(value)
        for i in range(j + 1, NBASIS):
            value = gram[i, j]
            for k in range(j):
                value = value - factor[i, k] * factor[j, k]
            factor[i, j] = value / factor[j, j]
    for (i, j), value in factor.items():
        chol[i * NBASIS + j] = value


def fit_group(z, tt, mix, chol, cs):
    @pl.loop(0, GROUP)
    def _(p):
        tt[pl.ds(pl.multiple_of(p * 8, 8), 8), :] = z[p, 64:72, :] + z[p, 136:144, :]

    parts = [tt[pl.ds(m + 1, GROUP, stride=8), :] for m in range(NBASIS)]

    def entry(i, j):
        return jnp.broadcast_to(chol[i * NBASIS + j, 0:1, :], (GROUP, SIDE))

    inner = []
    for k in range(NBASIS):
        total = parts[0] * mix[k, 0:1, :]
        for m in range(1, k + 1):
            total = total + parts[m] * mix[k, m : m + 1, :]
        value = jnp.broadcast_to(jnp.sum(total, axis=1, keepdims=True), (GROUP, SIDE))
        for j in range(k):
            value = value - entry(k, j) * inner[j]
        inner.append(value / entry(k, k))
    result = [None] * NBASIS
    for i in reversed(range(NBASIS)):
        value = inner[i]
        for j in range(i + 1, NBASIS):
            value = value - entry(j, i) * result[j]
        result[i] = value / entry(i, i)
    lane = lax.broadcasted_iota(jnp.int32, (GROUP, SIDE), 1)
    shown = jnp.zeros((GROUP, SIDE), F32)
    for k in range(NBASIS):
        cs[k] = result[k]
        shown = jnp.where(lane == k, result[k], shown)
    return shown


def filter_group(xs, z, tt, cs, fa, w2, v2, last, tc, ts, gain, mix, fw, chol):
    @pl.loop(0, GROUP // 2)
    def _(i):
        both = [xs[pl.ds(2 * i + q, SIDE, stride=STEP), :] for q in range(2)]
        x = jnp.concatenate([jnp.where(v > LIMIT, 0.0, v) for v in both], axis=1).astype(BF)
        res = dot(fa[...], jnp.concatenate([x, x], axis=0))
        z[2 * i] = res[:, :SIDE]
        z[2 * i + 1] = res[:, SIDE:]

    shown = fit_group(z, tt, mix, chol, cs)
    quad = 4

    @pl.loop(0, GROUP // quad)
    def _(i):
        real, imag = [], []
        for q in range(quad):
            p = i * quad + q
            zr, zi = z[p, :HROWS, :], z[p, HROWS:, :]
            for k in range(NBASIS):
                coef = cs[k, pl.ds(p, 1), :]
                zr = zr - coef * fw[k, :HROWS, :]
                zi = zi - coef * fw[k, HROWS:, :]
            real.append(zr * tc[...] + zi * ts[...])
            imag.append(zi * tc[...] - zr * ts[...])
        u = jnp.concatenate([jnp.concatenate(real, axis=0), jnp.concatenate(imag, axis=0)], axis=1)
        x = dot_right(u, w2)
        g = jnp.concatenate([gain[...]] * quad, axis=0)
        x = x * jnp.concatenate([g, g], axis=1)
        v = dot_right(x, v2)
        cols = []
        for q in range(quad):
            vr, vi = v[q * HROWS : (q + 1) * HROWS, :SIDE], v[q * HROWS : (q + 1) * HROWS, SIDE:]
            cols.append(jnp.concatenate([vr * tc[...] - vi * ts[...], vi * tc[...] + vr * ts[...]], axis=0))
        out = dot_left(last, jnp.concatenate(cols, axis=1))
        for q in range(quad):
            xs[pl.ds(i * quad + q, SIDE, stride=STEP), :] = out[:, q * SIDE : (q + 1) * SIDE]

    return shown


TILES = NPIX // SIDE
FLAT = TILES * ROWS
REACH = FLAT + 1
BLOCK = 8
BLOCKS = SIDE // BLOCK
SLOTS = 4


def place():
    wide, narrow = lax.axis_index("wide"), lax.axis_index("narrow")
    return wide, narrow, wide * 4 + narrow


def partner(i, j):
    wide, narrow, _ = place()
    x, y = lax.div(wide, 8), lax.rem(wide, 4)
    z = lax.rem(lax.div(wide, 4), 2) * 2 + lax.div(narrow, 2)
    x = lax.rem(x + i + j, 4)
    y = lax.rem(y + i // 4 + j // 2 if isinstance(i, int) else y + lax.div(i, 4) + j // 2, 4)
    z = lax.rem(z + j % 4, 4)
    core = lax.rem(lax.rem(narrow, 2) + j // 4, 2)
    return (x * 2 + lax.div(z, 2)) * 4 + y, lax.rem(z, 2) * 2 + core


def columns(ref, row, device):
    return ref.at[row, pl.ds(pl.multiple_of(device * OWN, 16), OWN)]


def exchange(row, source, target, send_sem, recv_sem):
    def send(i, j):
        wide, narrow = partner(i, j)
        pltpu.make_async_remote_copy(
            src_ref=source(wide * 4 + narrow),
            dst_ref=target,
            send_sem=send_sem.at[row],
            recv_sem=recv_sem.at[row],
            device_id=(wide, narrow),
            device_id_type=pl.DeviceIdType.MESH,
        ).start()

    @pl.loop(1, 16)
    def _(i):
        for j in range(8):
            send(i, j)

    for j in range(1, 8):
        send(0, j)


def wait_all(row, buffer, sem):
    block = buffer.at[row, pl.ds(0, NDEV - 1)]
    pltpu.make_async_copy(block, block, sem.at[row]).wait()


def wait_rows(row, buffer, sem):
    block = buffer.at[row, pl.ds(0, (NDEV - 1) * OWN)]
    pltpu.make_async_copy(block, block, sem.at[row]).wait()


def widen(cube_v, slot, work, block):
    base = pl.multiple_of(block * BLOCK * REACH, 8)
    for k in range(BLOCK):
        work[pl.ds(base + k * REACH, FLAT), :] = cube_v[slot, k].astype(F32)


def narrow_down(leave, slot, work, block):
    base = pl.multiple_of(block * BLOCK * REACH, 8)
    for k in range(BLOCK):
        leave[slot, k] = work[pl.ds(base + k * REACH, FLAT), :].astype(BF)


def turn_in(row, tile, work, marks, sent):
    block = work[pl.ds(tile * ROWS + row, SIDE, stride=REACH), :]
    turned = jnp.where(marks[0:1, :] > 0.0, FLAGGED, block.T)
    sent[row, pl.ds(pl.multiple_of(tile * SIDE, SIDE), SIDE), :] = turned.astype(BF)


def make_marks(flags, marks):
    lane = lax.broadcasted_iota(jnp.int32, (8, SIDE), 1)
    value = jnp.zeros((8, SIDE), F32)
    for f in range(SIDE // FLAGBLK):
        inside = (lane >= f * FLAGBLK) & (lane < (f + 1) * FLAGBLK)
        value = jnp.where(inside, flags[f].astype(F32), value)
    marks[...] = value


def make_taps(width, taps):
    w = jnp.broadcast_to(width[...], (8, SIDE))
    raw = [jnp.exp(-float((HALF - j) ** 2) / (2.0 * w * w)) for j in range(HALF + 1)]
    total = raw[HALF]
    for j in range(HALF):
        total = total + 2.0 * raw[j]
    for j in range(HALF + 1):
        taps[j] = raw[j] / total


def make_gain(line, gain):
    half = SIDE // 2

    def exact(a, b):
        return jnp.dot(a, b, preferred_element_type=F32, precision=lax.Precision.HIGHEST)

    low = line[...]
    row = lax.broadcasted_iota(jnp.int32, (half, HROWS), 0)
    col = lax.broadcasted_iota(jnp.int32, (half, HROWS), 1)
    first = lax.broadcasted_iota(jnp.int32, (SIDE, SIDE), 0)
    second = lax.broadcasted_iota(jnp.int32, (SIDE, SIDE), 1)
    turned = exact(jnp.where(row + col == half - 1, 1.0, 0.0), low)
    mirror = exact(turned, jnp.where(first + second == SIDE, 1.0, 0.0))
    edge = exact(jnp.where(row + col == half, 1.0, 0.0), low)
    lane = lax.broadcasted_iota(jnp.int32, (half, SIDE), 1)
    high = jnp.where(lane == 0, edge, mirror)
    gain[...] = jnp.concatenate([low[:half], high], axis=0).T[:HROWS] * (1.0 / NCHAN)


def beam_start(row, back, padded):
    last = (NPIX // GROUP + 1) * STEP
    padded[0:GROUP, :] = jnp.zeros((GROUP, SIDE), F32)
    padded[last : last + GROUP, :] = jnp.zeros((GROUP, SIDE), F32)

    @pl.loop(0, TILES)
    def _(i):
        at = pl.multiple_of(i * SIDE, SIDE)
        base = pl.multiple_of(i * 8 * STEP, 8)
        for k in range(8):
            padded[pl.ds(base + (k + 1) * STEP, GROUP), :] = back[row, pl.ds(at + k * GROUP, GROUP), :].astype(F32)


def beam_tile(row, tile, padded, taps, flat, work):
    base = pl.multiple_of(tile * 8 * STEP, 8)
    values = []
    for t in range(-HALF, GROUP + HALF):
        run, spot = t // GROUP, t % GROUP
        values.append(padded[pl.ds(base + (run + 1) * STEP + spot, 8, stride=STEP), :])
    for t in range(GROUP):
        total = values[t + HALF] * taps[HALF]
        for j in range(HALF):
            total = total + (values[t + j] + values[t + 2 * HALF - j]) * taps[j]
        flat[pl.ds(t, 8, stride=STEP), :] = total
    whole = jnp.concatenate([flat[k * STEP : k * STEP + GROUP, :] for k in range(8)], axis=0)
    work[pl.ds(tile * ROWS + row, SIDE, stride=REACH), :] = whole.T


def strip_kernel(
    cube, flags, line, width, fa, w2, v2, last, tc, ts, mix, full, plain, tiles, continuum,
    cube_v, work, sent, got, back, padded, flat, leave, marks, taps, gain, xs, z, tt, cs, fw, chol, shown, gathered,
    in_sem, out_sem, go_send, go_recv, home_send, home_recv, own_sem, fit_send, fit_recv,
):
    my_wide, my_narrow, me = place()

    def cube_part(part):
        slot = lax.rem(part, SLOTS)
        source = cube.at[pl.ds(part * BLOCK, BLOCK)]
        return pltpu.make_async_copy(source, cube_v.at[slot], in_sem.at[slot])

    def out_part(part):
        slot = lax.rem(part, 2)
        target = tiles.at[pl.ds(part * BLOCK, BLOCK)]
        return pltpu.make_async_copy(leave.at[slot], target, out_sem.at[slot])

    def own_go(row):
        return pltpu.make_async_copy(columns(sent, row, me), got.at[row, me], own_sem.at[row])

    def own_home(row):
        return pltpu.make_async_copy(got.at[row, me], columns(back, row, me), own_sem.at[ROWS + row])

    @pl.loop(0, SLOTS)
    def _(part):
        cube_part(part).start()

    make_marks(flags, marks)

    @pl.loop(0, BLOCKS)
    def _(part):
        cube_part(part).wait()
        widen(cube_v, lax.rem(part, SLOTS), work, part)

        @pl.when(part + SLOTS < BLOCKS)
        def _():
            cube_part(part + SLOTS).start()

    for row in range(ROWS):
        @pl.loop(0, TILES, step=4)
        def _(tile):
            for q in range(4):
                turn_in(row, tile + q, work, marks, sent)

        own_go(row).start()
        exchange(row, lambda d: columns(sent, row, d), got.at[row, me], go_send, go_recv)

    make_gain(line, gain)
    make_taps(width, taps)

    def fit_target(row):
        return row * (NDEV // ROWS) + me // ROWS

    def fit_remote(row):
        dest = fit_target(row)
        return pltpu.make_async_remote_copy(
            src_ref=shown.at[row],
            dst_ref=gathered.at[me % ROWS],
            send_sem=fit_send.at[row],
            recv_sem=fit_recv.at[me % ROWS],
            device_id=(dest // 4, dest % 4),
            device_id_type=pl.DeviceIdType.MESH,
        )

    def fit_local(row):
        return pltpu.make_async_copy(shown.at[row], gathered.at[me % ROWS], fit_send.at[row])

    for row in range(ROWS):
        own_go(row).wait()
        wait_all(row, got, go_recv)
        rows = got.at[row]
        if row == 0:
            unpack_group(rows, 0, xs)
            fit_setup(xs, full, plain, fw, chol)

        @pl.loop(0, OWN // GROUP)
        def _(g):
            start = pl.multiple_of(g * GROUP, GROUP)
            unpack_group(rows, start, xs)
            shown[row, pl.ds(start, GROUP), :] = filter_group(
                xs, z, tt, cs, fa, w2, v2, last, tc, ts, gain, mix, fw, chol
            )
            pack_group(rows, start, xs)

        own_home(row).start()
        exchange(row, lambda d: got.at[row, d], columns(back, row, me), home_send, home_recv)
        dest = fit_target(row)

        @pl.when(dest != me)
        def _():
            fit_remote(row).start()

        @pl.when(dest == me)
        def _():
            fit_local(row).start()

    for row in range(ROWS):
        own_home(row).wait()
        wait_rows(row, back, home_recv)
        beam_start(row, back, padded)

        @pl.loop(0, TILES)
        def _(tile):
            beam_tile(row, tile, padded, taps, flat, work)

    @pl.loop(0, BLOCKS)
    def _(part):
        @pl.when(part >= 2)
        def _():
            out_part(part - 2).wait()

        narrow_down(leave, lax.rem(part, 2), work, part)
        out_part(part).start()

    for row in range(ROWS):
        dest = fit_target(row)

        @pl.when(dest != me)
        def _():
            fit_remote(row).wait_send()

        @pl.when(dest == me)
        def _():
            fit_local(row).wait()

    for slot in range(ROWS):
        source = me % (NDEV // ROWS) * ROWS + slot

        @pl.when(source != me)
        def _():
            block = gathered.at[slot]
            pltpu.make_async_copy(block, block, fit_recv.at[slot]).wait()

    for slot in range(ROWS):
        continuum[slot * OWN : (slot + 1) * OWN, :] = gathered[slot]
    continuum[ROWS * OWN :, :] = jnp.zeros((2 * SIDE - ROWS * OWN, SIDE), F32)
    for row in range(ROWS):
        wait_rows(row, sent, go_send)
        wait_all(row, got, home_send)

    for part in (BLOCKS - 2, BLOCKS - 1):
        out_part(part).wait()


def leave_kernel(tiles, coefs, restored, continuum):
    restored[...] = tiles[...]
    continuum[...] = coefs[...].T[:NBASIS, : ROWS * OWN]


def params(**more):
    return pltpu.CompilerParams(vmem_limit_bytes=VMEM_BYTES, **more)


def body(cube, flags, line_gain, beam_width):
    tab = {k: jnp.asarray(v) for k, v in tables().items()}
    line = jnp.pad(line_gain, (0, HROWS * SIDE - line_gain.shape[0])).reshape(HROWS, SIDE)
    names = ("fa", "w2", "v2", "last", "tc", "ts", "mix", "full", "plain")
    ins = [line, beam_width[None, :]] + [tab[n] for n in names]
    dma = pltpu.SemaphoreType.DMA
    vmem = pltpu.VMEM
    flat = cube.reshape(SIDE, ROWS, TILES, SIDE).transpose(0, 2, 1, 3).reshape(SIDE, FLAT, SIDE)
    tiles, coefs = pl.pallas_call(
        strip_kernel,
        in_specs=[pl.BlockSpec(memory_space=pl.ANY), pl.BlockSpec(memory_space=pltpu.SMEM)]
        + [pl.BlockSpec(memory_space=vmem)] * len(ins),
        out_specs=[pl.BlockSpec(memory_space=pl.ANY), pl.BlockSpec(memory_space=vmem)],
        out_shape=[
            jax.ShapeDtypeStruct((SIDE, FLAT, SIDE), BF),
            jax.ShapeDtypeStruct((2 * SIDE, SIDE), F32),
        ],
        scratch_shapes=[
            vmem((SLOTS, BLOCK, FLAT, SIDE), BF),
            vmem((SIDE * REACH, SIDE), F32),
            vmem((ROWS, NPIX, SIDE), BF),
            vmem((ROWS, NDEV, OWN, SIDE), BF),
            vmem((ROWS, NPIX, SIDE), BF),
            vmem(((NPIX // GROUP + 2) * STEP, SIDE), F32),
            vmem((8 * STEP, SIDE), F32),
            vmem((2, BLOCK, FLAT, SIDE), BF),
            vmem((8, SIDE), F32),
            vmem((HALF + 1, 8, SIDE), F32),
            vmem((HROWS, SIDE), F32),
            vmem((SIDE * STEP, SIDE), F32),
            vmem((GROUP, 2 * HROWS, SIDE), F32),
            vmem((GROUP * 8, SIDE), F32),
            vmem((NBASIS, GROUP, SIDE), F32),
            vmem((NBASIS, 2 * HROWS, SIDE), F32),
            vmem((NBASIS * NBASIS, 8, SIDE), F32),
            vmem((ROWS, OWN, SIDE), F32),
            vmem((ROWS, OWN, SIDE), F32),
            dma((SLOTS,)),
            dma((2,)),
            dma((ROWS,)),
            dma((ROWS,)),
            dma((ROWS,)),
            dma((ROWS,)),
            dma((2 * ROWS,)),
            dma((ROWS,)),
            dma((ROWS,)),
        ],
        compiler_params=params(has_side_effects=True),
    )(flat, flags, *ins)
    restored, continuum = pl.pallas_call(
        leave_kernel,
        grid=(BLOCKS,),
        in_specs=[
            pl.BlockSpec((BLOCK, FLAT, SIDE), lambda i: (i, 0, 0)),
            pl.BlockSpec((2 * SIDE, SIDE), lambda i: (0, 0)),
        ],
        out_specs=[
            pl.BlockSpec((BLOCK, FLAT, SIDE), lambda i: (i, 0, 0)),
            pl.BlockSpec((NBASIS, ROWS * OWN), lambda i: (0, 0)),
        ],
        out_shape=[
            jax.ShapeDtypeStruct((SIDE, FLAT, SIDE), BF),
            jax.ShapeDtypeStruct((NBASIS, ROWS * OWN), F32),
        ],
        compiler_params=params(),
    )(tiles, coefs)
    restored = restored.reshape(SIDE, TILES, ROWS, SIDE).transpose(0, 2, 1, 3).reshape(SIDE, ROWS, NPIX)
    return (restored, continuum)


def solution(mesh):
    placed = (P(AXES, None, None), P(AXES), P(), P(AXES))
    return jax.shard_map(
        body,
        mesh=mesh,
        in_specs=placed,
        out_specs=(P(AXES, None, None), P(None, AXES)),
        check_vma=False,
    )
```

```python
import functools
import math

import jax
import jax.numpy as jnp
import numpy as np
from jax import lax
from jax.experimental import pallas as pl
from jax.experimental.pallas import tpu as pltpu
from jax.sharding import PartitionSpec as P

NDEV = 128
NBASIS = 6
HALF = 8
FLAGBLK = 16
ROWS = 4
NPIX = 6144
NCHAN = 16384
SIDE = 128
HROWS = 72
OWN = NPIX // NDEV
GROUP = 16
ZSTEP = 2 * HROWS + 8
KEPT = SIDE // 2 + 1
FLAGGED = 128.0
LIMIT = 100.0
BF = jnp.bfloat16
F32 = jnp.float32
VMEM_BYTES = 56 * 1024 * 1024
AXES = ("wide", "narrow")


def split3(x):
    hi = x.astype(BF)
    rest = x - hi.astype(np.float64)
    lo = rest.astype(BF)
    return hi, lo, (rest - lo.astype(np.float64)).astype(BF)


def legendre64(x):
    terms = [np.ones_like(x), x]
    for k in range(1, NBASIS - 1):
        terms.append(((2 * k + 1) * x * terms[k] - k * terms[k - 1]) / (k + 1))
    return np.stack(terms[:NBASIS])


@functools.cache
def tables():
    idx = np.arange(SIDE)
    turn = 2.0 * np.pi / SIDE
    half = SIDE // 2 + 1
    cos = np.cos(turn * (np.outer(idx, idx) % SIDE))
    sin = np.sin(turn * (np.outer(idx, idx) % SIDE))
    first = np.zeros((2 * HROWS, SIDE))
    first[:half] = cos[:half]
    first[HROWS : HROWS + half] = -sin[:half]
    plain = first.astype(np.float32)
    slow = legendre64((2.0 * idx + 1.0) / SIDE - 1.0)
    first[half : half + NBASIS] = slow
    fa_hi, fa_lo, fa_rest = split3(first)
    fa_hi = fa_hi.copy()
    fa_hi[HROWS + half : HROWS + half + NBASIS] = fa_rest[half : half + NBASIS]
    chan = np.arange(NCHAN)
    full = legendre64((2.0 * chan + 1.0) / NCHAN - 1.0).reshape(NBASIS, SIDE, SIDE)
    fit = np.linalg.pinv(slow.T)
    mix = np.einsum("ma,kab->kmb", fit, full)
    mix = np.where(np.arange(NBASIS)[None, :, None] <= np.arange(NBASIS)[:, None, None], mix, 0.0)
    times = np.full((half,), 2.0)
    times[0] = times[-1] = 1.0
    last = np.zeros((SIDE, 2 * HROWS))
    last[:, :half] = cos[:, :half] * times
    last[:, HROWS : HROWS + half] = -sin[:, :half] * times
    shift = np.arange(2 * SIDE) - SIDE
    turn_c = np.zeros((HROWS, 2 * SIDE))
    turn_s = np.zeros((HROWS, 2 * SIDE))
    turn_c[:half] = np.cos(2.0 * np.pi / NCHAN * np.outer(idx[:half], shift))
    turn_s[:half] = np.sin(2.0 * np.pi / NCHAN * np.outer(idx[:half], shift))
    l_hi, l_lo, _ = split3(last)
    f = np.float32
    return dict(
        fa=np.concatenate([fa_hi, fa_lo], axis=1), plain=plain, full=full.astype(f), mix=mix.astype(f),
        last=np.concatenate([l_hi, l_lo, l_hi], axis=1),
        waves=np.stack([cos, sin]).astype(f), turns=np.stack([turn_c, turn_s]).astype(f),
    )


def dot(a, b):
    return jnp.dot(a, b, preferred_element_type=F32)


def halves(x):
    hi = x.astype(BF)
    return hi, (x - hi.astype(F32)).astype(BF)


def dot_left(table, x):
    hi, lo = halves(x)
    return dot(table[...], jnp.concatenate([hi, hi, lo], axis=0))


def unpack_group(src, start, xs):
    @pl.loop(0, SIDE // 8)
    def _(i):
        block = src[pl.ds(i * 8, 8), pl.ds(start, GROUP), :].astype(F32)
        xs[pl.ds(pl.multiple_of(i * 8 * GROUP, 128), 8 * GROUP), :] = block.reshape(8 * GROUP, SIDE)


def pack_group(dst, start, xs):
    @pl.loop(0, SIDE // 8)
    def _(i):
        block = xs[pl.ds(pl.multiple_of(i * 8 * GROUP, 128), 8 * GROUP), :]
        dst[pl.ds(i * 8, 8), pl.ds(start, GROUP), :] = block.reshape(8, GROUP, SIDE).astype(BF)


def fit_setup(xs, full, plain, fw, chol):
    weight = jnp.where(xs[pl.ds(0, SIDE, stride=GROUP), :] > LIMIT, 0.0, 1.0)
    gram = {}
    fw[NBASIS * 2 * HROWS :, :] = jnp.zeros((2 * 2 * HROWS, SIDE), F32)
    for i in range(NBASIS):
        weighted = full[i] * weight
        fw[i * 2 * HROWS : (i + 1) * 2 * HROWS, :] = jnp.dot(plain[...], weighted, preferred_element_type=F32, precision=lax.Precision.HIGHEST)
        for j in range(i + 1):
            total = jnp.sum(jnp.sum(weighted * full[j], axis=0, keepdims=True), axis=1, keepdims=True)
            gram[i, j] = jnp.broadcast_to(total, (8, SIDE))
    factor = {}
    for j in range(NBASIS):
        value = gram[j, j]
        for k in range(j):
            value = value - factor[j, k] * factor[j, k]
        factor[j, j] = jnp.sqrt(value)
        for i in range(j + 1, NBASIS):
            value = gram[i, j]
            for k in range(j):
                value = value - factor[i, k] * factor[j, k]
            factor[i, j] = value / factor[j, j]
    for (i, j), value in factor.items():
        chol[i * NBASIS + j] = value


def make_matrices(gain, waves, turns, hs, mats):
    def exact(a, b):
        return jnp.dot(a, b, preferred_element_type=F32, precision=lax.Precision.HIGHEST)

    real, imag = exact(gain[...], waves[0]), exact(gain[...], waves[1])
    real, imag = jnp.concatenate([real, real], axis=1), jnp.concatenate([imag, imag], axis=1)
    hs[0] = real * turns[0] - imag * turns[1]
    hs[1] = real * turns[1] + imag * turns[0]

    @pl.loop(0, KEPT)
    def _(k):
        for part in range(2):
            rows = jnp.broadcast_to(hs[part, pl.ds(k, 1), :], (SIDE, 2 * SIDE))
            matrix = pltpu.roll(rows, 0, 1, stride=1, stride_axis=0)[:, SIDE:]
            hi, lo = halves(matrix)
            mats[k, 2 * part] = hi
            mats[k, 2 * part + 1] = lo
            if part == 1:
                mats[k, 4] = -hi
                mats[k, 5] = -lo


def fit_group(z, first, tt, mix, chol, cl):
    @pl.loop(0, GROUP)
    def _(p):
        base = pl.multiple_of((first + p) * ZSTEP, 8)
        tt[pl.ds(pl.multiple_of(p * 8, 8), 8), :] = z[pl.ds(base + 64, 8), :] + z[pl.ds(base + 136, 8), :]

    parts = [tt[pl.ds(m + 1, GROUP, stride=8), :] for m in range(NBASIS)]

    def entry(i, j):
        return jnp.broadcast_to(chol[i * NBASIS + j, 0:1, :], (GROUP, SIDE))

    inner = []
    for k in range(NBASIS):
        total = parts[0] * mix[k, 0:1, :]
        for m in range(1, k + 1):
            total = total + parts[m] * mix[k, m : m + 1, :]
        value = jnp.broadcast_to(jnp.sum(total, axis=1, keepdims=True), (GROUP, SIDE))
        for j in range(k):
            value = value - entry(k, j) * inner[j]
        inner.append(value / entry(k, k))
    result = [None] * NBASIS
    for i in reversed(range(NBASIS)):
        value = inner[i]
        for j in range(i + 1, NBASIS):
            value = value - entry(j, i) * result[j]
        result[i] = value / entry(i, i)
    lane = lax.broadcasted_iota(jnp.int32, (GROUP, SIDE), 1)
    shown = jnp.zeros((GROUP, SIDE), F32)
    parts = jnp.zeros((GROUP, SIDE), F32)
    for k in range(NBASIS):
        hi = result[k].astype(BF).astype(F32)
        shown = jnp.where(lane == k, result[k], shown)
        parts = jnp.where((lane == k) | (lane == 16 + k), hi, parts)
        parts = jnp.where(lane == 8 + k, result[k] - hi, parts)
    cl[pl.ds(pl.multiple_of(first, GROUP), GROUP), :] = parts.astype(BF)
    return shown


def spectrum_group(xs, z, first, fa):
    @pl.loop(0, GROUP // 4)
    def _(i):
        for h in range(2):
            p = 4 * i + 2 * h
            both = [xs[pl.ds(p + q, SIDE, stride=GROUP), :] for q in range(2)]
            x = jnp.concatenate([jnp.where(v > LIMIT, 0.0, v) for v in both], axis=1).astype(BF)
            res = dot(fa[...], jnp.concatenate([x, x], axis=0))
            for q in range(2):
                base = pl.multiple_of((first + p + q) * ZSTEP, 8)
                z[pl.ds(base, 2 * HROWS), :] = res[:, q * SIDE : (q + 1) * SIDE]


def filter_row(z, cl, fw, mats):
    def one(k):
        real, imag = pl.ds(k, OWN, stride=ZSTEP), pl.ds(k + HROWS, OWN, stride=ZSTEP)
        base = jnp.concatenate(
            [fw[pl.ds(k, 8, stride=2 * HROWS), :], fw[pl.ds(k + HROWS, 8, stride=2 * HROWS), :]], axis=1
        )
        hi = base.astype(BF).astype(F32)
        fill = jnp.zeros((SIDE - 24, 2 * SIDE), F32)
        smooth = dot(cl[...], jnp.concatenate([hi, hi, base - hi, fill], axis=0).astype(BF))
        value = jnp.concatenate([z[real, :], z[imag, :]], axis=1) - smooth
        hi, lo = halves(value)

        def matrix(part):
            up = jnp.concatenate([mats[k, part], mats[k, 2 + part]], axis=1)
            down = jnp.concatenate([mats[k, 4 + part], mats[k, part]], axis=1)
            return jnp.concatenate([up, down], axis=0)

        both = dot(jnp.concatenate([hi, lo], axis=0), matrix(0))
        out = both[:OWN] + both[OWN:] + dot(hi, matrix(1))
        z[real, :] = out[:, :SIDE]
        z[imag, :] = out[:, SIDE:]

    @pl.loop(0, KEPT // 5)
    def _(i):
        for j in range(5):
            one(i * 5 + j)


def channels_group(xs, z, first, last):
    quad = 4

    @pl.loop(0, GROUP // quad)
    def _(i):
        cols = []
        for q in range(quad):
            base = pl.multiple_of((first + i * quad + q) * ZSTEP, 8)
            cols.append(z[pl.ds(base, 2 * HROWS), :])
        out = dot_left(last, jnp.concatenate(cols, axis=1))
        for q in range(quad):
            xs[pl.ds(i * quad + q, SIDE, stride=GROUP), :] = out[:, q * SIDE : (q + 1) * SIDE]


TILES = NPIX // SIDE
FLAT = TILES * ROWS
REACH = FLAT + 8
BLOCK = 8
BLOCKS = SIDE // BLOCK


def place():
    wide, narrow = lax.axis_index("wide"), lax.axis_index("narrow")
    return wide, narrow, wide * 4 + narrow


def partner(i, j):
    wide, narrow, _ = place()
    x, y = lax.div(wide, 8), lax.rem(wide, 4)
    z = lax.rem(lax.div(wide, 4), 2) * 2 + lax.div(narrow, 2)
    x = lax.rem(x + i + j, 4)
    y = lax.rem(y + i // 4 + j // 2 if isinstance(i, int) else y + lax.div(i, 4) + j // 2, 4)
    z = lax.rem(z + j % 4, 4)
    core = lax.rem(lax.rem(narrow, 2) + j // 4, 2)
    return (x * 2 + lax.div(z, 2)) * 4 + y, lax.rem(z, 2) * 2 + core


def columns(ref, row, device):
    return ref.at[pl.ds(pl.multiple_of(row * NPIX + device * OWN, 16), OWN)]


def exchange(row, source, target, send_sem, recv_sem):
    def send(i, j):
        wide, narrow = partner(i, j)
        pltpu.make_async_remote_copy(
            src_ref=source(wide * 4 + narrow),
            dst_ref=target,
            send_sem=send_sem.at[row],
            recv_sem=recv_sem.at[row],
            device_id=(wide, narrow),
            device_id_type=pl.DeviceIdType.MESH,
        ).start()

    @pl.loop(1, 16)
    def _(i):
        for j in range(8):
            send(i, j)

    for j in range(1, 8):
        send(0, j)


def wait_all(row, buffer, sem):
    block = buffer.at[row, pl.ds(0, NDEV - 1)]
    pltpu.make_async_copy(block, block, sem.at[row]).wait()


def wait_rows(row, buffer, sem):
    block = buffer.at[pl.ds(row * NPIX, (NDEV - 1) * OWN)]
    pltpu.make_async_copy(block, block, sem.at[row]).wait()


def widen(landing, work, block):
    for k in range(BLOCK):
        c = block * BLOCK + k
        value = landing[pl.ds(pl.multiple_of(c * FLAT, 16), FLAT), :]
        work[pl.ds(pl.multiple_of(c * REACH, 8), FLAT), :] = value.astype(F32)


def narrow_down(leave, work, block):
    for k in range(BLOCK):
        c = block * BLOCK + k
        value = work[pl.ds(pl.multiple_of(c * REACH, 8), FLAT), :]
        leave[pl.ds(pl.multiple_of(c * FLAT, 16), FLAT), :] = value.astype(BF)


def turn_in(row, tile, work, marks, sent):
    block = work[pl.ds(tile * ROWS + row, SIDE, stride=REACH), :]
    turned = jnp.where(marks[0:1, :] > 0.0, FLAGGED, block.T)
    sent[pl.ds(pl.multiple_of(row * NPIX + tile * SIDE, SIDE), SIDE), :] = turned.astype(BF)


def make_marks(flags, marks):
    lane = lax.broadcasted_iota(jnp.int32, (8, SIDE), 1)
    value = jnp.zeros((8, SIDE), F32)
    for f in range(SIDE // FLAGBLK):
        inside = (lane >= f * FLAGBLK) & (lane < (f + 1) * FLAGBLK)
        value = jnp.where(inside, flags[f].astype(F32), value)
    marks[...] = value


def make_taps(width, taps):
    w = jnp.broadcast_to(width[...], (8, SIDE))
    raw = [jnp.exp(-float((HALF - j) ** 2) / (2.0 * w * w)) for j in range(HALF + 1)]
    total = raw[HALF]
    for j in range(HALF):
        total = total + 2.0 * raw[j]
    for j in range(HALF + 1):
        taps[j] = raw[j] / total


def make_gain(line, gain):
    half = SIDE // 2

    def exact(a, b):
        return jnp.dot(a, b, preferred_element_type=F32, precision=lax.Precision.HIGHEST)

    low = line[...]
    row = lax.broadcasted_iota(jnp.int32, (half, HROWS), 0)
    col = lax.broadcasted_iota(jnp.int32, (half, HROWS), 1)
    first = lax.broadcasted_iota(jnp.int32, (SIDE, SIDE), 0)
    second = lax.broadcasted_iota(jnp.int32, (SIDE, SIDE), 1)
    turned = exact(jnp.where(row + col == half - 1, 1.0, 0.0), low)
    mirror = exact(turned, jnp.where(first + second == SIDE, 1.0, 0.0))
    edge = exact(jnp.where(row + col == half, 1.0, 0.0), low)
    lane = lax.broadcasted_iota(jnp.int32, (half, SIDE), 1)
    high = jnp.where(lane == 0, edge, mirror)
    gain[...] = jnp.concatenate([low[:half], high], axis=0).T[:HROWS] * (1.0 / NCHAN)


def beam_start(row, back, padded):
    padded[0:HALF, :] = jnp.zeros((HALF, SIDE), F32)
    padded[HALF + NPIX : NPIX + 2 * HALF, :] = jnp.zeros((HALF, SIDE), F32)

    @pl.loop(0, TILES)
    def _(i):
        at = pl.multiple_of(i * SIDE, SIDE)
        padded[pl.ds(at + HALF, SIDE), :] = back[pl.ds(pl.multiple_of(row * NPIX + at, SIDE), SIDE), :].astype(F32)


def beam_tile(row, tile, padded, taps, flat, work):
    at = tile * SIDE
    run = SIDE // 8
    values = [padded[pl.ds(at + t, 8, stride=run), :] for t in range(run + 2 * HALF)]
    for t in range(run):
        total = values[t + HALF] * taps[HALF]
        for j in range(HALF):
            total = total + (values[t + j] + values[t + 2 * HALF - j]) * taps[j]
        flat[pl.ds(t, 8, stride=run), :] = total
    work[pl.ds(tile * ROWS + row, SIDE, stride=REACH), :] = flat[...].T


def strip_kernel(
    cube, flags, line, width, fa, last, waves, turns, mix, full, plain, tiles, continuum,
    work, sent, got, back, padded, flat, marks, taps, gain, hs, mats, xs, z, tt, cl, fw, chol, shown, gathered,
    in_sem, out_sem, go_send, go_recv, home_send, home_recv, own_sem, fit_send, fit_recv,
):
    my_wide, my_narrow, me = place()

    def rows_of(part):
        return pl.ds(pl.multiple_of(part * BLOCK * FLAT, 16), BLOCK * FLAT)

    def cube_part(part):
        return pltpu.make_async_copy(cube.at[rows_of(part)], back.at[rows_of(part)], in_sem.at[part])

    def out_part(part):
        return pltpu.make_async_copy(sent.at[rows_of(part)], tiles.at[rows_of(part)], out_sem.at[part])

    def own_go(row):
        return pltpu.make_async_copy(columns(sent, row, me), got.at[row, me], own_sem.at[row])

    def own_home(row):
        return pltpu.make_async_copy(got.at[row, me], columns(back, row, me), own_sem.at[ROWS + row])

    @pl.loop(0, BLOCKS)
    def _(part):
        cube_part(part).start()

    make_marks(flags, marks)

    @pl.loop(0, BLOCKS)
    def _(part):
        cube_part(part).wait()
        widen(back, work, part)

    for row in range(ROWS):
        @pl.loop(0, TILES, step=4)
        def _(tile):
            for q in range(4):
                turn_in(row, tile + q, work, marks, sent)

        own_go(row).start()
        exchange(row, lambda d: columns(sent, row, d), got.at[row, me], go_send, go_recv)

    make_gain(line, gain)
    make_taps(width, taps)
    make_matrices(gain, waves, turns, hs, mats)

    def fit_target(row):
        return row * (NDEV // ROWS) + me // ROWS

    def fit_remote(row):
        dest = fit_target(row)
        return pltpu.make_async_remote_copy(
            src_ref=shown.at[row],
            dst_ref=gathered.at[me % ROWS],
            send_sem=fit_send.at[row],
            recv_sem=fit_recv.at[me % ROWS],
            device_id=(dest // 4, dest % 4),
            device_id_type=pl.DeviceIdType.MESH,
        )

    def fit_local(row):
        return pltpu.make_async_copy(shown.at[row], gathered.at[me % ROWS], fit_send.at[row])

    for row in range(ROWS):
        own_go(row).wait()
        wait_all(row, got, go_recv)
        rows = got.at[row]
        if row == 0:
            unpack_group(rows, 0, xs)
            fit_setup(xs, full, plain, fw, chol)

        @pl.loop(0, OWN // GROUP)
        def _(g):
            start = pl.multiple_of(g * GROUP, GROUP)
            unpack_group(rows, start, xs)
            spectrum_group(xs, z, start, fa)
            shown[row, pl.ds(start, GROUP), :] = fit_group(z, start, tt, mix, chol, cl)

        filter_row(z, cl, fw, mats)

        @pl.loop(0, OWN // GROUP)
        def _(g):
            start = pl.multiple_of(g * GROUP, GROUP)
            channels_group(xs, z, start, last)
            pack_group(rows, start, xs)

        own_home(row).start()
        exchange(row, lambda d: got.at[row, d], columns(back, row, me), home_send, home_recv)
        dest = fit_target(row)

        @pl.when(dest != me)
        def _():
            fit_remote(row).start()

        @pl.when(dest == me)
        def _():
            fit_local(row).start()

    for row in range(ROWS):
        own_home(row).wait()
        wait_rows(row, back, home_recv)
        beam_start(row, back, padded)

        @pl.loop(0, TILES)
        def _(tile):
            beam_tile(row, tile, padded, taps, flat, work)

    for row in range(ROWS):
        wait_rows(row, sent, go_send)

    @pl.loop(0, BLOCKS)
    def _(part):
        narrow_down(sent, work, part)
        out_part(part).start()

    for row in range(ROWS):
        dest = fit_target(row)

        @pl.when(dest != me)
        def _():
            fit_remote(row).wait_send()

        @pl.when(dest == me)
        def _():
            fit_local(row).wait()

    for slot in range(ROWS):
        source = me % (NDEV // ROWS) * ROWS + slot

        @pl.when(source != me)
        def _():
            block = gathered.at[slot]
            pltpu.make_async_copy(block, block, fit_recv.at[slot]).wait()

    for slot in range(ROWS):
        continuum[slot * OWN : (slot + 1) * OWN, :] = gathered[slot]
    continuum[ROWS * OWN :, :] = jnp.zeros((2 * SIDE - ROWS * OWN, SIDE), F32)
    for row in range(ROWS):
        wait_all(row, got, home_send)

    @pl.loop(0, BLOCKS)
    def _(part):
        out_part(part).wait()


def leave_kernel(tiles, coefs, restored, continuum, buffer, in_sem, out_sem):
    def part(i, source, target, sem):
        rows = pl.ds(pl.multiple_of(i * BLOCK * FLAT, 16), BLOCK * FLAT)
        return pltpu.make_async_copy(source.at[rows], target.at[rows], sem.at[i])

    for i in range(BLOCKS):
        part(i, tiles, buffer, in_sem).start()
    continuum[...] = coefs[...].T[:NBASIS, : ROWS * OWN]
    for i in range(BLOCKS):
        part(i, tiles, buffer, in_sem).wait()
        part(i, buffer, restored, out_sem).start()
    for i in range(BLOCKS):
        part(i, buffer, restored, out_sem).wait()


def params(**more):
    return pltpu.CompilerParams(vmem_limit_bytes=VMEM_BYTES, **more)


def body(cube, flags, line_gain, beam_width):
    tab = {k: jnp.asarray(v) for k, v in tables().items()}
    line = jnp.pad(line_gain, (0, HROWS * SIDE - line_gain.shape[0])).reshape(HROWS, SIDE)
    names = ("fa", "last", "waves", "turns", "mix", "full", "plain")
    ins = [line, beam_width[None, :]] + [tab[n] for n in names]
    dma = pltpu.SemaphoreType.DMA
    vmem = pltpu.VMEM
    flat = cube.reshape(SIDE, ROWS, TILES, SIDE).transpose(0, 2, 1, 3).reshape(SIDE * FLAT, SIDE)
    tiles, coefs = pl.pallas_call(
        strip_kernel,
        in_specs=[pl.BlockSpec(memory_space=pl.ANY), pl.BlockSpec(memory_space=pltpu.SMEM)]
        + [pl.BlockSpec(memory_space=vmem)] * len(ins),
        out_specs=[pl.BlockSpec(memory_space=pl.ANY), pl.BlockSpec(memory_space=vmem)],
        out_shape=[
            jax.ShapeDtypeStruct((SIDE * FLAT, SIDE), BF),
            jax.ShapeDtypeStruct((2 * SIDE, SIDE), F32),
        ],
        scratch_shapes=[
            vmem((SIDE * REACH, SIDE), F32),
            vmem((ROWS * NPIX, SIDE), BF),
            vmem((ROWS, NDEV, OWN, SIDE), BF),
            vmem((ROWS * NPIX, SIDE), BF),
            vmem((NPIX + 2 * HALF, SIDE), F32),
            vmem((SIDE, SIDE), F32),
            vmem((8, SIDE), F32),
            vmem((HALF + 1, 8, SIDE), F32),
            vmem((HROWS, SIDE), F32),
            vmem((2, HROWS, 2 * SIDE), F32),
            vmem((KEPT, 6, SIDE, SIDE), BF),
            vmem((SIDE * GROUP, SIDE), F32),
            vmem((OWN * ZSTEP, SIDE), F32),
            vmem((GROUP * 8, SIDE), F32),
            vmem((OWN, SIDE), BF),
            vmem(((NBASIS + 2) * 2 * HROWS, SIDE), F32),
            vmem((NBASIS * NBASIS, 8, SIDE), F32),
            vmem((ROWS, OWN, SIDE), F32),
            vmem((ROWS, OWN, SIDE), F32),
            dma((BLOCKS,)),
            dma((BLOCKS,)),
            dma((ROWS,)),
            dma((ROWS,)),
            dma((ROWS,)),
            dma((ROWS,)),
            dma((2 * ROWS,)),
            dma((ROWS,)),
            dma((ROWS,)),
        ],
        compiler_params=params(has_side_effects=True),
    )(flat, flags, *ins)
    restored, continuum = pl.pallas_call(
        leave_kernel,
        in_specs=[pl.BlockSpec(memory_space=pl.ANY), pl.BlockSpec(memory_space=vmem)],
        out_specs=[pl.BlockSpec(memory_space=pl.ANY), pl.BlockSpec(memory_space=vmem)],
        out_shape=[
            jax.ShapeDtypeStruct((SIDE * FLAT, SIDE), BF),
            jax.ShapeDtypeStruct((NBASIS, ROWS * OWN), F32),
        ],
        scratch_shapes=[vmem((SIDE * FLAT, SIDE), BF), dma((BLOCKS,)), dma((BLOCKS,))],
        compiler_params=params(),
    )(tiles, coefs)
    restored = restored.reshape(SIDE, TILES, ROWS, SIDE).transpose(0, 2, 1, 3).reshape(SIDE, ROWS, NPIX)
    return (restored, continuum)


def solution(mesh):
    placed = (P(AXES, None, None), P(AXES), P(), P(AXES))
    return jax.shard_map(
        body,
        mesh=mesh,
        in_specs=placed,
        out_specs=(P(AXES, None, None), P(None, AXES)),
        check_vma=False,
    )
```

```python
import functools
import math

import jax
import jax.numpy as jnp
import numpy as np
from jax import lax
from jax.experimental import pallas as pl
from jax.experimental.pallas import tpu as pltpu
from jax.sharding import PartitionSpec as P

NDEV = 128
NBASIS = 6
HALF = 8
FLAGBLK = 16
ROWS = 4
NPIX = 6144
NCHAN = 16384
SIDE = 128
HROWS = 72
OWN = NPIX // NDEV
ZSTEP = 2 * HROWS + 8
KEPT = SIDE // 2 + 1
BINS = 13
FLAGGED = 128.0
LIMIT = 100.0
BF = jnp.bfloat16
F32 = jnp.float32
VMEM_BYTES = 61 * 1024 * 1024
AXES = ("wide", "narrow")


def split3(x):
    hi = x.astype(BF)
    rest = x - hi.astype(np.float64)
    lo = rest.astype(BF)
    return hi, lo, (rest - lo.astype(np.float64)).astype(BF)


def legendre64(x):
    terms = [np.ones_like(x), x]
    for k in range(1, NBASIS - 1):
        terms.append(((2 * k + 1) * x * terms[k] - k * terms[k - 1]) / (k + 1))
    return np.stack(terms[:NBASIS])


@functools.cache
def tables():
    idx = np.arange(SIDE)
    turn = 2.0 * np.pi / SIDE
    half = SIDE // 2 + 1
    cos = np.cos(turn * (np.outer(idx, idx) % SIDE))
    sin = np.sin(turn * (np.outer(idx, idx) % SIDE))
    first = np.zeros((2 * HROWS, SIDE))
    first[:half] = cos[:half]
    first[HROWS : HROWS + half] = -sin[:half]
    plain = first.astype(np.float32)
    slow = legendre64((2.0 * idx + 1.0) / SIDE - 1.0)
    first[half : half + NBASIS] = slow
    fa_hi, fa_lo, fa_rest = split3(first)
    fa_hi = fa_hi.copy()
    fa_hi[HROWS + half : HROWS + half + NBASIS] = fa_rest[half : half + NBASIS]
    chan = np.arange(NCHAN)
    full = legendre64((2.0 * chan + 1.0) / NCHAN - 1.0).reshape(NBASIS, SIDE, SIDE)
    fit = np.linalg.pinv(slow.T)
    mix = np.einsum("ma,kab->kmb", fit, full)
    mix = np.where(np.arange(NBASIS)[None, :, None] <= np.arange(NBASIS)[:, None, None], mix, 0.0)
    times = np.full((half,), 2.0)
    times[0] = times[-1] = 1.0
    last = np.zeros((SIDE, 2 * HROWS))
    last[:, :half] = cos[:, :half] * times
    last[:, HROWS : HROWS + half] = -sin[:, :half] * times
    shift = np.arange(2 * SIDE) - SIDE
    turn_c = np.zeros((HROWS, 2 * SIDE))
    turn_s = np.zeros((HROWS, 2 * SIDE))
    turn_c[:half] = np.cos(2.0 * np.pi / NCHAN * np.outer(idx[:half], shift))
    turn_s[:half] = np.sin(2.0 * np.pi / NCHAN * np.outer(idx[:half], shift))
    l_hi, l_lo, _ = split3(last)
    f = np.float32
    return dict(
        fa=np.concatenate([fa_hi, fa_lo], axis=1), plain=plain, full=full.astype(f), mix=mix.astype(f),
        last=np.concatenate([l_hi, l_lo, l_hi], axis=1),
        waves=np.stack([cos, sin]).astype(f), turns=np.stack([turn_c, turn_s]).astype(f),
    )


def dot(a, b):
    return jnp.dot(a, b, preferred_element_type=F32)


def halves(x):
    hi = x.astype(BF)
    return hi, (x - hi.astype(F32)).astype(BF)


def dot_left(table, x):
    hi, lo = halves(x)
    return dot(table[...], jnp.concatenate([hi, hi, lo], axis=0))


def unpack_row(src, xs):
    @pl.loop(0, SIDE // 8)
    def _(i):
        block = src[pl.ds(i * 8, 8), :, :].astype(F32)
        xs[pl.ds(pl.multiple_of(i * 8 * OWN, 128), 8 * OWN), :] = block.reshape(8 * OWN, SIDE)


def pack_block(dst, i, xs):
    block = xs[pl.ds(pl.multiple_of(i * 8 * OWN, 128), 8 * OWN), :]
    dst[pl.ds(i * 8, 8), :, :] = block.reshape(8, OWN, SIDE).astype(BF)


def fit_setup(xs, full, plain, fw, chol):
    weight = jnp.where(xs[pl.ds(0, SIDE, stride=OWN), :] > LIMIT, 0.0, 1.0)
    gram = {}
    fw[NBASIS * 2 * HROWS :, :] = jnp.zeros((2 * 2 * HROWS, SIDE), F32)
    for i in range(NBASIS):
        weighted = full[i] * weight
        fw[i * 2 * HROWS : (i + 1) * 2 * HROWS, :] = jnp.dot(plain[...], weighted, preferred_element_type=F32, precision=lax.Precision.HIGHEST)
        for j in range(i + 1):
            total = jnp.sum(jnp.sum(weighted * full[j], axis=0, keepdims=True), axis=1, keepdims=True)
            gram[i, j] = jnp.broadcast_to(total, (8, SIDE))
    factor = {}
    for j in range(NBASIS):
        value = gram[j, j]
        for k in range(j):
            value = value - factor[j, k] * factor[j, k]
        factor[j, j] = jnp.sqrt(value)
        for i in range(j + 1, NBASIS):
            value = gram[i, j]
            for k in range(j):
                value = value - factor[i, k] * factor[j, k]
            factor[i, j] = value / factor[j, j]
    for (i, j), value in factor.items():
        chol[i * NBASIS + j] = value


def make_matrices(gain, waves, turns, hs, mats):
    def exact(a, b):
        return jnp.dot(a, b, preferred_element_type=F32, precision=lax.Precision.HIGHEST)

    real, imag = exact(gain[...], waves[0]), exact(gain[...], waves[1])
    real, imag = jnp.concatenate([real, real], axis=1), jnp.concatenate([imag, imag], axis=1)
    hs[0] = real * turns[0] - imag * turns[1]
    hs[1] = real * turns[1] + imag * turns[0]

    @pl.loop(0, KEPT)
    def _(k):
        for part in range(2):
            rows = jnp.broadcast_to(hs[part, pl.ds(k, 1), :], (SIDE, 2 * SIDE))
            matrix = pltpu.roll(rows, 0, 1, stride=1, stride_axis=0)[:, SIDE:]
            hi, lo = halves(matrix)
            mats[k, 2 * part] = hi
            mats[k, 2 * part + 1] = lo
            if part == 1:
                mats[k, 4] = -hi
                mats[k, 5] = -lo


def fit_row(z, mix, chol, cl):
    parts = []
    for m in range(NBASIS):
        main = z[pl.ds(KEPT + m, OWN, stride=ZSTEP), :]
        parts.append(main + z[pl.ds(HROWS + KEPT + m, OWN, stride=ZSTEP), :])

    def entry(i, j):
        return jnp.broadcast_to(chol[i * NBASIS + j, 0:1, :], (OWN, SIDE))

    inner = []
    for k in range(NBASIS):
        total = parts[0] * mix[k, 0:1, :]
        for m in range(1, k + 1):
            total = total + parts[m] * mix[k, m : m + 1, :]
        value = jnp.broadcast_to(jnp.sum(total, axis=1, keepdims=True), (OWN, SIDE))
        for j in range(k):
            value = value - entry(k, j) * inner[j]
        inner.append(value / entry(k, k))
    result = [None] * NBASIS
    for i in reversed(range(NBASIS)):
        value = inner[i]
        for j in range(i + 1, NBASIS):
            value = value - entry(j, i) * result[j]
        result[i] = value / entry(i, i)
    lane = lax.broadcasted_iota(jnp.int32, (OWN, SIDE), 1)
    shown = jnp.zeros((OWN, SIDE), F32)
    parts = jnp.zeros((OWN, SIDE), F32)
    for k in range(NBASIS):
        hi = result[k].astype(BF).astype(F32)
        shown = jnp.where(lane == k, result[k], shown)
        parts = jnp.where((lane == k) | (lane == 16 + k), hi, parts)
        parts = jnp.where(lane == 8 + k, result[k] - hi, parts)
    cl[...] = parts.astype(BF)
    return shown


def spectrum_row(xs, z, fa):
    @pl.loop(0, 8)
    def _(i):
        for h in range(3):
            p = 6 * i + 2 * h
            both = [xs[pl.ds(p + q, SIDE, stride=OWN), :] for q in range(2)]
            x = jnp.concatenate([jnp.where(v > LIMIT, 0.0, v) for v in both], axis=1).astype(BF)
            res = dot(fa[...], jnp.concatenate([x, x], axis=0))
            for q in range(2):
                base = pl.multiple_of((p + q) * ZSTEP, 8)
                z[pl.ds(base, 2 * HROWS), :] = res[:, q * SIDE : (q + 1) * SIDE]


def filter_row(z, cl, fw, mats):
    def rows(k):
        return pl.ds(k, OWN, stride=ZSTEP), pl.ds(k + HROWS, OWN, stride=ZSTEP)

    def one(k, value):
        base = jnp.concatenate(
            [fw[pl.ds(k, 8, stride=2 * HROWS), :], fw[pl.ds(k + HROWS, 8, stride=2 * HROWS), :]], axis=1
        )
        hi = base.astype(BF).astype(F32)
        fill = jnp.zeros((SIDE - 24, 2 * SIDE), F32)
        smooth = dot(cl[...], jnp.concatenate([hi, hi, base - hi, fill], axis=0).astype(BF))
        hi, lo = halves(value - smooth)

        def matrix(part):
            up = jnp.concatenate([mats[k, part], mats[k, 2 + part]], axis=1)
            down = jnp.concatenate([mats[k, 4 + part], mats[k, part]], axis=1)
            return jnp.concatenate([up, down], axis=0)

        both = dot(jnp.concatenate([hi, lo], axis=0), matrix(0))
        return both[:OWN] + both[OWN:] + dot(hi, matrix(1))

    @pl.loop(0, KEPT // BINS)
    def _(i):
        values = []
        for j in range(BINS):
            real, imag = rows(i * BINS + j)
            values.append(jnp.concatenate([z[real, :], z[imag, :]], axis=1))
        values = [one(i * BINS + j, value) for j, value in enumerate(values)]
        for j, value in enumerate(values):
            real, imag = rows(i * BINS + j)
            z[real, :] = value[:, :SIDE]
            z[imag, :] = value[:, SIDE:]


def channels_row(xs, z, last):
    quad = 4

    @pl.loop(0, OWN // (2 * quad))
    def _(i):
        for h in range(2):
            first = (2 * i + h) * quad
            cols = []
            for q in range(quad):
                base = pl.multiple_of((first + q) * ZSTEP, 8)
                cols.append(z[pl.ds(base, 2 * HROWS), :])
            out = dot_left(last, jnp.concatenate(cols, axis=1))
            for q in range(quad):
                xs[pl.ds(first + q, SIDE, stride=OWN), :] = out[:, q * SIDE : (q + 1) * SIDE]


TILES = NPIX // SIDE
FLAT = TILES * ROWS
REACH = FLAT + 8
BLOCK = 8
BLOCKS = SIDE // BLOCK


def place():
    wide, narrow = lax.axis_index("wide"), lax.axis_index("narrow")
    return wide, narrow, wide * 4 + narrow


def columns(ref, row, device):
    return ref.at[pl.ds(pl.multiple_of(row * NPIX + device * OWN, 16), OWN)]


def exchange(row, make, source, target, send_sem, recv_sem):
    _, _, me = place()

    def block_of(i):
        return lax.rem(lax.div(me, 8) + 5 * i, 16)

    def send(i, j):
        device = block_of(i) * 8 + lax.rem(lax.rem(me, 8) + j, 8)
        pltpu.make_async_remote_copy(
            src_ref=source(device),
            dst_ref=target,
            send_sem=send_sem.at[row],
            recv_sem=recv_sem.at[row],
            device_id=(lax.div(device, 4), lax.rem(device, 4)),
            device_id_type=pl.DeviceIdType.MESH,
        ).start()

    make(block_of(0))
    for j in range(1, 8):
        send(0, j)
    make(block_of(1))

    @pl.loop(2, 16)
    def _(i):
        for j in range(8):
            send(i - 1, j)
        make(block_of(i))

    for j in range(8):
        send(15, j)


def wait_all(row, buffer, sem):
    block = buffer.at[row, pl.ds(0, NDEV - 1)]
    pltpu.make_async_copy(block, block, sem.at[row]).wait()


def wait_rows(row, buffer, sem):
    block = buffer.at[pl.ds(row * NPIX, (NDEV - 1) * OWN)]
    pltpu.make_async_copy(block, block, sem.at[row]).wait()


def widen(landing, work, block):
    for k in range(BLOCK):
        c = block * BLOCK + k
        value = landing[pl.ds(pl.multiple_of(c * FLAT, 16), FLAT), :]
        work[pl.ds(pl.multiple_of(c * REACH, 8), FLAT), :] = value.astype(F32)


def narrow_down(leave, work, block):
    for k in range(BLOCK):
        c = block * BLOCK + k
        value = work[pl.ds(pl.multiple_of(c * REACH, 8), FLAT), :]
        leave[pl.ds(pl.multiple_of(c * FLAT, 16), FLAT), :] = value.astype(BF)


def turn_in(row, tile, work, marks, sent):
    block = work[pl.ds(tile * ROWS + row, SIDE, stride=REACH), :]
    turned = jnp.where(marks[0:1, :] > 0.0, FLAGGED, block.T)
    sent[pl.ds(pl.multiple_of(row * NPIX + tile * SIDE, SIDE), SIDE), :] = turned.astype(BF)


def make_marks(flags, marks):
    lane = lax.broadcasted_iota(jnp.int32, (8, SIDE), 1)
    value = jnp.zeros((8, SIDE), F32)
    for f in range(SIDE // FLAGBLK):
        inside = (lane >= f * FLAGBLK) & (lane < (f + 1) * FLAGBLK)
        value = jnp.where(inside, flags[f].astype(F32), value)
    marks[...] = value


def make_taps(width, taps):
    w = jnp.broadcast_to(width[...], (8, SIDE))
    raw = [jnp.exp(-float((HALF - j) ** 2) / (2.0 * w * w)) for j in range(HALF + 1)]
    total = raw[HALF]
    for j in range(HALF):
        total = total + 2.0 * raw[j]
    for j in range(HALF + 1):
        taps[j] = raw[j] / total


def make_gain(line, gain):
    half = SIDE // 2

    def exact(a, b):
        return jnp.dot(a, b, preferred_element_type=F32, precision=lax.Precision.HIGHEST)

    low = line[...]
    row = lax.broadcasted_iota(jnp.int32, (half, HROWS), 0)
    col = lax.broadcasted_iota(jnp.int32, (half, HROWS), 1)
    first = lax.broadcasted_iota(jnp.int32, (SIDE, SIDE), 0)
    second = lax.broadcasted_iota(jnp.int32, (SIDE, SIDE), 1)
    turned = exact(jnp.where(row + col == half - 1, 1.0, 0.0), low)
    mirror = exact(turned, jnp.where(first + second == SIDE, 1.0, 0.0))
    edge = exact(jnp.where(row + col == half, 1.0, 0.0), low)
    lane = lax.broadcasted_iota(jnp.int32, (half, SIDE), 1)
    high = jnp.where(lane == 0, edge, mirror)
    gain[...] = jnp.concatenate([low[:half], high], axis=0).T[:HROWS] * (1.0 / NCHAN)


def beam_start(row, back, padded):
    padded[0:HALF, :] = jnp.zeros((HALF, SIDE), F32)
    padded[HALF + NPIX : NPIX + 2 * HALF, :] = jnp.zeros((HALF, SIDE), F32)

    @pl.loop(0, TILES)
    def _(i):
        at = pl.multiple_of(i * SIDE, SIDE)
        padded[pl.ds(at + HALF, SIDE), :] = back[pl.ds(pl.multiple_of(row * NPIX + at, SIDE), SIDE), :].astype(F32)


def beam_tile(row, tile, padded, taps, flat, work):
    at = tile * SIDE
    run = SIDE // 8
    values = [padded[pl.ds(at + t, 8, stride=run), :] for t in range(run + 2 * HALF)]
    for t in range(run):
        total = values[t + HALF] * taps[HALF]
        for j in range(HALF):
            total = total + (values[t + j] + values[t + 2 * HALF - j]) * taps[j]
        flat[pl.ds(t, 8, stride=run), :] = total


def beam_row(row, padded, taps, flats, work):
    @pl.loop(0, TILES // len(flats))
    def _(i):
        for q, flat in enumerate(flats):
            beam_tile(row, i * len(flats) + q, padded, taps, flat, work)
        for q, flat in enumerate(flats):
            tile = i * len(flats) + q
            work[pl.ds(tile * ROWS + row, SIDE, stride=REACH), :] = flat[...].T


def strip_kernel(
    cube, flags, line, width, fa, last, waves, turns, mix, full, plain, tiles, continuum,
    work, sent, got, back, padded, flat0, flat1, flat2, flat3, marks, taps, gain, hs, mats, xs, z, cl, fw, chol, shown, gathered,
    in_sem, out_sem, go_send, go_recv, home_send, home_recv, own_sem, fit_send, fit_recv,
):
    my_wide, my_narrow, me = place()

    def rows_of(part):
        return pl.ds(pl.multiple_of(part * BLOCK * FLAT, 16), BLOCK * FLAT)

    def cube_part(part):
        return pltpu.make_async_copy(cube.at[rows_of(part)], back.at[rows_of(part)], in_sem.at[part])

    def out_part(part):
        return pltpu.make_async_copy(sent.at[rows_of(part)], tiles.at[rows_of(part)], out_sem.at[part])

    def own_go(row):
        return pltpu.make_async_copy(columns(sent, row, me), got.at[row, me], own_sem.at[row])

    def own_home(row):
        return pltpu.make_async_copy(got.at[row, me], columns(back, row, me), own_sem.at[ROWS + row])

    @pl.loop(0, BLOCKS)
    def _(part):
        cube_part(part).start()

    make_marks(flags, marks)

    @pl.loop(0, BLOCKS)
    def _(part):
        cube_part(part).wait()
        widen(back, work, part)

    for row in range(ROWS):
        def make(block):
            for q in range(3):
                turn_in(row, block * 3 + q, work, marks, sent)

        exchange(row, make, lambda d: columns(sent, row, d), got.at[row, me], go_send, go_recv)
        own_go(row).start()

    make_gain(line, gain)
    make_taps(width, taps)
    make_matrices(gain, waves, turns, hs, mats)

    def fit_target(row):
        return row * (NDEV // ROWS) + me // ROWS

    def fit_remote(row):
        dest = fit_target(row)
        return pltpu.make_async_remote_copy(
            src_ref=shown.at[row],
            dst_ref=gathered.at[me % ROWS],
            send_sem=fit_send.at[row],
            recv_sem=fit_recv.at[me % ROWS],
            device_id=(dest // 4, dest % 4),
            device_id_type=pl.DeviceIdType.MESH,
        )

    def fit_local(row):
        return pltpu.make_async_copy(shown.at[row], gathered.at[me % ROWS], fit_send.at[row])

    for row in range(ROWS):
        own_go(row).wait()
        wait_all(row, got, go_recv)
        rows = got.at[row]
        unpack_row(rows, xs)
        if row == 0:
            fit_setup(xs, full, plain, fw, chol)
        spectrum_row(xs, z, fa)
        shown[row] = fit_row(z, mix, chol, cl)
        filter_row(z, cl, fw, mats)
        channels_row(xs, z, last)
        exchange(
            row, lambda i: pack_block(rows, i, xs), lambda d: got.at[row, d], columns(back, row, me), home_send, home_recv
        )
        own_home(row).start()
        dest = fit_target(row)

        @pl.when(dest != me)
        def _():
            fit_remote(row).start()

        @pl.when(dest == me)
        def _():
            fit_local(row).start()

    for row in range(ROWS):
        own_home(row).wait()
        wait_rows(row, back, home_recv)
        beam_start(row, back, padded)
        beam_row(row, padded, taps, (flat0, flat1, flat2, flat3), work)

    for row in range(ROWS):
        wait_rows(row, sent, go_send)

    @pl.loop(0, BLOCKS)
    def _(part):
        narrow_down(sent, work, part)
        out_part(part).start()

    for row in range(ROWS):
        dest = fit_target(row)

        @pl.when(dest != me)
        def _():
            fit_remote(row).wait_send()

        @pl.when(dest == me)
        def _():
            fit_local(row).wait()

    for slot in range(ROWS):
        source = me % (NDEV // ROWS) * ROWS + slot

        @pl.when(source != me)
        def _():
            block = gathered.at[slot]
            pltpu.make_async_copy(block, block, fit_recv.at[slot]).wait()

    for slot in range(ROWS):
        continuum[slot * OWN : (slot + 1) * OWN, :] = gathered[slot]
    continuum[ROWS * OWN :, :] = jnp.zeros((2 * SIDE - ROWS * OWN, SIDE), F32)
    for row in range(ROWS):
        wait_all(row, got, home_send)

    @pl.loop(0, BLOCKS)
    def _(part):
        out_part(part).wait()


def leave_kernel(tiles, coefs, restored, continuum, buffer, in_sem, out_sem):
    def part(i, source, target, sem):
        rows = pl.ds(pl.multiple_of(i * BLOCK * FLAT, 16), BLOCK * FLAT)
        return pltpu.make_async_copy(source.at[rows], target.at[rows], sem.at[i])

    for i in range(BLOCKS):
        part(i, tiles, buffer, in_sem).start()
    continuum[...] = coefs[...].T[:NBASIS, : ROWS * OWN]
    for i in range(BLOCKS):
        part(i, tiles, buffer, in_sem).wait()
        part(i, buffer, restored, out_sem).start()
    for i in range(BLOCKS):
        part(i, buffer, restored, out_sem).wait()


def params(**more):
    return pltpu.CompilerParams(vmem_limit_bytes=VMEM_BYTES, **more)


def body(cube, flags, line_gain, beam_width):
    tab = {k: jnp.asarray(v) for k, v in tables().items()}
    line = jnp.pad(line_gain, (0, HROWS * SIDE - line_gain.shape[0])).reshape(HROWS, SIDE)
    names = ("fa", "last", "waves", "turns", "mix", "full", "plain")
    ins = [line, beam_width[None, :]] + [tab[n] for n in names]
    dma = pltpu.SemaphoreType.DMA
    vmem = pltpu.VMEM
    flat = cube.reshape(SIDE, ROWS, TILES, SIDE).transpose(0, 2, 1, 3).reshape(SIDE * FLAT, SIDE)
    tiles, coefs = pl.pallas_call(
        strip_kernel,
        in_specs=[pl.BlockSpec(memory_space=pl.ANY), pl.BlockSpec(memory_space=pltpu.SMEM)]
        + [pl.BlockSpec(memory_space=vmem)] * len(ins),
        out_specs=[pl.BlockSpec(memory_space=pl.ANY), pl.BlockSpec(memory_space=vmem)],
        out_shape=[
            jax.ShapeDtypeStruct((SIDE * FLAT, SIDE), BF),
            jax.ShapeDtypeStruct((2 * SIDE, SIDE), F32),
        ],
        scratch_shapes=[
            vmem((SIDE * REACH, SIDE), F32),
            vmem((ROWS * NPIX, SIDE), BF),
            vmem((ROWS, NDEV, OWN, SIDE), BF),
            vmem((ROWS * NPIX, SIDE), BF),
            vmem((NPIX + 2 * HALF, SIDE), F32),
            vmem((SIDE, SIDE), F32),
            vmem((SIDE, SIDE), F32),
            vmem((SIDE, SIDE), F32),
            vmem((SIDE, SIDE), F32),
            vmem((8, SIDE), F32),
            vmem((HALF + 1, 8, SIDE), F32),
            vmem((HROWS, SIDE), F32),
            vmem((2, HROWS, 2 * SIDE), F32),
            vmem((KEPT, 6, SIDE, SIDE), BF),
            vmem((SIDE * OWN, SIDE), F32),
            vmem((OWN * ZSTEP, SIDE), F32),
            vmem((OWN, SIDE), BF),
            vmem(((NBASIS + 2) * 2 * HROWS, SIDE), F32),
            vmem((NBASIS * NBASIS, 8, SIDE), F32),
            vmem((ROWS, OWN, SIDE), F32),
            vmem((ROWS, OWN, SIDE), F32),
            dma((BLOCKS,)),
            dma((BLOCKS,)),
            dma((ROWS,)),
            dma((ROWS,)),
            dma((ROWS,)),
            dma((ROWS,)),
            dma((2 * ROWS,)),
            dma((ROWS,)),
            dma((ROWS,)),
        ],
        compiler_params=params(has_side_effects=True),
    )(flat, flags, *ins)
    restored, continuum = pl.pallas_call(
        leave_kernel,
        in_specs=[pl.BlockSpec(memory_space=pl.ANY), pl.BlockSpec(memory_space=vmem)],
        out_specs=[pl.BlockSpec(memory_space=pl.ANY), pl.BlockSpec(memory_space=vmem)],
        out_shape=[
            jax.ShapeDtypeStruct((SIDE * FLAT, SIDE), BF),
            jax.ShapeDtypeStruct((NBASIS, ROWS * OWN), F32),
        ],
        scratch_shapes=[vmem((SIDE * FLAT, SIDE), BF), dma((BLOCKS,)), dma((BLOCKS,))],
        compiler_params=params(),
    )(tiles, coefs)
    restored = restored.reshape(SIDE, TILES, ROWS, SIDE).transpose(0, 2, 1, 3).reshape(SIDE, ROWS, NPIX)
    return (restored, continuum)


def solution(mesh):
    placed = (P(AXES, None, None), P(AXES), P(), P(AXES))
    return jax.shard_map(
        body,
        mesh=mesh,
        in_specs=placed,
        out_specs=(P(AXES, None, None), P(None, AXES)),
        check_vma=False,
    )
```

```python
import functools
import math

import jax
import jax.numpy as jnp
import numpy as np
from jax import lax
from jax.experimental import pallas as pl
from jax.experimental.pallas import tpu as pltpu
from jax.sharding import PartitionSpec as P

NDEV = 128
NBASIS = 6
HALF = 8
FLAGBLK = 16
ROWS = 4
NPIX = 6144
NCHAN = 16384
SIDE = 128
HROWS = 72
OWN = NPIX // NDEV
ZSTEP = 2 * HROWS + 8
KEPT = SIDE // 2 + 1
BINS = 13
FLAGGED = 128.0
LIMIT = 100.0
BF = jnp.bfloat16
F32 = jnp.float32
VMEM_BYTES = 61 * 1024 * 1024
AXES = ("wide", "narrow")


def split3(x):
    hi = x.astype(BF)
    rest = x - hi.astype(np.float64)
    lo = rest.astype(BF)
    return hi, lo, (rest - lo.astype(np.float64)).astype(BF)


def legendre64(x):
    terms = [np.ones_like(x), x]
    for k in range(1, NBASIS - 1):
        terms.append(((2 * k + 1) * x * terms[k] - k * terms[k - 1]) / (k + 1))
    return np.stack(terms[:NBASIS])


@functools.cache
def tables():
    idx = np.arange(SIDE)
    turn = 2.0 * np.pi / SIDE
    half = SIDE // 2 + 1
    cos = np.cos(turn * (np.outer(idx, idx) % SIDE))
    sin = np.sin(turn * (np.outer(idx, idx) % SIDE))
    first = np.zeros((2 * HROWS, SIDE))
    first[:half] = cos[:half]
    first[HROWS : HROWS + half] = -sin[:half]
    plain = first.astype(np.float32)
    slow = legendre64((2.0 * idx + 1.0) / SIDE - 1.0)
    first[half : half + NBASIS] = slow
    fa_hi, fa_lo, fa_rest = split3(first)
    fa_hi = fa_hi.copy()
    fa_hi[HROWS + half : HROWS + half + NBASIS] = fa_rest[half : half + NBASIS]
    chan = np.arange(NCHAN)
    full = legendre64((2.0 * chan + 1.0) / NCHAN - 1.0).reshape(NBASIS, SIDE, SIDE)
    fit = np.linalg.pinv(slow.T)
    mix = np.einsum("ma,kab->kmb", fit, full)
    mix = np.where(np.arange(NBASIS)[None, :, None] <= np.arange(NBASIS)[:, None, None], mix, 0.0)
    times = np.full((half,), 2.0)
    times[0] = times[-1] = 1.0
    last = np.zeros((SIDE, 2 * HROWS))
    last[:, :half] = cos[:, :half] * times
    last[:, HROWS : HROWS + half] = -sin[:, :half] * times
    shift = np.arange(2 * SIDE) - SIDE
    turn_c = np.zeros((HROWS, 2 * SIDE))
    turn_s = np.zeros((HROWS, 2 * SIDE))
    turn_c[:half] = np.cos(2.0 * np.pi / NCHAN * np.outer(idx[:half], shift))
    turn_s[:half] = np.sin(2.0 * np.pi / NCHAN * np.outer(idx[:half], shift))
    l_hi, l_lo, _ = split3(last)
    f = np.float32
    return dict(
        fa=np.concatenate([fa_hi, fa_lo], axis=1), plain=plain, full=full.astype(f), mix=mix.astype(f),
        last=np.concatenate([l_hi, l_lo, l_hi], axis=1),
        waves=np.stack([cos, sin]).astype(f), turns=np.stack([turn_c, turn_s]).astype(f),
    )


def dot(a, b):
    return jnp.dot(a, b, preferred_element_type=F32)


def halves(x):
    hi = x.astype(BF)
    return hi, (x - hi.astype(F32)).astype(BF)


def dot_left(table, x):
    hi, lo = halves(x)
    return dot(table[...], jnp.concatenate([hi, hi, lo], axis=0))


def unpack_row(src, xs):
    @pl.loop(0, SIDE // 8)
    def _(i):
        block = src[pl.ds(i * 8, 8), :, :].astype(F32)
        xs[pl.ds(pl.multiple_of(i * 8 * OWN, 128), 8 * OWN), :] = block.reshape(8 * OWN, SIDE)


def pack_block(dst, i, xs):
    block = xs[pl.ds(pl.multiple_of(i * 8 * OWN, 128), 8 * OWN), :]
    dst[pl.ds(i * 8, 8), :, :] = block.reshape(8, OWN, SIDE).astype(BF)


def fit_setup(xs, full, plain, fw, chol):
    weight = jnp.where(xs[pl.ds(0, SIDE, stride=OWN), :] > LIMIT, 0.0, 1.0)
    gram = {}
    fw[NBASIS * 2 * HROWS :, :] = jnp.zeros((2 * 2 * HROWS, SIDE), F32)
    for i in range(NBASIS):
        weighted = full[i] * weight
        fw[i * 2 * HROWS : (i + 1) * 2 * HROWS, :] = jnp.dot(plain[...], weighted, preferred_element_type=F32, precision=lax.Precision.HIGHEST)
        for j in range(i + 1):
            total = jnp.sum(jnp.sum(weighted * full[j], axis=0, keepdims=True), axis=1, keepdims=True)
            gram[i, j] = jnp.broadcast_to(total, (8, SIDE))
    factor = {}
    for j in range(NBASIS):
        value = gram[j, j]
        for k in range(j):
            value = value - factor[j, k] * factor[j, k]
        factor[j, j] = jnp.sqrt(value)
        for i in range(j + 1, NBASIS):
            value = gram[i, j]
            for k in range(j):
                value = value - factor[i, k] * factor[j, k]
            factor[i, j] = value / factor[j, j]
    for (i, j), value in factor.items():
        chol[i * NBASIS + j] = value


def make_matrices(gain, waves, turns, hs, mats):
    def exact(a, b):
        return jnp.dot(a, b, preferred_element_type=F32, precision=lax.Precision.HIGHEST)

    real, imag = exact(gain[...], waves[0]), exact(gain[...], waves[1])
    real, imag = jnp.concatenate([real, real], axis=1), jnp.concatenate([imag, imag], axis=1)
    hs[0] = real * turns[0] - imag * turns[1]
    hs[1] = real * turns[1] + imag * turns[0]

    @pl.loop(0, KEPT)
    def _(k):
        for part in range(2):
            rows = jnp.broadcast_to(hs[part, pl.ds(k, 1), :], (SIDE, 2 * SIDE))
            matrix = pltpu.roll(rows, 0, 1, stride=1, stride_axis=0)[:, SIDE:]
            hi, lo = halves(matrix)
            mats[k, 2 * part] = hi
            mats[k, 2 * part + 1] = lo
            if part == 1:
                mats[k, 4] = -hi
                mats[k, 5] = -lo


def fit_row(z, mix, chol, cl):
    parts = []
    for m in range(NBASIS):
        main = z[pl.ds(KEPT + m, OWN, stride=ZSTEP), :]
        parts.append(main + z[pl.ds(HROWS + KEPT + m, OWN, stride=ZSTEP), :])

    def entry(i, j):
        return jnp.broadcast_to(chol[i * NBASIS + j, 0:1, :], (OWN, SIDE))

    inner = []
    for k in range(NBASIS):
        total = parts[0] * mix[k, 0:1, :]
        for m in range(1, k + 1):
            total = total + parts[m] * mix[k, m : m + 1, :]
        value = jnp.broadcast_to(jnp.sum(total, axis=1, keepdims=True), (OWN, SIDE))
        for j in range(k):
            value = value - entry(k, j) * inner[j]
        inner.append(value / entry(k, k))
    result = [None] * NBASIS
    for i in reversed(range(NBASIS)):
        value = inner[i]
        for j in range(i + 1, NBASIS):
            value = value - entry(j, i) * result[j]
        result[i] = value / entry(i, i)
    lane = lax.broadcasted_iota(jnp.int32, (OWN, SIDE), 1)
    shown = jnp.zeros((OWN, SIDE), F32)
    parts = jnp.zeros((OWN, SIDE), F32)
    for k in range(NBASIS):
        hi = result[k].astype(BF).astype(F32)
        shown = jnp.where(lane == k, result[k], shown)
        parts = jnp.where((lane == k) | (lane == 16 + k), hi, parts)
        parts = jnp.where(lane == 8 + k, result[k] - hi, parts)
    cl[...] = parts.astype(BF)
    return shown


def spectrum_row(xs, z, fa):
    @pl.loop(0, 8)
    def _(i):
        for h in range(3):
            p = 6 * i + 2 * h
            both = [xs[pl.ds(p + q, SIDE, stride=OWN), :] for q in range(2)]
            x = jnp.concatenate([jnp.where(v > LIMIT, 0.0, v) for v in both], axis=1).astype(BF)
            res = dot(fa[...], jnp.concatenate([x, x], axis=0))
            for q in range(2):
                base = pl.multiple_of((p + q) * ZSTEP, 8)
                z[pl.ds(base, 2 * HROWS), :] = res[:, q * SIDE : (q + 1) * SIDE]


def filter_row(z, cl, fw, mats):
    def rows(k):
        return pl.ds(k, OWN, stride=ZSTEP), pl.ds(k + HROWS, OWN, stride=ZSTEP)

    def one(k, value):
        base = jnp.concatenate(
            [fw[pl.ds(k, 8, stride=2 * HROWS), :], fw[pl.ds(k + HROWS, 8, stride=2 * HROWS), :]], axis=1
        )
        hi = base.astype(BF).astype(F32)
        fill = jnp.zeros((SIDE - 24, 2 * SIDE), F32)
        smooth = dot(cl[...], jnp.concatenate([hi, hi, base - hi, fill], axis=0).astype(BF))
        hi, lo = halves(value - smooth)

        def matrix(part):
            up = jnp.concatenate([mats[k, part], mats[k, 2 + part]], axis=1)
            down = jnp.concatenate([mats[k, 4 + part], mats[k, part]], axis=1)
            return jnp.concatenate([up, down], axis=0)

        both = dot(jnp.concatenate([hi, lo], axis=0), matrix(0))
        return both[:OWN] + both[OWN:] + dot(hi, matrix(1))

    @pl.loop(0, KEPT // BINS)
    def _(i):
        values = []
        for j in range(BINS):
            real, imag = rows(i * BINS + j)
            values.append(jnp.concatenate([z[real, :], z[imag, :]], axis=1))
        values = [one(i * BINS + j, value) for j, value in enumerate(values)]
        for j, value in enumerate(values):
            real, imag = rows(i * BINS + j)
            z[real, :] = value[:, :SIDE]
            z[imag, :] = value[:, SIDE:]


def channels_row(xs, z, last):
    quad = 4

    @pl.loop(0, OWN // (2 * quad))
    def _(i):
        for h in range(2):
            first = (2 * i + h) * quad
            cols = []
            for q in range(quad):
                base = pl.multiple_of((first + q) * ZSTEP, 8)
                cols.append(z[pl.ds(base, 2 * HROWS), :])
            out = dot_left(last, jnp.concatenate(cols, axis=1))
            for q in range(quad):
                xs[pl.ds(first + q, SIDE, stride=OWN), :] = out[:, q * SIDE : (q + 1) * SIDE]


TILES = NPIX // SIDE
FLAT = TILES * ROWS
REACH = FLAT + 8
PART = 4 * ROWS
PARTS = FLAT // PART
BLOCK = 8
BLOCKS = SIDE // BLOCK


def place():
    wide, narrow = lax.axis_index("wide"), lax.axis_index("narrow")
    return wide, narrow, wide * 4 + narrow


def columns(ref, row, device):
    slab = row * (NPIX // FLAT) + lax.div(device, 4)
    return ref.at[slab, pl.ds(pl.multiple_of(lax.rem(device, 4) * OWN, 16), OWN)]


def partner(i, j):
    wide, narrow, _ = place()
    x, y = lax.div(wide, 8), lax.rem(wide, 4)
    z = lax.rem(lax.div(wide, 4), 2) * 2 + lax.div(narrow, 2)
    x = lax.rem(x + i + j, 4)
    y = lax.rem(y + (i // 4 if isinstance(i, int) else lax.div(i, 4)) + j // 2, 4)
    z = lax.rem(z + j % 4, 4)
    core = lax.rem(lax.rem(narrow, 2) + j // 4, 2)
    return (x * 2 + lax.div(z, 2)) * 4 + y, lax.rem(z, 2) * 2 + core


def exchange(row, source, target, send_sem, recv_sem, beside=None):
    def send(i, j):
        wide, narrow = partner(i, j)
        pltpu.make_async_remote_copy(
            src_ref=source(wide * 4 + narrow),
            dst_ref=target,
            send_sem=send_sem.at[row],
            recv_sem=recv_sem.at[row],
            device_id=(wide, narrow),
            device_id_type=pl.DeviceIdType.MESH,
        ).start()

    @pl.loop(1, 16)
    def _(i):
        for j in range(8):
            send(i, j)
        if beside is not None:
            beside(i)

    for j in range(1, 8):
        send(0, j)
    if beside is not None:
        beside(0)


def wait_all(row, buffer, sem):
    block = buffer.at[row, pl.ds(0, NDEV - 1)]
    pltpu.make_async_copy(block, block, sem.at[row]).wait()


def part_rows(part):
    return pl.ds(pl.multiple_of(part * PART, 16), PART)


def widen(landing, work, part):
    @pl.loop(0, SIDE // 8)
    def _(i):
        for k in range(8):
            c = i * 8 + k
            value = landing[c, part_rows(part), :]
            work[pl.ds(pl.multiple_of(c * REACH + part * PART, 8), PART), :] = value.astype(F32)


def narrow_down(leave, work, block):
    for k in range(BLOCK):
        c = block * BLOCK + k
        value = work[pl.ds(pl.multiple_of(c * REACH, 8), FLAT), :]
        leave[c] = value.astype(BF)


def turn_in(row, tile, work, marks, sent):
    block = work[pl.ds(tile * ROWS + row, SIDE, stride=REACH), :]
    turned = jnp.where(marks[0:1, :] > 0.0, FLAGGED, block.T).astype(BF)
    for h in range(2):
        place_at = tile * 2 + h
        slab = row * (NPIX // FLAT) + lax.div(place_at, 3)
        start = pl.multiple_of(lax.rem(place_at, 3) * (SIDE // 2), 16)
        sent[slab, pl.ds(start, SIDE // 2), :] = turned[h * (SIDE // 2) : (h + 1) * (SIDE // 2)]


def make_marks(flags, marks):
    lane = lax.broadcasted_iota(jnp.int32, (8, SIDE), 1)
    value = jnp.zeros((8, SIDE), F32)
    for f in range(SIDE // FLAGBLK):
        inside = (lane >= f * FLAGBLK) & (lane < (f + 1) * FLAGBLK)
        value = jnp.where(inside, flags[f].astype(F32), value)
    marks[...] = value


def make_taps(width, taps):
    w = jnp.broadcast_to(width[...], (8, SIDE))
    raw = [jnp.exp(-float((HALF - j) ** 2) / (2.0 * w * w)) for j in range(HALF + 1)]
    total = raw[HALF]
    for j in range(HALF):
        total = total + 2.0 * raw[j]
    for j in range(HALF + 1):
        taps[j] = raw[j] / total


def make_gain(line, gain):
    half = SIDE // 2

    def exact(a, b):
        return jnp.dot(a, b, preferred_element_type=F32, precision=lax.Precision.HIGHEST)

    low = jnp.concatenate([line[pl.ds(k * SIDE, SIDE)].reshape(1, SIDE) for k in range(half)], axis=0)
    low = jnp.concatenate([low, jnp.broadcast_to(line[pl.ds(half * SIDE, 1)].reshape(1, 1), (8, SIDE))], axis=0)
    row = lax.broadcasted_iota(jnp.int32, (half, HROWS), 0)
    col = lax.broadcasted_iota(jnp.int32, (half, HROWS), 1)
    first = lax.broadcasted_iota(jnp.int32, (SIDE, SIDE), 0)
    second = lax.broadcasted_iota(jnp.int32, (SIDE, SIDE), 1)
    turned = exact(jnp.where(row + col == half - 1, 1.0, 0.0), low)
    mirror = exact(turned, jnp.where(first + second == SIDE, 1.0, 0.0))
    edge = exact(jnp.where(row + col == half, 1.0, 0.0), low)
    lane = lax.broadcasted_iota(jnp.int32, (half, SIDE), 1)
    high = jnp.where(lane == 0, edge, mirror)
    gain[...] = jnp.concatenate([low[:half], high], axis=0).T[:HROWS] * (1.0 / NCHAN)


def beam_start(row, back, padded):
    padded[0:HALF, :] = jnp.zeros((HALF, SIDE), F32)
    padded[HALF + NPIX : NPIX + 2 * HALF, :] = jnp.zeros((HALF, SIDE), F32)

    @pl.loop(0, NPIX // FLAT)
    def _(i):
        at = pl.multiple_of(i * FLAT + HALF, 8)
        padded[pl.ds(at, FLAT), :] = back[row * (NPIX // FLAT) + i].astype(F32)


def beam_tile(row, tile, padded, taps, flat, work):
    at = tile * SIDE
    run = SIDE // 8
    values = [padded[pl.ds(at + t, 8, stride=run), :] for t in range(run + 2 * HALF)]
    for t in range(run):
        total = values[t + HALF] * taps[HALF]
        for j in range(HALF):
            total = total + (values[t + j] + values[t + 2 * HALF - j]) * taps[j]
        flat[pl.ds(t, 8, stride=run), :] = total


def beam_row(row, padded, taps, flats, work):
    @pl.loop(0, TILES // len(flats))
    def _(i):
        for q, flat in enumerate(flats):
            beam_tile(row, i * len(flats) + q, padded, taps, flat, work)
        for q, flat in enumerate(flats):
            tile = i * len(flats) + q
            work[pl.ds(tile * ROWS + row, SIDE, stride=REACH), :] = flat[...].T


def strip_kernel(
    cube, flags, line, width, fa_in, last_in, waves_in, turns_in, mix_in, full_in, plain_in, tiles, final, continuum,
    work, sent, got, back, padded, flat0, flat1, flat2, flat3, marks, taps, gain, hs, mats, xs, z, cl, fw, chol,
    shown, gathered, fa, last, waves, turns, mix, full, plain,
    in_sem, out_sem, table_sem, go_send, go_recv, home_send, home_recv, own_sem, fit_send, fit_recv,
):
    my_wide, my_narrow, me = place()
    tables_in = (fa_in, last_in, waves_in, turns_in, mix_in, full_in, plain_in)
    tables_at = (fa, last, waves, turns, mix, full, plain)

    def table(n):
        return pltpu.make_async_copy(tables_in[n], tables_at[n], table_sem.at[n])

    def cube_part(part):
        source = cube.at[:, part_rows(part), :]
        return pltpu.make_async_copy(source, back.at[:, part_rows(part), :], in_sem.at[part])

    def out_part(part):
        channels = pl.ds(part * BLOCK, BLOCK)
        return pltpu.make_async_copy(sent.at[channels], tiles.at[channels], out_sem.at[part])

    def home(row):
        return columns(back, row, me) if row < ROWS - 1 else columns(final, 0, me)

    def own_go(row):
        return pltpu.make_async_copy(columns(sent, row, me), got.at[row, me], own_sem.at[row])

    def own_home(row):
        return pltpu.make_async_copy(got.at[row, me], home(row), own_sem.at[ROWS + row])

    for part in range(PARTS):
        cube_part(part).start()
    for n in range(len(tables_in)):
        table(n).start()
    make_marks(flags, marks)

    @pl.loop(0, PARTS)
    def _(part):
        cube_part(part).wait()
        widen(back, work, part)
        for q in range(4):
            turn_in(0, part * 4 + q, work, marks, sent)

    for row in range(ROWS):
        def beside(i):
            for q in range(3):
                turn_in(row + 1, i * 3 + q, work, marks, sent)

        own_go(row).start()
        exchange(
            row, lambda d: columns(sent, row, d), got.at[row, me], go_send, go_recv, beside if row < ROWS - 1 else None
        )

    for n in range(len(tables_in)):
        table(n).wait()
    make_gain(line, gain)
    make_taps(width, taps)
    make_matrices(gain, waves, turns, hs, mats)

    def fit_target(row):
        return row * (NDEV // ROWS) + me // ROWS

    def fit_remote(row):
        dest = fit_target(row)
        return pltpu.make_async_remote_copy(
            src_ref=shown.at[row],
            dst_ref=gathered.at[me % ROWS],
            send_sem=fit_send.at[row],
            recv_sem=fit_recv.at[me % ROWS],
            device_id=(dest // 4, dest % 4),
            device_id_type=pl.DeviceIdType.MESH,
        )

    def fit_local(row):
        return pltpu.make_async_copy(shown.at[row], gathered.at[me % ROWS], fit_send.at[row])

    for row in range(ROWS):
        own_go(row).wait()
        wait_all(row, got, go_recv)
        rows = got.at[row]
        unpack_row(rows, xs)
        if row == 0:
            fit_setup(xs, full, plain, fw, chol)
        spectrum_row(xs, z, fa)
        shown[row] = fit_row(z, mix, chol, cl)
        filter_row(z, cl, fw, mats)
        channels_row(xs, z, last)

        @pl.loop(0, SIDE // 8)
        def _(i):
            pack_block(rows, i, xs)

        own_home(row).start()
        exchange(row, lambda d: got.at[row, d], home(row), home_send, home_recv)
        dest = fit_target(row)

        @pl.when(dest != me)
        def _():
            fit_remote(row).start()

        @pl.when(dest == me)
        def _():
            fit_local(row).start()

    for row in range(ROWS - 1):
        own_home(row).wait()
        wait_all(row, got, home_recv)
        beam_start(row, back, padded)
        beam_row(row, padded, taps, (flat0, flat1, flat2, flat3), work)

    for row in range(ROWS):
        wait_all(row, got, go_send)

    @pl.loop(0, BLOCKS)
    def _(part):
        narrow_down(sent, work, part)
        out_part(part).start()

    for row in range(ROWS):
        dest = fit_target(row)

        @pl.when(dest != me)
        def _():
            fit_remote(row).wait_send()

        @pl.when(dest == me)
        def _():
            fit_local(row).wait()

    for slot in range(ROWS):
        source = me % (NDEV // ROWS) * ROWS + slot

        @pl.when(source != me)
        def _():
            block = gathered.at[slot]
            pltpu.make_async_copy(block, block, fit_recv.at[slot]).wait()

    for slot in range(ROWS):
        continuum[slot * OWN : (slot + 1) * OWN, :] = gathered[slot]
    continuum[ROWS * OWN :, :] = jnp.zeros((2 * SIDE - ROWS * OWN, SIDE), F32)
    own_home(ROWS - 1).wait()
    wait_all(ROWS - 1, got, home_recv)
    for row in range(ROWS):
        wait_all(row, got, home_send)

    @pl.loop(0, BLOCKS)
    def _(part):
        out_part(part).wait()


def leave_kernel(
    tiles, final, width, coefs, restored, continuum,
    landing, leave, last_row, padded, flat0, flat1, flat2, flat3, work, taps, in_sem, out_sem, row_sem,
):
    def in_part(part):
        rows = part_rows(part)
        return pltpu.make_async_copy(tiles.at[:, rows, :], landing.at[:, rows, :], in_sem.at[part])

    def out_part(part):
        rows = part_rows(part)
        return pltpu.make_async_copy(leave.at[:, rows, :], restored.at[:, rows, :], out_sem.at[part])

    def row_part(n):
        slabs = pl.ds(n * 8, 8)
        return pltpu.make_async_copy(final.at[slabs], last_row.at[slabs], row_sem.at[n])

    for n in range(4):
        row_part(n).start()
    for part in range(PARTS):
        in_part(part).start()
    make_taps(width, taps)
    continuum[...] = coefs[...].T[:NBASIS, : ROWS * OWN]
    for n in range(4):
        row_part(n).wait()
    beam_start(0, last_row, padded)
    flats = (flat0, flat1, flat2, flat3)

    @pl.loop(0, PARTS)
    def _(part):
        for q, flat in enumerate(flats):
            beam_tile(0, part * 4 + q, padded, taps, flat, None)
        in_part(part).wait()

        @pl.loop(0, SIDE // 8)
        def _(i):
            for k in range(8):
                c = i * 8 + k
                value = landing[c, part_rows(part), :].astype(F32)
                work[pl.ds(pl.multiple_of(c * (PART + 8), 8), PART), :] = value

        for q, flat in enumerate(flats):
            work[pl.ds(q * ROWS + ROWS - 1, SIDE, stride=PART + 8), :] = flat[...].T

        @pl.loop(0, SIDE // 8)
        def _(i):
            for k in range(8):
                c = i * 8 + k
                value = work[pl.ds(pl.multiple_of(c * (PART + 8), 8), PART), :]
                leave[c, part_rows(part), :] = value.astype(BF)

        out_part(part).start()

    @pl.loop(0, PARTS)
    def _(part):
        out_part(part).wait()


def params(**more):
    return pltpu.CompilerParams(vmem_limit_bytes=VMEM_BYTES, **more)


def body(cube, flags, line_gain, beam_width):
    tab = tables()
    names = ("fa", "last", "waves", "turns", "mix", "full", "plain")
    ins = [jnp.asarray(tab[n]) for n in names]
    width = beam_width[None, :]
    dma = pltpu.SemaphoreType.DMA
    vmem = pltpu.VMEM
    hbm = pl.BlockSpec(memory_space=pl.ANY)
    near = pl.BlockSpec(memory_space=vmem)
    slabs = (SIDE, FLAT, SIDE)
    row_slabs = (NPIX // FLAT, FLAT, SIDE)
    flat_tile = [vmem((SIDE, SIDE), F32)] * 4
    flat = cube.reshape(SIDE, ROWS, TILES, SIDE).transpose(0, 2, 1, 3).reshape(slabs)
    tiles, final, coefs = pl.pallas_call(
        strip_kernel,
        in_specs=[hbm, pl.BlockSpec(memory_space=pltpu.SMEM), near, near] + [hbm] * len(ins),
        out_specs=[hbm, hbm, near],
        out_shape=[
            jax.ShapeDtypeStruct(slabs, BF),
            jax.ShapeDtypeStruct(row_slabs, BF),
            jax.ShapeDtypeStruct((2 * SIDE, SIDE), F32),
        ],
        scratch_shapes=[
            vmem((SIDE * REACH, SIDE), F32),
            vmem(slabs, BF),
            vmem((ROWS, NDEV, OWN, SIDE), BF),
            vmem(slabs, BF),
            vmem((NPIX + 2 * HALF, SIDE), F32),
            *flat_tile,
            vmem((8, SIDE), F32),
            vmem((HALF + 1, 8, SIDE), F32),
            vmem((HROWS, SIDE), F32),
            vmem((2, HROWS, 2 * SIDE), F32),
            vmem((KEPT, 6, SIDE, SIDE), BF),
            vmem((SIDE * OWN, SIDE), F32),
            vmem((OWN * ZSTEP, SIDE), F32),
            vmem((OWN, SIDE), BF),
            vmem(((NBASIS + 2) * 2 * HROWS, SIDE), F32),
            vmem((NBASIS * NBASIS, 8, SIDE), F32),
            vmem((ROWS, OWN, SIDE), F32),
            vmem((ROWS, OWN, SIDE), F32),
            *[vmem(t.shape, t.dtype) for t in ins],
            dma((PARTS,)),
            dma((BLOCKS,)),
            dma((len(ins),)),
            dma((ROWS,)),
            dma((ROWS,)),
            dma((ROWS,)),
            dma((ROWS,)),
            dma((2 * ROWS,)),
            dma((ROWS,)),
            dma((ROWS,)),
        ],
        compiler_params=params(has_side_effects=True),
    )(flat, flags, line_gain, width, *ins)
    restored, continuum = pl.pallas_call(
        leave_kernel,
        in_specs=[hbm, hbm, near, near],
        out_specs=[hbm, near],
        out_shape=[
            jax.ShapeDtypeStruct(slabs, BF),
            jax.ShapeDtypeStruct((NBASIS, ROWS * OWN), F32),
        ],
        scratch_shapes=[
            vmem(slabs, BF),
            vmem(slabs, BF),
            vmem(row_slabs, BF),
            vmem((NPIX + 2 * HALF, SIDE), F32),
            *flat_tile,
            vmem((SIDE * (PART + 8), SIDE), F32),
            vmem((HALF + 1, 8, SIDE), F32),
            dma((PARTS,)),
            dma((PARTS,)),
            dma((4,)),
        ],
        compiler_params=params(),
    )(tiles, final, width, coefs)
    restored = restored.reshape(SIDE, TILES, ROWS, SIDE).transpose(0, 2, 1, 3).reshape(SIDE, ROWS, NPIX)
    return (restored, continuum)


def solution(mesh):
    placed = (P(AXES, None, None), P(AXES), P(), P(AXES))
    return jax.shard_map(
        body,
        mesh=mesh,
        in_specs=placed,
        out_specs=(P(AXES, None, None), P(None, AXES)),
        check_vma=False,
    )
```

```python
import functools
import math

import jax
import jax.numpy as jnp
import numpy as np
from jax import lax
from jax.experimental import pallas as pl
from jax.experimental.pallas import tpu as pltpu
from jax.sharding import PartitionSpec as P

NDEV = 128
NBASIS = 6
HALF = 8
FLAGBLK = 16
ROWS = 4
NPIX = 6144
NCHAN = 16384
SIDE = 128
HROWS = 72
OWN = NPIX // NDEV
ZSTEP = 2 * HROWS + 8
KEPT = SIDE // 2 + 1
BINS = 13
FLAGGED = 128.0
LIMIT = 100.0
BF = jnp.bfloat16
F32 = jnp.float32
VMEM_BYTES = 61 * 1024 * 1024
AXES = ("wide", "narrow")


def split3(x):
    hi = x.astype(BF)
    rest = x - hi.astype(np.float64)
    lo = rest.astype(BF)
    return hi, lo, (rest - lo.astype(np.float64)).astype(BF)


def legendre64(x):
    terms = [np.ones_like(x), x]
    for k in range(1, NBASIS - 1):
        terms.append(((2 * k + 1) * x * terms[k] - k * terms[k - 1]) / (k + 1))
    return np.stack(terms[:NBASIS])


@functools.cache
def tables():
    idx = np.arange(SIDE)
    turn = 2.0 * np.pi / SIDE
    half = SIDE // 2 + 1
    cos = np.cos(turn * (np.outer(idx, idx) % SIDE))
    sin = np.sin(turn * (np.outer(idx, idx) % SIDE))
    first = np.zeros((2 * HROWS, SIDE))
    first[:half] = cos[:half]
    first[HROWS : HROWS + half] = -sin[:half]
    plain = first.astype(np.float32)
    slow = legendre64((2.0 * idx + 1.0) / SIDE - 1.0)
    first[half : half + NBASIS] = slow
    fa_hi, fa_lo, fa_rest = split3(first)
    fa_hi = fa_hi.copy()
    fa_hi[HROWS + half : HROWS + half + NBASIS] = fa_rest[half : half + NBASIS]
    chan = np.arange(NCHAN)
    full = legendre64((2.0 * chan + 1.0) / NCHAN - 1.0).reshape(NBASIS, SIDE, SIDE)
    fit = np.linalg.pinv(slow.T)
    mix = np.einsum("ma,kab->kmb", fit, full)
    mix = np.where(np.arange(NBASIS)[None, :, None] <= np.arange(NBASIS)[:, None, None], mix, 0.0)
    times = np.full((half,), 2.0)
    times[0] = times[-1] = 1.0
    last = np.zeros((SIDE, 2 * HROWS))
    last[:, :half] = cos[:, :half] * times
    last[:, HROWS : HROWS + half] = -sin[:, :half] * times
    shift = np.arange(2 * SIDE) - SIDE
    turn_c = np.zeros((HROWS, 2 * SIDE))
    turn_s = np.zeros((HROWS, 2 * SIDE))
    turn_c[:half] = np.cos(2.0 * np.pi / NCHAN * np.outer(idx[:half], shift))
    turn_s[:half] = np.sin(2.0 * np.pi / NCHAN * np.outer(idx[:half], shift))
    l_hi, l_lo, _ = split3(last)
    f = np.float32
    return dict(
        fa=np.concatenate([fa_hi, fa_lo], axis=1), plain=plain, full=full.astype(f), mix=mix.astype(f),
        last=np.concatenate([l_hi, l_lo, l_hi], axis=1),
        waves=np.stack([cos, sin]).astype(f), turns=np.stack([turn_c, turn_s]).astype(f),
    )


def dot(a, b):
    return jnp.dot(a, b, preferred_element_type=F32)


def halves(x):
    hi = x.astype(BF)
    return hi, (x - hi.astype(F32)).astype(BF)


def dot_left(table, x):
    hi, lo = halves(x)
    return dot(table[...], jnp.concatenate([hi, hi, lo], axis=0))


def unpack_row(src, xs):
    @pl.loop(0, SIDE // 8)
    def _(i):
        block = src[pl.ds(i * 8, 8), :, :].astype(F32)
        xs[pl.ds(pl.multiple_of(i * 8 * OWN, 128), 8 * OWN), :] = block.reshape(8 * OWN, SIDE)


def pack_block(dst, i, xs):
    block = xs[pl.ds(pl.multiple_of(i * 8 * OWN, 128), 8 * OWN), :]
    dst[pl.ds(i * 8, 8), :, :] = block.reshape(8, OWN, SIDE).astype(BF)


def fit_setup(xs, full, plain, fw, chol):
    weight = jnp.where(xs[pl.ds(0, SIDE, stride=OWN), :] > LIMIT, 0.0, 1.0)
    gram = {}
    fw[NBASIS * 2 * HROWS :, :] = jnp.zeros((2 * 2 * HROWS, SIDE), F32)
    for i in range(NBASIS):
        weighted = full[i] * weight
        fw[i * 2 * HROWS : (i + 1) * 2 * HROWS, :] = jnp.dot(plain[...], weighted, preferred_element_type=F32, precision=lax.Precision.HIGHEST)
        for j in range(i + 1):
            total = jnp.sum(jnp.sum(weighted * full[j], axis=0, keepdims=True), axis=1, keepdims=True)
            gram[i, j] = jnp.broadcast_to(total, (8, SIDE))
    factor = {}
    for j in range(NBASIS):
        value = gram[j, j]
        for k in range(j):
            value = value - factor[j, k] * factor[j, k]
        factor[j, j] = jnp.sqrt(value)
        for i in range(j + 1, NBASIS):
            value = gram[i, j]
            for k in range(j):
                value = value - factor[i, k] * factor[j, k]
            factor[i, j] = value / factor[j, j]
    for (i, j), value in factor.items():
        chol[i * NBASIS + j] = value


def make_matrices(gain, waves, turns, hs, mats):
    def exact(a, b):
        return jnp.dot(a, b, preferred_element_type=F32, precision=lax.Precision.HIGHEST)

    real, imag = exact(gain[...], waves[0]), exact(gain[...], waves[1])
    real, imag = jnp.concatenate([real, real], axis=1), jnp.concatenate([imag, imag], axis=1)
    hs[0] = real * turns[0] - imag * turns[1]
    hs[1] = real * turns[1] + imag * turns[0]

    @pl.loop(0, KEPT)
    def _(k):
        for part in range(2):
            rows = jnp.broadcast_to(hs[part, pl.ds(k, 1), :], (SIDE, 2 * SIDE))
            matrix = pltpu.roll(rows, 0, 1, stride=1, stride_axis=0)[:, SIDE:]
            hi, lo = halves(matrix)
            mats[k, 2 * part] = hi
            mats[k, 2 * part + 1] = lo
            if part == 1:
                mats[k, 4] = -hi
                mats[k, 5] = -lo


def fit_row(z, mix, chol, cl):
    parts = []
    for m in range(NBASIS):
        main = z[pl.ds(KEPT + m, OWN, stride=ZSTEP), :]
        parts.append(main + z[pl.ds(HROWS + KEPT + m, OWN, stride=ZSTEP), :])

    def entry(i, j):
        return jnp.broadcast_to(chol[i * NBASIS + j, 0:1, :], (OWN, SIDE))

    inner = []
    for k in range(NBASIS):
        total = parts[0] * mix[k, 0:1, :]
        for m in range(1, k + 1):
            total = total + parts[m] * mix[k, m : m + 1, :]
        value = jnp.broadcast_to(jnp.sum(total, axis=1, keepdims=True), (OWN, SIDE))
        for j in range(k):
            value = value - entry(k, j) * inner[j]
        inner.append(value / entry(k, k))
    result = [None] * NBASIS
    for i in reversed(range(NBASIS)):
        value = inner[i]
        for j in range(i + 1, NBASIS):
            value = value - entry(j, i) * result[j]
        result[i] = value / entry(i, i)
    lane = lax.broadcasted_iota(jnp.int32, (OWN, SIDE), 1)
    shown = jnp.zeros((OWN, SIDE), F32)
    parts = jnp.zeros((OWN, SIDE), F32)
    for k in range(NBASIS):
        hi = result[k].astype(BF).astype(F32)
        shown = jnp.where(lane == k, result[k], shown)
        parts = jnp.where((lane == k) | (lane == 16 + k), hi, parts)
        parts = jnp.where(lane == 8 + k, result[k] - hi, parts)
    cl[...] = parts.astype(BF)
    return shown


def spectrum_row(xs, z, fa):
    @pl.loop(0, 8)
    def _(i):
        for h in range(3):
            p = 6 * i + 2 * h
            both = [xs[pl.ds(p + q, SIDE, stride=OWN), :] for q in range(2)]
            x = jnp.concatenate([jnp.where(v > LIMIT, 0.0, v) for v in both], axis=1).astype(BF)
            res = dot(fa[...], jnp.concatenate([x, x], axis=0))
            for q in range(2):
                base = pl.multiple_of((p + q) * ZSTEP, 8)
                z[pl.ds(base, 2 * HROWS), :] = res[:, q * SIDE : (q + 1) * SIDE]


def filter_row(z, cl, fw, mats):
    def rows(k):
        return pl.ds(k, OWN, stride=ZSTEP), pl.ds(k + HROWS, OWN, stride=ZSTEP)

    def one(k, value):
        base = jnp.concatenate(
            [fw[pl.ds(k, 8, stride=2 * HROWS), :], fw[pl.ds(k + HROWS, 8, stride=2 * HROWS), :]], axis=1
        )
        hi = base.astype(BF).astype(F32)
        fill = jnp.zeros((SIDE - 24, 2 * SIDE), F32)
        smooth = dot(cl[...], jnp.concatenate([hi, hi, base - hi, fill], axis=0).astype(BF))
        hi, lo = halves(value - smooth)

        def matrix(part):
            up = jnp.concatenate([mats[k, part], mats[k, 2 + part]], axis=1)
            down = jnp.concatenate([mats[k, 4 + part], mats[k, part]], axis=1)
            return jnp.concatenate([up, down], axis=0)

        both = dot(jnp.concatenate([hi, lo], axis=0), matrix(0))
        return both[:OWN] + both[OWN:] + dot(hi, matrix(1))

    @pl.loop(0, KEPT // BINS)
    def _(i):
        values = []
        for j in range(BINS):
            real, imag = rows(i * BINS + j)
            values.append(jnp.concatenate([z[real, :], z[imag, :]], axis=1))
        values = [one(i * BINS + j, value) for j, value in enumerate(values)]
        for j, value in enumerate(values):
            real, imag = rows(i * BINS + j)
            z[real, :] = value[:, :SIDE]
            z[imag, :] = value[:, SIDE:]


def channels_row(xs, z, last):
    quad = 4

    @pl.loop(0, OWN // (2 * quad))
    def _(i):
        for h in range(2):
            first = (2 * i + h) * quad
            cols = []
            for q in range(quad):
                base = pl.multiple_of((first + q) * ZSTEP, 8)
                cols.append(z[pl.ds(base, 2 * HROWS), :])
            out = dot_left(last, jnp.concatenate(cols, axis=1))
            for q in range(quad):
                xs[pl.ds(first + q, SIDE, stride=OWN), :] = out[:, q * SIDE : (q + 1) * SIDE]


TILES = NPIX // SIDE
FLAT = TILES * ROWS
REACH = FLAT + 8
PART = 4 * ROWS
PARTS = FLAT // PART
BLOCK = 8
BLOCKS = SIDE // BLOCK


def place():
    wide, narrow = lax.axis_index("wide"), lax.axis_index("narrow")
    return wide, narrow, wide * 4 + narrow


def columns(ref, row, device):
    slab = row * (NPIX // FLAT) + lax.div(device, 4)
    return ref.at[slab, pl.ds(pl.multiple_of(lax.rem(device, 4) * OWN, 16), OWN)]


def partner(i, j):
    wide, narrow, _ = place()
    x, y = lax.div(wide, 8), lax.rem(wide, 4)
    z = lax.rem(lax.div(wide, 4), 2) * 2 + lax.div(narrow, 2)
    step = (0, 2, 1, 3)[j % 4]
    x = lax.rem(x + step, 4)
    y = lax.rem(y + step + i % 4 if isinstance(i, int) else y + step + lax.rem(i, 4), 4)
    z = lax.rem(z + step + (i // 4 if isinstance(i, int) else lax.div(i, 4)), 4)
    core = lax.rem(lax.rem(narrow, 2) + j // 4, 2)
    return (x * 2 + lax.div(z, 2)) * 4 + y, lax.rem(z, 2) * 2 + core


def exchange(row, source, target, send_sem, recv_sem, beside=None):
    def send(i, j):
        wide, narrow = partner(i, j)
        pltpu.make_async_remote_copy(
            src_ref=source(wide * 4 + narrow),
            dst_ref=target,
            send_sem=send_sem.at[row],
            recv_sem=recv_sem.at[row],
            device_id=(wide, narrow),
            device_id_type=pl.DeviceIdType.MESH,
        ).start()

    @pl.loop(1, 16)
    def _(i):
        for j in range(8):
            send(i, j)
        if beside is not None:
            beside(i)

    for j in range(1, 8):
        send(0, j)
    if beside is not None:
        beside(0)


def wait_all(row, buffer, sem):
    block = buffer.at[row, pl.ds(0, NDEV - 1)]
    pltpu.make_async_copy(block, block, sem.at[row]).wait()


def part_rows(part):
    return pl.ds(pl.multiple_of(part * PART, 16), PART)


def widen(landing, work, part):
    @pl.loop(0, SIDE // 32)
    def _(i):
        for k in range(32):
            c = i * 32 + k
            value = landing[c, part_rows(part), :]
            work[pl.ds(pl.multiple_of(c * REACH + part * PART, 8), PART), :] = value.astype(F32)


def narrow_down(leave, work, block):
    for k in range(BLOCK):
        c = block * BLOCK + k
        value = work[pl.ds(pl.multiple_of(c * REACH, 8), FLAT), :]
        leave[c] = value.astype(BF)


def turn_in(row, tile, work, marks, sent):
    block = work[pl.ds(tile * ROWS + row, SIDE, stride=REACH), :]
    turned = jnp.where(marks[0:1, :] > 0.0, FLAGGED, block.T).astype(BF)
    for h in range(2):
        place_at = tile * 2 + h
        slab = row * (NPIX // FLAT) + lax.div(place_at, 3)
        start = pl.multiple_of(lax.rem(place_at, 3) * (SIDE // 2), 16)
        sent[slab, pl.ds(start, SIDE // 2), :] = turned[h * (SIDE // 2) : (h + 1) * (SIDE // 2)]


def make_marks(flags, marks):
    lane = lax.broadcasted_iota(jnp.int32, (8, SIDE), 1)
    value = jnp.zeros((8, SIDE), F32)
    for f in range(SIDE // FLAGBLK):
        inside = (lane >= f * FLAGBLK) & (lane < (f + 1) * FLAGBLK)
        value = jnp.where(inside, flags[f].astype(F32), value)
    marks[...] = value


def make_taps(width, taps):
    w = jnp.broadcast_to(width[...], (8, SIDE))
    raw = [jnp.exp(-float((HALF - j) ** 2) / (2.0 * w * w)) for j in range(HALF + 1)]
    total = raw[HALF]
    for j in range(HALF):
        total = total + 2.0 * raw[j]
    for j in range(HALF + 1):
        taps[j] = raw[j] / total


def make_gain(line, gain):
    half = SIDE // 2

    def exact(a, b):
        return jnp.dot(a, b, preferred_element_type=F32, precision=lax.Precision.HIGHEST)

    low = jnp.concatenate([line[pl.ds(k * SIDE, SIDE)].reshape(1, SIDE) for k in range(half)], axis=0)
    low = jnp.concatenate([low, jnp.broadcast_to(line[pl.ds(half * SIDE, 1)].reshape(1, 1), (8, SIDE))], axis=0)
    row = lax.broadcasted_iota(jnp.int32, (half, HROWS), 0)
    col = lax.broadcasted_iota(jnp.int32, (half, HROWS), 1)
    first = lax.broadcasted_iota(jnp.int32, (SIDE, SIDE), 0)
    second = lax.broadcasted_iota(jnp.int32, (SIDE, SIDE), 1)
    turned = exact(jnp.where(row + col == half - 1, 1.0, 0.0), low)
    mirror = exact(turned, jnp.where(first + second == SIDE, 1.0, 0.0))
    edge = exact(jnp.where(row + col == half, 1.0, 0.0), low)
    lane = lax.broadcasted_iota(jnp.int32, (half, SIDE), 1)
    high = jnp.where(lane == 0, edge, mirror)
    gain[...] = jnp.concatenate([low[:half], high], axis=0).T[:HROWS] * (1.0 / NCHAN)


def beam_start(row, back, padded):
    padded[0:HALF, :] = jnp.zeros((HALF, SIDE), F32)
    padded[HALF + NPIX : NPIX + 2 * HALF, :] = jnp.zeros((HALF, SIDE), F32)

    @pl.loop(0, NPIX // FLAT)
    def _(i):
        at = pl.multiple_of(i * FLAT + HALF, 8)
        padded[pl.ds(at, FLAT), :] = back[row * (NPIX // FLAT) + i].astype(F32)


def beam_tile(row, tile, padded, taps, flat, work):
    at = tile * SIDE
    run = SIDE // 8
    values = [padded[pl.ds(at + t, 8, stride=run), :] for t in range(run + 2 * HALF)]
    for t in range(run):
        total = values[t + HALF] * taps[HALF]
        for j in range(HALF):
            total = total + (values[t + j] + values[t + 2 * HALF - j]) * taps[j]
        flat[pl.ds(t, 8, stride=run), :] = total


def beam_row(row, padded, taps, flats, work):
    @pl.loop(0, TILES // len(flats))
    def _(i):
        for q, flat in enumerate(flats):
            beam_tile(row, i * len(flats) + q, padded, taps, flat, work)
        for q, flat in enumerate(flats):
            tile = i * len(flats) + q
            work[pl.ds(tile * ROWS + row, SIDE, stride=REACH), :] = flat[...].T


def strip_kernel(
    cube, flags, line, width, fa_in, last_in, waves_in, turns_in, mix_in, full_in, plain_in, tiles, final, continuum,
    work, sent, got, back, padded, flat0, flat1, flat2, flat3, marks, taps, gain, hs, mats, xs, z, cl, fw, chol,
    shown, gathered, fa, last, waves, turns, mix, full, plain,
    in_sem, out_sem, table_sem, go_send, go_recv, home_send, home_recv, own_sem, fit_send, fit_recv,
):
    my_wide, my_narrow, me = place()
    tables_in = (fa_in, last_in, waves_in, turns_in, mix_in, full_in, plain_in)
    tables_at = (fa, last, waves, turns, mix, full, plain)

    def table(n):
        return pltpu.make_async_copy(tables_in[n], tables_at[n], table_sem.at[n])

    def cube_part(part):
        source = cube.at[:, part_rows(part), :]
        return pltpu.make_async_copy(source, back.at[:, part_rows(part), :], in_sem.at[part])

    def out_part(part):
        channels = pl.ds(part * BLOCK, BLOCK)
        return pltpu.make_async_copy(sent.at[channels], tiles.at[channels], out_sem.at[part])

    def home(row):
        return columns(back, row, me) if row < ROWS - 1 else columns(final, 0, me)

    def own_go(row):
        return pltpu.make_async_copy(columns(sent, row, me), got.at[row, me], own_sem.at[row])

    def own_home(row):
        return pltpu.make_async_copy(got.at[row, me], home(row), own_sem.at[ROWS + row])

    for part in range(PARTS):
        cube_part(part).start()
    for n in range(len(tables_in)):
        table(n).start()
    make_marks(flags, marks)

    @pl.loop(0, PARTS)
    def _(part):
        cube_part(part).wait()
        widen(back, work, part)
        for q in range(4):
            turn_in(0, part * 4 + q, work, marks, sent)

    for row in range(ROWS):
        def beside(i):
            for q in range(3):
                turn_in(row + 1, i * 3 + q, work, marks, sent)

        own_go(row).start()
        exchange(
            row, lambda d: columns(sent, row, d), got.at[row, me], go_send, go_recv, beside if row < ROWS - 1 else None
        )

    for n in range(len(tables_in)):
        table(n).wait()
    make_gain(line, gain)
    make_taps(width, taps)
    make_matrices(gain, waves, turns, hs, mats)

    def fit_target(row):
        return row * (NDEV // ROWS) + me // ROWS

    def fit_remote(row):
        dest = fit_target(row)
        return pltpu.make_async_remote_copy(
            src_ref=shown.at[row],
            dst_ref=gathered.at[me % ROWS],
            send_sem=fit_send.at[row],
            recv_sem=fit_recv.at[me % ROWS],
            device_id=(dest // 4, dest % 4),
            device_id_type=pl.DeviceIdType.MESH,
        )

    def fit_local(row):
        return pltpu.make_async_copy(shown.at[row], gathered.at[me % ROWS], fit_send.at[row])

    for row in range(ROWS):
        own_go(row).wait()
        wait_all(row, got, go_recv)
        rows = got.at[row]
        unpack_row(rows, xs)
        if row == 0:
            fit_setup(xs, full, plain, fw, chol)
        spectrum_row(xs, z, fa)
        shown[row] = fit_row(z, mix, chol, cl)
        filter_row(z, cl, fw, mats)
        channels_row(xs, z, last)

        @pl.loop(0, SIDE // 8)
        def _(i):
            pack_block(rows, i, xs)

        own_home(row).start()
        exchange(row, lambda d: got.at[row, d], home(row), home_send, home_recv)
        dest = fit_target(row)

        @pl.when(dest != me)
        def _():
            fit_remote(row).start()

        @pl.when(dest == me)
        def _():
            fit_local(row).start()

    for row in range(ROWS - 1):
        own_home(row).wait()
        wait_all(row, got, home_recv)
        beam_start(row, back, padded)
        beam_row(row, padded, taps, (flat0, flat1, flat2, flat3), work)

    for row in range(ROWS):
        wait_all(row, got, go_send)

    @pl.loop(0, BLOCKS)
    def _(part):
        narrow_down(sent, work, part)
        out_part(part).start()

    for row in range(ROWS):
        dest = fit_target(row)

        @pl.when(dest != me)
        def _():
            fit_remote(row).wait_send()

        @pl.when(dest == me)
        def _():
            fit_local(row).wait()

    for slot in range(ROWS):
        source = me % (NDEV // ROWS) * ROWS + slot

        @pl.when(source != me)
        def _():
            block = gathered.at[slot]
            pltpu.make_async_copy(block, block, fit_recv.at[slot]).wait()

    for slot in range(ROWS):
        continuum[slot * OWN : (slot + 1) * OWN, :] = gathered[slot]
    continuum[ROWS * OWN :, :] = jnp.zeros((2 * SIDE - ROWS * OWN, SIDE), F32)
    own_home(ROWS - 1).wait()
    wait_all(ROWS - 1, got, home_recv)
    for row in range(ROWS):
        wait_all(row, got, home_send)

    @pl.loop(0, BLOCKS)
    def _(part):
        out_part(part).wait()


def leave_kernel(
    tiles, final, width, coefs, restored, continuum,
    landing, leave, last_row, padded, flat0, flat1, flat2, flat3, work, taps, in_sem, out_sem, row_sem,
):
    def in_part(part):
        rows = part_rows(part)
        return pltpu.make_async_copy(tiles.at[:, rows, :], landing.at[:, rows, :], in_sem.at[part])

    def out_part(part):
        rows = part_rows(part)
        return pltpu.make_async_copy(leave.at[:, rows, :], restored.at[:, rows, :], out_sem.at[part])

    def row_part(n):
        slabs = pl.ds(n * 8, 8)
        return pltpu.make_async_copy(final.at[slabs], last_row.at[slabs], row_sem.at[n])

    for n in range(4):
        row_part(n).start()
    for part in range(PARTS):
        in_part(part).start()
    make_taps(width, taps)
    continuum[...] = coefs[...].T[:NBASIS, : ROWS * OWN]
    for n in range(4):
        row_part(n).wait()
    beam_start(0, last_row, padded)
    flats = (flat0, flat1, flat2, flat3)

    @pl.loop(0, PARTS)
    def _(part):
        for q, flat in enumerate(flats):
            beam_tile(0, part * 4 + q, padded, taps, flat, None)
        in_part(part).wait()

        @pl.loop(0, SIDE // 32)
        def _(i):
            for k in range(32):
                c = i * 32 + k
                value = landing[c, part_rows(part), :].astype(F32)
                work[pl.ds(pl.multiple_of(c * (PART + 8), 8), PART), :] = value

        for q, flat in enumerate(flats):
            work[pl.ds(q * ROWS + ROWS - 1, SIDE, stride=PART + 8), :] = flat[...].T

        @pl.loop(0, SIDE // 32)
        def _(i):
            for k in range(32):
                c = i * 32 + k
                value = work[pl.ds(pl.multiple_of(c * (PART + 8), 8), PART), :]
                leave[c, part_rows(part), :] = value.astype(BF)

        out_part(part).start()

    @pl.loop(0, PARTS)
    def _(part):
        out_part(part).wait()


def params(**more):
    return pltpu.CompilerParams(vmem_limit_bytes=VMEM_BYTES, **more)


def body(cube, flags, line_gain, beam_width):
    tab = tables()
    names = ("fa", "last", "waves", "turns", "mix", "full", "plain")
    ins = [jnp.asarray(tab[n]) for n in names]
    width = beam_width[None, :]
    dma = pltpu.SemaphoreType.DMA
    vmem = pltpu.VMEM
    hbm = pl.BlockSpec(memory_space=pl.ANY)
    near = pl.BlockSpec(memory_space=vmem)
    slabs = (SIDE, FLAT, SIDE)
    row_slabs = (NPIX // FLAT, FLAT, SIDE)
    flat_tile = [vmem((SIDE, SIDE), F32)] * 4
    flat = cube.reshape(SIDE, ROWS, TILES, SIDE).transpose(0, 2, 1, 3).reshape(slabs)
    tiles, final, coefs = pl.pallas_call(
        strip_kernel,
        in_specs=[hbm, pl.BlockSpec(memory_space=pltpu.SMEM), near, near] + [hbm] * len(ins),
        out_specs=[hbm, hbm, near],
        out_shape=[
            jax.ShapeDtypeStruct(slabs, BF),
            jax.ShapeDtypeStruct(row_slabs, BF),
            jax.ShapeDtypeStruct((2 * SIDE, SIDE), F32),
        ],
        scratch_shapes=[
            vmem((SIDE * REACH, SIDE), F32),
            vmem(slabs, BF),
            vmem((ROWS, NDEV, OWN, SIDE), BF),
            vmem(slabs, BF),
            vmem((NPIX + 2 * HALF, SIDE), F32),
            *flat_tile,
            vmem((8, SIDE), F32),
            vmem((HALF + 1, 8, SIDE), F32),
            vmem((HROWS, SIDE), F32),
            vmem((2, HROWS, 2 * SIDE), F32),
            vmem((KEPT, 6, SIDE, SIDE), BF),
            vmem((SIDE * OWN, SIDE), F32),
            vmem((OWN * ZSTEP, SIDE), F32),
            vmem((OWN, SIDE), BF),
            vmem(((NBASIS + 2) * 2 * HROWS, SIDE), F32),
            vmem((NBASIS * NBASIS, 8, SIDE), F32),
            vmem((ROWS, OWN, SIDE), F32),
            vmem((ROWS, OWN, SIDE), F32),
            *[vmem(t.shape, t.dtype) for t in ins],
            dma((PARTS,)),
            dma((BLOCKS,)),
            dma((len(ins),)),
            dma((ROWS,)),
            dma((ROWS,)),
            dma((ROWS,)),
            dma((ROWS,)),
            dma((2 * ROWS,)),
            dma((ROWS,)),
            dma((ROWS,)),
        ],
        compiler_params=params(has_side_effects=True),
    )(flat, flags, line_gain, width, *ins)
    restored, continuum = pl.pallas_call(
        leave_kernel,
        in_specs=[hbm, hbm, near, near],
        out_specs=[hbm, near],
        out_shape=[
            jax.ShapeDtypeStruct(slabs, BF),
            jax.ShapeDtypeStruct((NBASIS, ROWS * OWN), F32),
        ],
        scratch_shapes=[
            vmem(slabs, BF),
            vmem(slabs, BF),
            vmem(row_slabs, BF),
            vmem((NPIX + 2 * HALF, SIDE), F32),
            *flat_tile,
            vmem((SIDE * (PART + 8), SIDE), F32),
            vmem((HALF + 1, 8, SIDE), F32),
            dma((PARTS,)),
            dma((PARTS,)),
            dma((4,)),
        ],
        compiler_params=params(),
    )(tiles, final, width, coefs)
    restored = restored.reshape(SIDE, TILES, ROWS, SIDE).transpose(0, 2, 1, 3).reshape(SIDE, ROWS, NPIX)
    return (restored, continuum)


def solution(mesh):
    placed = (P(AXES, None, None), P(AXES), P(), P(AXES))
    return jax.shard_map(
        body,
        mesh=mesh,
        in_specs=placed,
        out_specs=(P(AXES, None, None), P(None, AXES)),
        check_vma=False,
    )
```

```python
import functools
import math

import jax
import jax.numpy as jnp
import numpy as np
from jax import lax
from jax.experimental import pallas as pl
from jax.experimental.pallas import tpu as pltpu
from jax.sharding import PartitionSpec as P

NDEV = 128
NBASIS = 6
HALF = 8
FLAGBLK = 16
ROWS = 4
NPIX = 6144
NCHAN = 16384
SIDE = 128
HROWS = 72
OWN = NPIX // NDEV
ZSTEP = 2 * HROWS + 8
KEPT = SIDE // 2 + 1
BINS = 13
FLAGGED = 128.0
LIMIT = 100.0
BF = jnp.bfloat16
F32 = jnp.float32
VMEM_BYTES = 61 * 1024 * 1024
AXES = ("wide", "narrow")


def split3(x):
    hi = x.astype(BF)
    rest = x - hi.astype(np.float64)
    lo = rest.astype(BF)
    return hi, lo, (rest - lo.astype(np.float64)).astype(BF)


def legendre64(x):
    terms = [np.ones_like(x), x]
    for k in range(1, NBASIS - 1):
        terms.append(((2 * k + 1) * x * terms[k] - k * terms[k - 1]) / (k + 1))
    return np.stack(terms[:NBASIS])


@functools.cache
def tables():
    idx = np.arange(SIDE)
    turn = 2.0 * np.pi / SIDE
    half = SIDE // 2 + 1
    cos = np.cos(turn * (np.outer(idx, idx) % SIDE))
    sin = np.sin(turn * (np.outer(idx, idx) % SIDE))
    first = np.zeros((2 * HROWS, SIDE))
    first[:half] = cos[:half]
    first[HROWS : HROWS + half] = -sin[:half]
    plain = first.astype(np.float32)
    slow = legendre64((2.0 * idx + 1.0) / SIDE - 1.0)
    first[half : half + NBASIS] = slow
    fa_hi, fa_lo, fa_rest = split3(first)
    fa_hi = fa_hi.copy()
    fa_hi[HROWS + half : HROWS + half + NBASIS] = fa_rest[half : half + NBASIS]
    chan = np.arange(NCHAN)
    full = legendre64((2.0 * chan + 1.0) / NCHAN - 1.0).reshape(NBASIS, SIDE, SIDE)
    fit = np.linalg.pinv(slow.T)
    mix = np.einsum("ma,kab->kmb", fit, full)
    mix = np.where(np.arange(NBASIS)[None, :, None] <= np.arange(NBASIS)[:, None, None], mix, 0.0)
    times = np.full((half,), 2.0)
    times[0] = times[-1] = 1.0
    last = np.zeros((SIDE, 2 * HROWS))
    last[:, :half] = cos[:, :half] * times
    last[:, HROWS : HROWS + half] = -sin[:, :half] * times
    shift = np.arange(2 * SIDE) - SIDE
    turn_c = np.zeros((HROWS, 2 * SIDE))
    turn_s = np.zeros((HROWS, 2 * SIDE))
    turn_c[:half] = np.cos(2.0 * np.pi / NCHAN * np.outer(idx[:half], shift))
    turn_s[:half] = np.sin(2.0 * np.pi / NCHAN * np.outer(idx[:half], shift))
    l_hi, l_lo, _ = split3(last)
    f = np.float32
    return dict(
        fa=np.concatenate([fa_hi, fa_lo], axis=1), plain=plain, full=full.astype(f), mix=mix.astype(f),
        last=np.concatenate([l_hi, l_lo, l_hi], axis=1),
        waves=np.stack([cos, sin]).astype(f), turns=np.stack([turn_c, turn_s]).astype(f),
    )


def dot(a, b):
    return jnp.dot(a, b, preferred_element_type=F32)


def halves(x):
    hi = x.astype(BF)
    return hi, (x - hi.astype(F32)).astype(BF)


def dot_left(table, x):
    hi, lo = halves(x)
    return dot(table[...], jnp.concatenate([hi, hi, lo], axis=0))


def unpack_row(src, xs):
    @pl.loop(0, SIDE // 8)
    def _(i):
        block = src[pl.ds(i * 8, 8), :, :].astype(F32)
        xs[pl.ds(pl.multiple_of(i * 8 * OWN, 128), 8 * OWN), :] = block.reshape(8 * OWN, SIDE)


def pack_block(dst, i, xs):
    block = xs[pl.ds(pl.multiple_of(i * 8 * OWN, 128), 8 * OWN), :]
    dst[pl.ds(i * 8, 8), :, :] = block.reshape(8, OWN, SIDE).astype(BF)


def fit_setup(xs, full, plain, fw, chol):
    weight = jnp.where(xs[pl.ds(0, SIDE, stride=OWN), :] > LIMIT, 0.0, 1.0)
    gram = {}
    fw[NBASIS * 2 * HROWS :, :] = jnp.zeros((2 * 2 * HROWS, SIDE), F32)
    for i in range(NBASIS):
        weighted = full[i] * weight
        fw[i * 2 * HROWS : (i + 1) * 2 * HROWS, :] = jnp.dot(plain[...], weighted, preferred_element_type=F32, precision=lax.Precision.HIGHEST)
        for j in range(i + 1):
            total = jnp.sum(jnp.sum(weighted * full[j], axis=0, keepdims=True), axis=1, keepdims=True)
            gram[i, j] = jnp.broadcast_to(total, (8, SIDE))
    factor = {}
    for j in range(NBASIS):
        value = gram[j, j]
        for k in range(j):
            value = value - factor[j, k] * factor[j, k]
        factor[j, j] = jnp.sqrt(value)
        for i in range(j + 1, NBASIS):
            value = gram[i, j]
            for k in range(j):
                value = value - factor[i, k] * factor[j, k]
            factor[i, j] = value / factor[j, j]
    for (i, j), value in factor.items():
        chol[i * NBASIS + j] = value


def make_matrices(gain, waves, turns, hs, mats, send=None):
    def exact(a, b):
        return jnp.dot(a, b, preferred_element_type=F32, precision=lax.Precision.HIGHEST)

    real, imag = exact(gain[...], waves[0]), exact(gain[...], waves[1])
    real, imag = jnp.concatenate([real, real], axis=1), jnp.concatenate([imag, imag], axis=1)
    hs[0] = real * turns[0] - imag * turns[1]
    hs[1] = real * turns[1] + imag * turns[0]

    def one(k):
        for part in range(2):
            rows = jnp.broadcast_to(hs[part, pl.ds(k, 1), :], (SIDE, 2 * SIDE))
            matrix = pltpu.roll(rows, 0, 1, stride=1, stride_axis=0)[:, SIDE:]
            hi, lo = halves(matrix)
            mats[k, 2 * part] = hi
            mats[k, 2 * part + 1] = lo
            if part == 1:
                mats[k, 4] = -hi
                mats[k, 5] = -lo

    def turn(t):
        for j in range(BINS):
            one(t * BINS + j)

    beside_bins(send, turn)


def fit_row(z, mix, chol, cl):
    parts = []
    for m in range(NBASIS):
        main = z[pl.ds(KEPT + m, OWN, stride=ZSTEP), :]
        parts.append(main + z[pl.ds(HROWS + KEPT + m, OWN, stride=ZSTEP), :])

    def entry(i, j):
        return jnp.broadcast_to(chol[i * NBASIS + j, 0:1, :], (OWN, SIDE))

    inner = []
    for k in range(NBASIS):
        total = parts[0] * mix[k, 0:1, :]
        for m in range(1, k + 1):
            total = total + parts[m] * mix[k, m : m + 1, :]
        value = jnp.broadcast_to(jnp.sum(total, axis=1, keepdims=True), (OWN, SIDE))
        for j in range(k):
            value = value - entry(k, j) * inner[j]
        inner.append(value / entry(k, k))
    result = [None] * NBASIS
    for i in reversed(range(NBASIS)):
        value = inner[i]
        for j in range(i + 1, NBASIS):
            value = value - entry(j, i) * result[j]
        result[i] = value / entry(i, i)
    lane = lax.broadcasted_iota(jnp.int32, (OWN, SIDE), 1)
    shown = jnp.zeros((OWN, SIDE), F32)
    parts = jnp.zeros((OWN, SIDE), F32)
    for k in range(NBASIS):
        hi = result[k].astype(BF).astype(F32)
        shown = jnp.where(lane == k, result[k], shown)
        parts = jnp.where((lane == k) | (lane == 16 + k), hi, parts)
        parts = jnp.where(lane == 8 + k, result[k] - hi, parts)
    cl[...] = parts.astype(BF)
    return shown


def spectrum_row(xs, z, fa):
    @pl.loop(0, 8)
    def _(i):
        for h in range(3):
            p = 6 * i + 2 * h
            both = [xs[pl.ds(p + q, SIDE, stride=OWN), :] for q in range(2)]
            x = jnp.concatenate([jnp.where(v > LIMIT, 0.0, v) for v in both], axis=1).astype(BF)
            res = dot(fa[...], jnp.concatenate([x, x], axis=0))
            for q in range(2):
                base = pl.multiple_of((p + q) * ZSTEP, 8)
                z[pl.ds(base, 2 * HROWS), :] = res[:, q * SIDE : (q + 1) * SIDE]


def filter_row(z, cl, fw, mats, send=None):
    def rows(k):
        return pl.ds(k, OWN, stride=ZSTEP), pl.ds(k + HROWS, OWN, stride=ZSTEP)

    def one(k, value):
        base = jnp.concatenate(
            [fw[pl.ds(k, 8, stride=2 * HROWS), :], fw[pl.ds(k + HROWS, 8, stride=2 * HROWS), :]], axis=1
        )
        hi = base.astype(BF).astype(F32)
        fill = jnp.zeros((SIDE - 24, 2 * SIDE), F32)
        smooth = dot(cl[...], jnp.concatenate([hi, hi, base - hi, fill], axis=0).astype(BF))
        hi, lo = halves(value - smooth)

        def matrix(part):
            up = jnp.concatenate([mats[k, part], mats[k, 2 + part]], axis=1)
            down = jnp.concatenate([mats[k, 4 + part], mats[k, part]], axis=1)
            return jnp.concatenate([up, down], axis=0)

        both = dot(jnp.concatenate([hi, lo], axis=0), matrix(0))
        return both[:OWN] + both[OWN:] + dot(hi, matrix(1))

    def turn(i):
        values = []
        for j in range(BINS):
            real, imag = rows(i * BINS + j)
            values.append(jnp.concatenate([z[real, :], z[imag, :]], axis=1))
        values = [one(i * BINS + j, value) for j, value in enumerate(values)]
        for j, value in enumerate(values):
            real, imag = rows(i * BINS + j)
            z[real, :] = value[:, :SIDE]
            z[imag, :] = value[:, SIDE:]

    beside_bins(send, turn)


def channels_row(xs, z, last):
    quad = 4

    @pl.loop(0, OWN // (2 * quad))
    def _(i):
        for h in range(2):
            first = (2 * i + h) * quad
            cols = []
            for q in range(quad):
                base = pl.multiple_of((first + q) * ZSTEP, 8)
                cols.append(z[pl.ds(base, 2 * HROWS), :])
            out = dot_left(last, jnp.concatenate(cols, axis=1))
            for q in range(quad):
                xs[pl.ds(first + q, SIDE, stride=OWN), :] = out[:, q * SIDE : (q + 1) * SIDE]


TILES = NPIX // SIDE
FLAT = TILES * ROWS
REACH = FLAT + 8
PART = 4 * ROWS
PARTS = FLAT // PART
BLOCK = 8
BLOCKS = SIDE // BLOCK


def place():
    wide, narrow = lax.axis_index("wide"), lax.axis_index("narrow")
    return wide, narrow, wide * 4 + narrow


def columns(ref, row, device):
    slab = row * (NPIX // FLAT) + lax.div(device, 4)
    return ref.at[slab, pl.ds(pl.multiple_of(lax.rem(device, 4) * OWN, 16), OWN)]


def partner(i, j):
    wide, narrow, _ = place()
    x, y = lax.div(wide, 8), lax.rem(wide, 4)
    z = lax.rem(lax.div(wide, 4), 2) * 2 + lax.div(narrow, 2)
    step = (0, 2, 1, 3)[j % 4]
    x = lax.rem(x + step, 4)
    y = lax.rem(y + step + i % 4 if isinstance(i, int) else y + step + lax.rem(i, 4), 4)
    z = lax.rem(z + step + (i // 4 if isinstance(i, int) else lax.div(i, 4)), 4)
    core = lax.rem(lax.rem(narrow, 2) + j // 4, 2)
    return (x * 2 + lax.div(z, 2)) * 4 + y, lax.rem(z, 2) * 2 + core


def sender(row, source, target, send_sem, recv_sem):
    def send(i, j):
        wide, narrow = partner(i, j)
        pltpu.make_async_remote_copy(
            src_ref=source(wide * 4 + narrow),
            dst_ref=target,
            send_sem=send_sem.at[row],
            recv_sem=recv_sem.at[row],
            device_id=(wide, narrow),
            device_id_type=pl.DeviceIdType.MESH,
        ).start()

    return send


def send_all(send, beside=None):
    @pl.loop(1, 16)
    def _(i):
        for j in range(8):
            send(i, j)
        if beside is not None:
            beside(i)

    for j in range(1, 8):
        send(0, j)
    if beside is not None:
        beside(0)


def beside_bins(send, work):
    @pl.loop(0, KEPT // BINS)
    def _(t):
        if send is not None:
            for d in range(1, 4):
                for j in range(8):
                    send(3 * t + d, j)
        work(t)

    if send is not None:
        for j in range(1, 8):
            send(0, j)


def wait_all(row, buffer, sem):
    block = buffer.at[row, pl.ds(0, NDEV - 1)]
    pltpu.make_async_copy(block, block, sem.at[row]).wait()


def part_rows(part):
    return pl.ds(pl.multiple_of(part * PART, 16), PART)


def widen(landing, work, part):
    @pl.loop(0, SIDE // 32)
    def _(i):
        for k in range(32):
            c = i * 32 + k
            value = landing[c, part_rows(part), :]
            work[pl.ds(pl.multiple_of(c * REACH + part * PART, 8), PART), :] = value.astype(F32)


def narrow_down(leave, work, block):
    for k in range(BLOCK):
        c = block * BLOCK + k
        value = work[pl.ds(pl.multiple_of(c * REACH, 8), FLAT), :]
        leave[c] = value.astype(BF)


def turn_in(row, tile, work, marks, sent):
    block = work[pl.ds(tile * ROWS + row, SIDE, stride=REACH), :]
    turned = jnp.where(marks[0:1, :] > 0.0, FLAGGED, block.T).astype(BF)
    for h in range(2):
        place_at = tile * 2 + h
        slab = row * (NPIX // FLAT) + lax.div(place_at, 3)
        start = pl.multiple_of(lax.rem(place_at, 3) * (SIDE // 2), 16)
        sent[slab, pl.ds(start, SIDE // 2), :] = turned[h * (SIDE // 2) : (h + 1) * (SIDE // 2)]


def make_marks(flags, marks):
    lane = lax.broadcasted_iota(jnp.int32, (8, SIDE), 1)
    value = jnp.zeros((8, SIDE), F32)
    for f in range(SIDE // FLAGBLK):
        inside = (lane >= f * FLAGBLK) & (lane < (f + 1) * FLAGBLK)
        value = jnp.where(inside, flags[f].astype(F32), value)
    marks[...] = value


def make_taps(width, taps):
    w = jnp.broadcast_to(width[...], (8, SIDE))
    raw = [jnp.exp(-float((HALF - j) ** 2) / (2.0 * w * w)) for j in range(HALF + 1)]
    total = raw[HALF]
    for j in range(HALF):
        total = total + 2.0 * raw[j]
    for j in range(HALF + 1):
        taps[j] = raw[j] / total


def make_gain(line, gain):
    half = SIDE // 2

    def exact(a, b):
        return jnp.dot(a, b, preferred_element_type=F32, precision=lax.Precision.HIGHEST)

    low = jnp.concatenate([line[pl.ds(k * SIDE, SIDE)].reshape(1, SIDE) for k in range(half)], axis=0)
    low = jnp.concatenate([low, jnp.broadcast_to(line[pl.ds(half * SIDE, 1)].reshape(1, 1), (8, SIDE))], axis=0)
    row = lax.broadcasted_iota(jnp.int32, (half, HROWS), 0)
    col = lax.broadcasted_iota(jnp.int32, (half, HROWS), 1)
    first = lax.broadcasted_iota(jnp.int32, (SIDE, SIDE), 0)
    second = lax.broadcasted_iota(jnp.int32, (SIDE, SIDE), 1)
    turned = exact(jnp.where(row + col == half - 1, 1.0, 0.0), low)
    mirror = exact(turned, jnp.where(first + second == SIDE, 1.0, 0.0))
    edge = exact(jnp.where(row + col == half, 1.0, 0.0), low)
    lane = lax.broadcasted_iota(jnp.int32, (half, SIDE), 1)
    high = jnp.where(lane == 0, edge, mirror)
    gain[...] = jnp.concatenate([low[:half], high], axis=0).T[:HROWS] * (1.0 / NCHAN)


def beam_start(row, back, padded):
    padded[0:HALF, :] = jnp.zeros((HALF, SIDE), F32)
    padded[HALF + NPIX : NPIX + 2 * HALF, :] = jnp.zeros((HALF, SIDE), F32)

    @pl.loop(0, NPIX // FLAT)
    def _(i):
        at = pl.multiple_of(i * FLAT + HALF, 8)
        padded[pl.ds(at, FLAT), :] = back[row * (NPIX // FLAT) + i].astype(F32)


def beam_tile(row, tile, padded, taps, flat, work):
    at = tile * SIDE
    run = SIDE // 8
    values = [padded[pl.ds(at + t, 8, stride=run), :] for t in range(run + 2 * HALF)]
    for t in range(run):
        total = values[t + HALF] * taps[HALF]
        for j in range(HALF):
            total = total + (values[t + j] + values[t + 2 * HALF - j]) * taps[j]
        flat[pl.ds(t, 8, stride=run), :] = total


def beam_row(row, padded, taps, flats, work):
    @pl.loop(0, TILES // len(flats))
    def _(i):
        for q, flat in enumerate(flats):
            beam_tile(row, i * len(flats) + q, padded, taps, flat, work)
        for q, flat in enumerate(flats):
            tile = i * len(flats) + q
            work[pl.ds(tile * ROWS + row, SIDE, stride=REACH), :] = flat[...].T


def strip_kernel(
    cube, flags, line, width, fa_in, last_in, waves_in, turns_in, mix_in, full_in, plain_in, tiles, final, continuum,
    work, sent, got, back, padded, flat0, flat1, flat2, flat3, marks, taps, gain, hs, mats, xs, z, cl, fw, chol,
    shown, gathered, fa, last, waves, turns, mix, full, plain,
    in_sem, out_sem, table_sem, go_send, go_recv, home_send, home_recv, own_sem, fit_send, fit_recv,
):
    my_wide, my_narrow, me = place()
    tables_in = (fa_in, last_in, waves_in, turns_in, mix_in, full_in, plain_in)
    tables_at = (fa, last, waves, turns, mix, full, plain)

    def table(n):
        return pltpu.make_async_copy(tables_in[n], tables_at[n], table_sem.at[n])

    def cube_part(part):
        source = cube.at[:, part_rows(part), :]
        return pltpu.make_async_copy(source, back.at[:, part_rows(part), :], in_sem.at[part])

    def out_part(part):
        channels = pl.ds(part * BLOCK, BLOCK)
        return pltpu.make_async_copy(sent.at[channels], tiles.at[channels], out_sem.at[part])

    def home(row):
        return columns(back, row, me) if row < ROWS - 1 else columns(final, 0, me)

    def own_go(row):
        return pltpu.make_async_copy(columns(sent, row, me), got.at[row, me], own_sem.at[row])

    def own_home(row):
        return pltpu.make_async_copy(got.at[row, me], home(row), own_sem.at[ROWS + row])

    for part in range(PARTS):
        cube_part(part).start()
    for n in range(len(tables_in)):
        table(n).start()
    make_marks(flags, marks)

    @pl.loop(0, PARTS)
    def _(part):
        cube_part(part).wait()
        widen(back, work, part)
        for q in range(4):
            turn_in(0, part * 4 + q, work, marks, sent)

    for row in range(ROWS):
        def beside(i):
            for q in range(3):
                turn_in(row + 1, i * 3 + q, work, marks, sent)

        own_go(row).start()
        go = sender(row, lambda d, row=row: columns(sent, row, d), got.at[row, me], go_send, go_recv)
        if row < ROWS - 1:
            send_all(go, beside)

    for n in range(len(tables_in)):
        table(n).wait()
    make_gain(line, gain)
    make_taps(width, taps)
    make_matrices(gain, waves, turns, hs, mats, go)

    def fit_target(row):
        return row * (NDEV // ROWS) + me // ROWS

    def fit_remote(row):
        dest = fit_target(row)
        return pltpu.make_async_remote_copy(
            src_ref=shown.at[row],
            dst_ref=gathered.at[me % ROWS],
            send_sem=fit_send.at[row],
            recv_sem=fit_recv.at[me % ROWS],
            device_id=(dest // 4, dest % 4),
            device_id_type=pl.DeviceIdType.MESH,
        )

    def fit_local(row):
        return pltpu.make_async_copy(shown.at[row], gathered.at[me % ROWS], fit_send.at[row])

    back_home = None
    for row in range(ROWS):
        own_go(row).wait()
        wait_all(row, got, go_recv)
        rows = got.at[row]
        unpack_row(rows, xs)
        if row == 0:
            fit_setup(xs, full, plain, fw, chol)
        spectrum_row(xs, z, fa)
        shown[row] = fit_row(z, mix, chol, cl)
        filter_row(z, cl, fw, mats, back_home)
        channels_row(xs, z, last)

        @pl.loop(0, SIDE // 8)
        def _(i):
            pack_block(rows, i, xs)

        own_home(row).start()
        back_home = sender(row, lambda d, row=row: got.at[row, d], home(row), home_send, home_recv)
        if row == ROWS - 1:
            send_all(back_home)
        dest = fit_target(row)

        @pl.when(dest != me)
        def _():
            fit_remote(row).start()

        @pl.when(dest == me)
        def _():
            fit_local(row).start()

    for row in range(ROWS - 1):
        own_home(row).wait()
        wait_all(row, got, home_recv)
        beam_start(row, back, padded)
        beam_row(row, padded, taps, (flat0, flat1, flat2, flat3), work)

    for row in range(ROWS):
        wait_all(row, got, go_send)

    @pl.loop(0, BLOCKS)
    def _(part):
        narrow_down(sent, work, part)
        out_part(part).start()

    for row in range(ROWS):
        dest = fit_target(row)

        @pl.when(dest != me)
        def _():
            fit_remote(row).wait_send()

        @pl.when(dest == me)
        def _():
            fit_local(row).wait()

    for slot in range(ROWS):
        source = me % (NDEV // ROWS) * ROWS + slot

        @pl.when(source != me)
        def _():
            block = gathered.at[slot]
            pltpu.make_async_copy(block, block, fit_recv.at[slot]).wait()

    for slot in range(ROWS):
        continuum[slot * OWN : (slot + 1) * OWN, :] = gathered[slot]
    continuum[ROWS * OWN :, :] = jnp.zeros((2 * SIDE - ROWS * OWN, SIDE), F32)
    own_home(ROWS - 1).wait()
    wait_all(ROWS - 1, got, home_recv)
    for row in range(ROWS):
        wait_all(row, got, home_send)

    @pl.loop(0, BLOCKS)
    def _(part):
        out_part(part).wait()


def leave_kernel(
    tiles, final, width, coefs, restored, continuum,
    landing, leave, last_row, padded, flat0, flat1, flat2, flat3, work, taps, in_sem, out_sem, row_sem,
):
    def in_part(part):
        rows = part_rows(part)
        return pltpu.make_async_copy(tiles.at[:, rows, :], landing.at[:, rows, :], in_sem.at[part])

    def out_part(part):
        rows = part_rows(part)
        return pltpu.make_async_copy(leave.at[:, rows, :], restored.at[:, rows, :], out_sem.at[part])

    def row_part(n):
        slabs = pl.ds(n * 8, 8)
        return pltpu.make_async_copy(final.at[slabs], last_row.at[slabs], row_sem.at[n])

    for n in range(4):
        row_part(n).start()
    for part in range(PARTS):
        in_part(part).start()
    make_taps(width, taps)
    continuum[...] = coefs[...].T[:NBASIS, : ROWS * OWN]
    for n in range(4):
        row_part(n).wait()
    beam_start(0, last_row, padded)
    flats = (flat0, flat1, flat2, flat3)

    @pl.loop(0, PARTS)
    def _(part):
        for q, flat in enumerate(flats):
            beam_tile(0, part * 4 + q, padded, taps, flat, None)
        in_part(part).wait()

        @pl.loop(0, SIDE // 32)
        def _(i):
            for k in range(32):
                c = i * 32 + k
                value = landing[c, part_rows(part), :].astype(F32)
                work[pl.ds(pl.multiple_of(c * (PART + 8), 8), PART), :] = value

        for q, flat in enumerate(flats):
            work[pl.ds(q * ROWS + ROWS - 1, SIDE, stride=PART + 8), :] = flat[...].T

        @pl.loop(0, SIDE // 32)
        def _(i):
            for k in range(32):
                c = i * 32 + k
                value = work[pl.ds(pl.multiple_of(c * (PART + 8), 8), PART), :]
                leave[c, part_rows(part), :] = value.astype(BF)

        out_part(part).start()

    @pl.loop(0, PARTS)
    def _(part):
        out_part(part).wait()


def params(**more):
    return pltpu.CompilerParams(vmem_limit_bytes=VMEM_BYTES, **more)


def body(cube, flags, line_gain, beam_width):
    tab = tables()
    names = ("fa", "last", "waves", "turns", "mix", "full", "plain")
    ins = [jnp.asarray(tab[n]) for n in names]
    width = beam_width[None, :]
    dma = pltpu.SemaphoreType.DMA
    vmem = pltpu.VMEM
    hbm = pl.BlockSpec(memory_space=pl.ANY)
    near = pl.BlockSpec(memory_space=vmem)
    slabs = (SIDE, FLAT, SIDE)
    row_slabs = (NPIX // FLAT, FLAT, SIDE)
    flat_tile = [vmem((SIDE, SIDE), F32)] * 4
    flat = cube.reshape(SIDE, ROWS, TILES, SIDE).transpose(0, 2, 1, 3).reshape(slabs)
    tiles, final, coefs = pl.pallas_call(
        strip_kernel,
        in_specs=[hbm, pl.BlockSpec(memory_space=pltpu.SMEM), near, near] + [hbm] * len(ins),
        out_specs=[hbm, hbm, near],
        out_shape=[
            jax.ShapeDtypeStruct(slabs, BF),
            jax.ShapeDtypeStruct(row_slabs, BF),
            jax.ShapeDtypeStruct((2 * SIDE, SIDE), F32),
        ],
        scratch_shapes=[
            vmem((SIDE * REACH, SIDE), F32),
            vmem(slabs, BF),
            vmem((ROWS, NDEV, OWN, SIDE), BF),
            vmem(slabs, BF),
            vmem((NPIX + 2 * HALF, SIDE), F32),
            *flat_tile,
            vmem((8, SIDE), F32),
            vmem((HALF + 1, 8, SIDE), F32),
            vmem((HROWS, SIDE), F32),
            vmem((2, HROWS, 2 * SIDE), F32),
            vmem((KEPT, 6, SIDE, SIDE), BF),
            vmem((SIDE * OWN, SIDE), F32),
            vmem((OWN * ZSTEP, SIDE), F32),
            vmem((OWN, SIDE), BF),
            vmem(((NBASIS + 2) * 2 * HROWS, SIDE), F32),
            vmem((NBASIS * NBASIS, 8, SIDE), F32),
            vmem((ROWS, OWN, SIDE), F32),
            vmem((ROWS, OWN, SIDE), F32),
            *[vmem(t.shape, t.dtype) for t in ins],
            dma((PARTS,)),
            dma((BLOCKS,)),
            dma((len(ins),)),
            dma((ROWS,)),
            dma((ROWS,)),
            dma((ROWS,)),
            dma((ROWS,)),
            dma((2 * ROWS,)),
            dma((ROWS,)),
            dma((ROWS,)),
        ],
        compiler_params=params(has_side_effects=True),
    )(flat, flags, line_gain, width, *ins)
    restored, continuum = pl.pallas_call(
        leave_kernel,
        in_specs=[hbm, hbm, near, near],
        out_specs=[hbm, near],
        out_shape=[
            jax.ShapeDtypeStruct(slabs, BF),
            jax.ShapeDtypeStruct((NBASIS, ROWS * OWN), F32),
        ],
        scratch_shapes=[
            vmem(slabs, BF),
            vmem(slabs, BF),
            vmem(row_slabs, BF),
            vmem((NPIX + 2 * HALF, SIDE), F32),
            *flat_tile,
            vmem((SIDE * (PART + 8), SIDE), F32),
            vmem((HALF + 1, 8, SIDE), F32),
            dma((PARTS,)),
            dma((PARTS,)),
            dma((4,)),
        ],
        compiler_params=params(),
    )(tiles, final, width, coefs)
    restored = restored.reshape(SIDE, TILES, ROWS, SIDE).transpose(0, 2, 1, 3).reshape(SIDE, ROWS, NPIX)
    return (restored, continuum)


def solution(mesh):
    placed = (P(AXES, None, None), P(AXES), P(), P(AXES))
    return jax.shard_map(
        body,
        mesh=mesh,
        in_specs=placed,
        out_specs=(P(AXES, None, None), P(None, AXES)),
        check_vma=False,
    )
```

```python
import functools
import math

import jax
import jax.numpy as jnp
import numpy as np
from jax import lax
from jax.experimental import pallas as pl
from jax.experimental.pallas import tpu as pltpu
from jax.sharding import PartitionSpec as P

NDEV = 128
NBASIS = 6
HALF = 8
FLAGBLK = 16
ROWS = 4
NPIX = 6144
NCHAN = 16384
SIDE = 128
HROWS = 72
OWN = NPIX // NDEV
ZSTEP = 2 * HROWS + 8
KEPT = SIDE // 2 + 1
BINS = 13
FLAGGED = 128.0
LIMIT = 100.0
BF = jnp.bfloat16
F32 = jnp.float32
VMEM_BYTES = 61 * 1024 * 1024
AXES = ("wide", "narrow")


def split3(x):
    hi = x.astype(BF)
    rest = x - hi.astype(np.float64)
    lo = rest.astype(BF)
    return hi, lo, (rest - lo.astype(np.float64)).astype(BF)


def legendre64(x):
    terms = [np.ones_like(x), x]
    for k in range(1, NBASIS - 1):
        terms.append(((2 * k + 1) * x * terms[k] - k * terms[k - 1]) / (k + 1))
    return np.stack(terms[:NBASIS])


@functools.cache
def tables():
    idx = np.arange(SIDE)
    turn = 2.0 * np.pi / SIDE
    half = SIDE // 2 + 1
    cos = np.cos(turn * (np.outer(idx, idx) % SIDE))
    sin = np.sin(turn * (np.outer(idx, idx) % SIDE))
    first = np.zeros((2 * HROWS, SIDE))
    first[:half] = cos[:half]
    first[HROWS : HROWS + half] = -sin[:half]
    plain = first.astype(np.float32)
    slow = legendre64((2.0 * idx + 1.0) / SIDE - 1.0)
    first[half : half + NBASIS] = slow
    fa_hi, fa_lo, fa_rest = split3(first)
    fa_hi = fa_hi.copy()
    fa_hi[HROWS + half : HROWS + half + NBASIS] = fa_rest[half : half + NBASIS]
    chan = np.arange(NCHAN)
    full = legendre64((2.0 * chan + 1.0) / NCHAN - 1.0).reshape(NBASIS, SIDE, SIDE)
    fit = np.linalg.pinv(slow.T)
    mix = np.einsum("ma,kab->kmb", fit, full)
    mix = np.where(np.arange(NBASIS)[None, :, None] <= np.arange(NBASIS)[:, None, None], mix, 0.0)
    times = np.full((half,), 2.0)
    times[0] = times[-1] = 1.0
    last = np.zeros((SIDE, 2 * HROWS))
    last[:, :half] = cos[:, :half] * times
    last[:, HROWS : HROWS + half] = -sin[:, :half] * times
    shift = np.arange(2 * SIDE) - SIDE
    turn_c = np.zeros((HROWS, 2 * SIDE))
    turn_s = np.zeros((HROWS, 2 * SIDE))
    turn_c[:half] = np.cos(2.0 * np.pi / NCHAN * np.outer(idx[:half], shift))
    turn_s[:half] = np.sin(2.0 * np.pi / NCHAN * np.outer(idx[:half], shift))
    l_hi, l_lo, _ = split3(last)
    f = np.float32
    return dict(
        fa=np.concatenate([fa_hi, fa_lo], axis=1), plain=plain, full=full.astype(f), mix=mix.astype(f),
        last=np.concatenate([l_hi, l_lo, l_hi], axis=1),
        waves=np.stack([cos, sin]).astype(f), turns=np.stack([turn_c, turn_s]).astype(f),
    )


def dot(a, b):
    return jnp.dot(a, b, preferred_element_type=F32)


def halves(x):
    hi = x.astype(BF)
    return hi, (x - hi.astype(F32)).astype(BF)


def dot_left(table, x):
    hi, lo = halves(x)
    return dot(table[...], jnp.concatenate([hi, hi, lo], axis=0))


def unpack_row(src, xs):
    @pl.loop(0, SIDE // 8)
    def _(i):
        block = src[pl.ds(i * 8, 8), :, :].astype(F32)
        xs[pl.ds(pl.multiple_of(i * 8 * OWN, 128), 8 * OWN), :] = block.reshape(8 * OWN, SIDE)


def pack_block(dst, i, xs):
    block = xs[pl.ds(pl.multiple_of(i * 8 * OWN, 128), 8 * OWN), :]
    dst[pl.ds(i * 8, 8), :, :] = block.reshape(8, OWN, SIDE).astype(BF)


def fit_setup(xs, full, plain, fw, chol):
    weight = jnp.where(xs[pl.ds(0, SIDE, stride=OWN), :] > LIMIT, 0.0, 1.0)
    gram = {}
    fw[NBASIS * 2 * HROWS :, :] = jnp.zeros((2 * 2 * HROWS, SIDE), F32)
    for i in range(NBASIS):
        weighted = full[i] * weight
        fw[i * 2 * HROWS : (i + 1) * 2 * HROWS, :] = jnp.dot(plain[...], weighted, preferred_element_type=F32, precision=lax.Precision.HIGHEST)
        for j in range(i + 1):
            total = jnp.sum(jnp.sum(weighted * full[j], axis=0, keepdims=True), axis=1, keepdims=True)
            gram[i, j] = jnp.broadcast_to(total, (8, SIDE))
    factor = {}
    for j in range(NBASIS):
        value = gram[j, j]
        for k in range(j):
            value = value - factor[j, k] * factor[j, k]
        factor[j, j] = jnp.sqrt(value)
        for i in range(j + 1, NBASIS):
            value = gram[i, j]
            for k in range(j):
                value = value - factor[i, k] * factor[j, k]
            factor[i, j] = value / factor[j, j]
    for (i, j), value in factor.items():
        chol[i * NBASIS + j] = value


def make_matrices(gain, waves, turns, hs, mats, send=None):
    def exact(a, b):
        return jnp.dot(a, b, preferred_element_type=F32, precision=lax.Precision.HIGHEST)

    real, imag = exact(gain[...], waves[0]), exact(gain[...], waves[1])
    real, imag = jnp.concatenate([real, real], axis=1), jnp.concatenate([imag, imag], axis=1)
    hs[0] = real * turns[0] - imag * turns[1]
    hs[1] = real * turns[1] + imag * turns[0]

    def one(k):
        for part in range(2):
            rows = jnp.broadcast_to(hs[part, pl.ds(k, 1), :], (SIDE, 2 * SIDE))
            matrix = pltpu.roll(rows, 0, 1, stride=1, stride_axis=0)[:, SIDE:]
            hi, lo = halves(matrix)
            mats[k, 2 * part] = hi
            mats[k, 2 * part + 1] = lo
            if part == 1:
                mats[k, 4] = -hi
                mats[k, 5] = -lo

    def turn(t):
        for j in range(BINS):
            one(t * BINS + j)

    beside_bins(send, turn)


def fit_row(z, mix, chol, cl):
    parts = []
    for m in range(NBASIS):
        main = z[pl.ds(KEPT + m, OWN, stride=ZSTEP), :]
        parts.append(main + z[pl.ds(HROWS + KEPT + m, OWN, stride=ZSTEP), :])

    def entry(i, j):
        return jnp.broadcast_to(chol[i * NBASIS + j, 0:1, :], (OWN, SIDE))

    inner = []
    for k in range(NBASIS):
        total = parts[0] * mix[k, 0:1, :]
        for m in range(1, k + 1):
            total = total + parts[m] * mix[k, m : m + 1, :]
        value = jnp.broadcast_to(jnp.sum(total, axis=1, keepdims=True), (OWN, SIDE))
        for j in range(k):
            value = value - entry(k, j) * inner[j]
        inner.append(value / entry(k, k))
    result = [None] * NBASIS
    for i in reversed(range(NBASIS)):
        value = inner[i]
        for j in range(i + 1, NBASIS):
            value = value - entry(j, i) * result[j]
        result[i] = value / entry(i, i)
    lane = lax.broadcasted_iota(jnp.int32, (OWN, SIDE), 1)
    shown = jnp.zeros((OWN, SIDE), F32)
    parts = jnp.zeros((OWN, SIDE), F32)
    for k in range(NBASIS):
        hi = result[k].astype(BF).astype(F32)
        shown = jnp.where(lane == k, result[k], shown)
        parts = jnp.where((lane == k) | (lane == 16 + k), hi, parts)
        parts = jnp.where(lane == 8 + k, result[k] - hi, parts)
    cl[...] = parts.astype(BF)
    return shown


def spectrum_row(xs, z, fa):
    @pl.loop(0, 8)
    def _(i):
        for h in range(3):
            p = 6 * i + 2 * h
            both = [xs[pl.ds(p + q, SIDE, stride=OWN), :] for q in range(2)]
            x = jnp.concatenate([jnp.where(v > LIMIT, 0.0, v) for v in both], axis=1).astype(BF)
            res = dot(fa[...], jnp.concatenate([x, x], axis=0))
            for q in range(2):
                base = pl.multiple_of((p + q) * ZSTEP, 8)
                z[pl.ds(base, 2 * HROWS), :] = res[:, q * SIDE : (q + 1) * SIDE]


def filter_row(z, cl, fw, mats, send=None):
    def rows(k):
        return pl.ds(k, OWN, stride=ZSTEP), pl.ds(k + HROWS, OWN, stride=ZSTEP)

    def one(k, value):
        base = jnp.concatenate(
            [fw[pl.ds(k, 8, stride=2 * HROWS), :], fw[pl.ds(k + HROWS, 8, stride=2 * HROWS), :]], axis=1
        )
        hi = base.astype(BF).astype(F32)
        fill = jnp.zeros((SIDE - 24, 2 * SIDE), F32)
        smooth = dot(cl[...], jnp.concatenate([hi, hi, base - hi, fill], axis=0).astype(BF))
        hi, lo = halves(value - smooth)

        def matrix(part):
            up = jnp.concatenate([mats[k, part], mats[k, 2 + part]], axis=1)
            down = jnp.concatenate([mats[k, 4 + part], mats[k, part]], axis=1)
            return jnp.concatenate([up, down], axis=0)

        both = dot(jnp.concatenate([hi, lo], axis=0), matrix(0))
        return both[:OWN] + both[OWN:] + dot(hi, matrix(1))

    def turn(i):
        values = []
        for j in range(BINS):
            real, imag = rows(i * BINS + j)
            values.append(jnp.concatenate([z[real, :], z[imag, :]], axis=1))
        values = [one(i * BINS + j, value) for j, value in enumerate(values)]
        for j, value in enumerate(values):
            real, imag = rows(i * BINS + j)
            z[real, :] = value[:, :SIDE]
            z[imag, :] = value[:, SIDE:]

    beside_bins(send, turn)


def channels_row(xs, z, last):
    quad = 4

    @pl.loop(0, OWN // (2 * quad))
    def _(i):
        for h in range(2):
            first = (2 * i + h) * quad
            cols = []
            for q in range(quad):
                base = pl.multiple_of((first + q) * ZSTEP, 8)
                cols.append(z[pl.ds(base, 2 * HROWS), :])
            out = dot_left(last, jnp.concatenate(cols, axis=1))
            for q in range(quad):
                xs[pl.ds(first + q, SIDE, stride=OWN), :] = out[:, q * SIDE : (q + 1) * SIDE]


TILES = NPIX // SIDE
FLAT = TILES * ROWS
REACH = FLAT + 8
PART = 4 * ROWS
PARTS = FLAT // PART
BLOCK = 8
BLOCKS = SIDE // BLOCK


def place():
    wide, narrow = lax.axis_index("wide"), lax.axis_index("narrow")
    return wide, narrow, wide * 4 + narrow


def columns(ref, row, device):
    slab = row * (NPIX // FLAT) + lax.div(device, 4)
    return ref.at[slab, pl.ds(pl.multiple_of(lax.rem(device, 4) * OWN, 16), OWN)]


def partner(i, j):
    wide, narrow, _ = place()
    x, y = lax.div(wide, 8), lax.rem(wide, 4)
    z = lax.rem(lax.div(wide, 4), 2) * 2 + lax.div(narrow, 2)
    step = (0, 2, 1, 3)[j % 4]
    x = lax.rem(x + step, 4)
    y = lax.rem(y + step + i % 4 if isinstance(i, int) else y + step + lax.rem(i, 4), 4)
    z = lax.rem(z + step + (i // 4 if isinstance(i, int) else lax.div(i, 4)), 4)
    core = lax.rem(lax.rem(narrow, 2) + j // 4, 2)
    return (x * 2 + lax.div(z, 2)) * 4 + y, lax.rem(z, 2) * 2 + core


def sender(row, source, target, send_sem, recv_sem):
    def send(i, j):
        wide, narrow = partner(i, j)
        pltpu.make_async_remote_copy(
            src_ref=source(wide * 4 + narrow),
            dst_ref=target,
            send_sem=send_sem.at[row],
            recv_sem=recv_sem.at[row],
            device_id=(wide, narrow),
            device_id_type=pl.DeviceIdType.MESH,
        ).start()

    return send


def send_all(send, beside=None):
    @pl.loop(1, 16)
    def _(i):
        for j in range(8):
            send(i, j)
        if beside is not None:
            beside(i)

    for j in range(1, 8):
        send(0, j)
    if beside is not None:
        beside(0)


def beside_bins(send, work):
    @pl.loop(0, KEPT // BINS)
    def _(t):
        if send is not None:
            for d in range(1, 4):
                for j in range(8):
                    send(3 * t + d, j)
        work(t)

    if send is not None:
        for j in range(1, 8):
            send(0, j)


def wait_all(row, buffer, sem):
    block = buffer.at[row, pl.ds(0, NDEV - 1)]
    pltpu.make_async_copy(block, block, sem.at[row]).wait()


def part_rows(part):
    return pl.ds(pl.multiple_of(part * PART, 16), PART)


def widen(landing, work, part):
    @pl.loop(0, SIDE // 32)
    def _(i):
        for k in range(32):
            c = i * 32 + k
            value = landing[c, part_rows(part), :]
            work[pl.ds(pl.multiple_of(c * REACH + part * PART, 8), PART), :] = value.astype(F32)


def narrow_down(leave, work, block):
    for k in range(BLOCK):
        c = block * BLOCK + k
        value = work[pl.ds(pl.multiple_of(c * REACH, 8), FLAT), :]
        leave[c] = value.astype(BF)


def turn_in(row, tile, work, marks, sent):
    block = work[pl.ds(tile * ROWS + row, SIDE, stride=REACH), :]
    turned = jnp.where(marks[0:1, :] > 0.0, FLAGGED, block.T).astype(BF)
    for h in range(2):
        place_at = tile * 2 + h
        slab = row * (NPIX // FLAT) + lax.div(place_at, 3)
        start = pl.multiple_of(lax.rem(place_at, 3) * (SIDE // 2), 16)
        sent[slab, pl.ds(start, SIDE // 2), :] = turned[h * (SIDE // 2) : (h + 1) * (SIDE // 2)]


def make_marks(flags, marks):
    lane = lax.broadcasted_iota(jnp.int32, (8, SIDE), 1)
    value = jnp.zeros((8, SIDE), F32)
    for f in range(SIDE // FLAGBLK):
        inside = (lane >= f * FLAGBLK) & (lane < (f + 1) * FLAGBLK)
        value = jnp.where(inside, flags[f].astype(F32), value)
    marks[...] = value


def make_taps(width, taps):
    w = jnp.broadcast_to(width[...], (8, SIDE))
    raw = [jnp.exp(-float((HALF - j) ** 2) / (2.0 * w * w)) for j in range(HALF + 1)]
    total = raw[HALF]
    for j in range(HALF):
        total = total + 2.0 * raw[j]
    for j in range(HALF + 1):
        taps[j] = raw[j] / total


def make_gain(line, gain):
    half = SIDE // 2

    def exact(a, b):
        return jnp.dot(a, b, preferred_element_type=F32, precision=lax.Precision.HIGHEST)

    low = jnp.concatenate([line[pl.ds(k * SIDE, SIDE)].reshape(1, SIDE) for k in range(half)], axis=0)
    low = jnp.concatenate([low, jnp.broadcast_to(line[pl.ds(half * SIDE, 1)].reshape(1, 1), (8, SIDE))], axis=0)
    row = lax.broadcasted_iota(jnp.int32, (half, HROWS), 0)
    col = lax.broadcasted_iota(jnp.int32, (half, HROWS), 1)
    first = lax.broadcasted_iota(jnp.int32, (SIDE, SIDE), 0)
    second = lax.broadcasted_iota(jnp.int32, (SIDE, SIDE), 1)
    turned = exact(jnp.where(row + col == half - 1, 1.0, 0.0), low)
    mirror = exact(turned, jnp.where(first + second == SIDE, 1.0, 0.0))
    edge = exact(jnp.where(row + col == half, 1.0, 0.0), low)
    lane = lax.broadcasted_iota(jnp.int32, (half, SIDE), 1)
    high = jnp.where(lane == 0, edge, mirror)
    gain[...] = jnp.concatenate([low[:half], high], axis=0).T[:HROWS] * (1.0 / NCHAN)


def beam_start(row, back, padded):
    padded[0:HALF, :] = jnp.zeros((HALF, SIDE), F32)
    padded[HALF + NPIX : NPIX + 2 * HALF, :] = jnp.zeros((HALF, SIDE), F32)

    @pl.loop(0, NPIX // FLAT)
    def _(i):
        at = pl.multiple_of(i * FLAT + HALF, 8)
        padded[pl.ds(at, FLAT), :] = back[row * (NPIX // FLAT) + i].astype(F32)


def beam_tile(row, tile, padded, taps, flat, work):
    at = tile * SIDE
    run = SIDE // 8
    values = [padded[pl.ds(at + t, 8, stride=run), :] for t in range(run + 2 * HALF)]
    for t in range(run):
        total = values[t + HALF] * taps[HALF]
        for j in range(HALF):
            total = total + (values[t + j] + values[t + 2 * HALF - j]) * taps[j]
        flat[pl.ds(t, 8, stride=run), :] = total


def beam_row(row, padded, taps, flats, work):
    @pl.loop(0, TILES // len(flats))
    def _(i):
        for q, flat in enumerate(flats):
            beam_tile(row, i * len(flats) + q, padded, taps, flat, work)
        for q, flat in enumerate(flats):
            tile = i * len(flats) + q
            work[pl.ds(tile * ROWS + row, SIDE, stride=REACH), :] = flat[...].T
            if row == ROWS - 2:
                work[pl.ds(tile * ROWS + ROWS - 1, SIDE, stride=REACH), :] = jnp.zeros((SIDE, SIDE), F32)


def strip_kernel(
    cube, flags, line, width, fa_in, last_in, waves_in, turns_in, mix_in, full_in, plain_in, tiles, final, continuum,
    work, sent, got, back, padded, flat0, flat1, flat2, flat3, marks, taps, gain, hs, mats, xs, z, cl, fw, chol,
    shown, gathered, fa, last, waves, turns, mix, full, plain,
    in_sem, out_sem, table_sem, go_send, go_recv, home_send, home_recv, own_sem, fit_send, fit_recv,
):
    my_wide, my_narrow, me = place()
    tables_in = (fa_in, last_in, waves_in, turns_in, mix_in, full_in, plain_in)
    tables_at = (fa, last, waves, turns, mix, full, plain)

    def table(n):
        return pltpu.make_async_copy(tables_in[n], tables_at[n], table_sem.at[n])

    def cube_part(part):
        source = cube.at[:, part_rows(part), :]
        return pltpu.make_async_copy(source, back.at[:, part_rows(part), :], in_sem.at[part])

    def out_part(part):
        channels = pl.ds(part * BLOCK, BLOCK)
        return pltpu.make_async_copy(sent.at[channels], tiles.at[channels], out_sem.at[part])

    def home(row):
        return columns(back, row, me) if row < ROWS - 1 else columns(final, 0, me)

    def own_go(row):
        return pltpu.make_async_copy(columns(sent, row, me), got.at[row, me], own_sem.at[row])

    def own_home(row):
        return pltpu.make_async_copy(got.at[row, me], home(row), own_sem.at[ROWS + row])

    for part in range(PARTS):
        cube_part(part).start()
    for n in range(len(tables_in)):
        table(n).start()
    make_marks(flags, marks)

    @pl.loop(0, PARTS)
    def _(part):
        cube_part(part).wait()
        widen(back, work, part)
        for q in range(4):
            turn_in(0, part * 4 + q, work, marks, sent)

    for row in range(ROWS):
        def beside(i):
            for q in range(3):
                turn_in(row + 1, i * 3 + q, work, marks, sent)

        own_go(row).start()
        go = sender(row, lambda d, row=row: columns(sent, row, d), got.at[row, me], go_send, go_recv)
        if row < ROWS - 1:
            send_all(go, beside)

    for n in range(len(tables_in)):
        table(n).wait()
    make_gain(line, gain)
    make_taps(width, taps)
    make_matrices(gain, waves, turns, hs, mats, go)

    def fit_target(row):
        return row * (NDEV // ROWS) + me // ROWS

    def fit_remote(row):
        dest = fit_target(row)
        return pltpu.make_async_remote_copy(
            src_ref=shown.at[row],
            dst_ref=gathered.at[me % ROWS],
            send_sem=fit_send.at[row],
            recv_sem=fit_recv.at[me % ROWS],
            device_id=(dest // 4, dest % 4),
            device_id_type=pl.DeviceIdType.MESH,
        )

    def fit_local(row):
        return pltpu.make_async_copy(shown.at[row], gathered.at[me % ROWS], fit_send.at[row])

    back_home = None
    for row in range(ROWS):
        own_go(row).wait()
        wait_all(row, got, go_recv)
        rows = got.at[row]
        unpack_row(rows, xs)
        if row == 0:
            fit_setup(xs, full, plain, fw, chol)
        spectrum_row(xs, z, fa)
        shown[row] = fit_row(z, mix, chol, cl)
        filter_row(z, cl, fw, mats, back_home)
        channels_row(xs, z, last)

        @pl.loop(0, SIDE // 8)
        def _(i):
            pack_block(rows, i, xs)

        own_home(row).start()
        back_home = sender(row, lambda d, row=row: got.at[row, d], home(row), home_send, home_recv)
        if row == ROWS - 1:
            send_all(back_home)
        dest = fit_target(row)

        @pl.when(dest != me)
        def _():
            fit_remote(row).start()

        @pl.when(dest == me)
        def _():
            fit_local(row).start()

    for row in range(ROWS - 1):
        own_home(row).wait()
        wait_all(row, got, home_recv)
        beam_start(row, back, padded)
        beam_row(row, padded, taps, (flat0, flat1, flat2, flat3), work)

    for row in range(ROWS):
        wait_all(row, got, go_send)

    @pl.loop(0, BLOCKS)
    def _(part):
        narrow_down(sent, work, part)
        out_part(part).start()

    for row in range(ROWS):
        dest = fit_target(row)

        @pl.when(dest != me)
        def _():
            fit_remote(row).wait_send()

        @pl.when(dest == me)
        def _():
            fit_local(row).wait()

    for slot in range(ROWS):
        source = me % (NDEV // ROWS) * ROWS + slot

        @pl.when(source != me)
        def _():
            block = gathered.at[slot]
            pltpu.make_async_copy(block, block, fit_recv.at[slot]).wait()

    for slot in range(ROWS):
        continuum[slot * OWN : (slot + 1) * OWN, :] = gathered[slot]
    continuum[ROWS * OWN :, :] = jnp.zeros((2 * SIDE - ROWS * OWN, SIDE), F32)
    own_home(ROWS - 1).wait()
    wait_all(ROWS - 1, got, home_recv)
    for row in range(ROWS):
        wait_all(row, got, home_send)

    @pl.loop(0, BLOCKS)
    def _(part):
        out_part(part).wait()


def leave_kernel(
    tiles, final, width, coefs, restored, continuum,
    landing, leave, last_row, padded, flat0, flat1, flat2, flat3, work, taps, in_sem, out_sem, row_sem,
):
    def in_part(part):
        rows = part_rows(part)
        return pltpu.make_async_copy(tiles.at[:, rows, :], landing.at[:, rows, :], in_sem.at[part])

    def out_part(part):
        rows = part_rows(part)
        return pltpu.make_async_copy(leave.at[:, rows, :], restored.at[:, rows, :], out_sem.at[part])

    def row_part(n):
        slabs = pl.ds(n * 8, 8)
        return pltpu.make_async_copy(final.at[slabs], last_row.at[slabs], row_sem.at[n])

    for n in range(4):
        row_part(n).start()
    for part in range(PARTS):
        in_part(part).start()
    make_taps(width, taps)
    continuum[...] = coefs[...].T[:NBASIS, : ROWS * OWN]
    work[...] = jnp.zeros(work.shape, F32)
    padded[0:HALF, :] = jnp.zeros((HALF, SIDE), F32)
    padded[HALF + NPIX : NPIX + 2 * HALF, :] = jnp.zeros((HALF, SIDE), F32)
    for n in range(4):
        row_part(n).wait()

        @pl.loop(n * 8, n * 8 + 8)
        def _(i):
            at = pl.multiple_of(i * FLAT + HALF, 8)
            padded[pl.ds(at, FLAT), :] = last_row[i].astype(F32)

    flats = (flat0, flat1, flat2, flat3)

    def beams(part):
        for q, flat in enumerate(flats):
            beam_tile(0, part * 4 + q, padded, taps, flat, None)

    beams(0)

    @pl.loop(0, PARTS)
    def _(part):
        in_part(part).wait()
        for q, flat in enumerate(flats):
            work[pl.ds(q * ROWS + ROWS - 1, SIDE, stride=PART + 8), :] = flat[...].T
        beams(lax.min(part + 1, PARTS - 1))
        for c in range(SIDE):
            value = work[c * (PART + 8) : c * (PART + 8) + PART, :].astype(BF)
            leave[c, part_rows(part), :] = landing[c, part_rows(part), :] + value
        out_part(part).start()

    @pl.loop(0, PARTS)
    def _(part):
        out_part(part).wait()


def params(**more):
    return pltpu.CompilerParams(vmem_limit_bytes=VMEM_BYTES, **more)


def body(cube, flags, line_gain, beam_width):
    tab = tables()
    names = ("fa", "last", "waves", "turns", "mix", "full", "plain")
    ins = [jnp.asarray(tab[n]) for n in names]
    width = beam_width[None, :]
    dma = pltpu.SemaphoreType.DMA
    vmem = pltpu.VMEM
    hbm = pl.BlockSpec(memory_space=pl.ANY)
    near = pl.BlockSpec(memory_space=vmem)
    slabs = (SIDE, FLAT, SIDE)
    row_slabs = (NPIX // FLAT, FLAT, SIDE)
    flat_tile = [vmem((SIDE, SIDE), F32)] * 4
    flat = cube.reshape(SIDE, ROWS, TILES, SIDE).transpose(0, 2, 1, 3).reshape(slabs)
    tiles, final, coefs = pl.pallas_call(
        strip_kernel,
        in_specs=[hbm, pl.BlockSpec(memory_space=pltpu.SMEM), near, near] + [hbm] * len(ins),
        out_specs=[hbm, hbm, near],
        out_shape=[
            jax.ShapeDtypeStruct(slabs, BF),
            jax.ShapeDtypeStruct(row_slabs, BF),
            jax.ShapeDtypeStruct((2 * SIDE, SIDE), F32),
        ],
        scratch_shapes=[
            vmem((SIDE * REACH, SIDE), F32),
            vmem(slabs, BF),
            vmem((ROWS, NDEV, OWN, SIDE), BF),
            vmem(slabs, BF),
            vmem((NPIX + 2 * HALF, SIDE), F32),
            *flat_tile,
            vmem((8, SIDE), F32),
            vmem((HALF + 1, 8, SIDE), F32),
            vmem((HROWS, SIDE), F32),
            vmem((2, HROWS, 2 * SIDE), F32),
            vmem((KEPT, 6, SIDE, SIDE), BF),
            vmem((SIDE * OWN, SIDE), F32),
            vmem((OWN * ZSTEP, SIDE), F32),
            vmem((OWN, SIDE), BF),
            vmem(((NBASIS + 2) * 2 * HROWS, SIDE), F32),
            vmem((NBASIS * NBASIS, 8, SIDE), F32),
            vmem((ROWS, OWN, SIDE), F32),
            vmem((ROWS, OWN, SIDE), F32),
            *[vmem(t.shape, t.dtype) for t in ins],
            dma((PARTS,)),
            dma((BLOCKS,)),
            dma((len(ins),)),
            dma((ROWS,)),
            dma((ROWS,)),
            dma((ROWS,)),
            dma((ROWS,)),
            dma((2 * ROWS,)),
            dma((ROWS,)),
            dma((ROWS,)),
        ],
        compiler_params=params(has_side_effects=True),
    )(flat, flags, line_gain, width, *ins)
    restored, continuum = pl.pallas_call(
        leave_kernel,
        in_specs=[hbm, hbm, near, near],
        out_specs=[hbm, near],
        out_shape=[
            jax.ShapeDtypeStruct(slabs, BF),
            jax.ShapeDtypeStruct((NBASIS, ROWS * OWN), F32),
        ],
        scratch_shapes=[
            vmem(slabs, BF),
            vmem(slabs, BF),
            vmem(row_slabs, BF),
            vmem((NPIX + 2 * HALF, SIDE), F32),
            *flat_tile,
            vmem((SIDE * (PART + 8), SIDE), F32),
            vmem((HALF + 1, 8, SIDE), F32),
            dma((PARTS,)),
            dma((PARTS,)),
            dma((4,)),
        ],
        compiler_params=params(),
    )(tiles, final, width, coefs)
    restored = restored.reshape(SIDE, TILES, ROWS, SIDE).transpose(0, 2, 1, 3).reshape(SIDE, ROWS, NPIX)
    return (restored, continuum)


def solution(mesh):
    placed = (P(AXES, None, None), P(AXES), P(), P(AXES))
    return jax.shard_map(
        body,
        mesh=mesh,
        in_specs=placed,
        out_specs=(P(AXES, None, None), P(None, AXES)),
        check_vma=False,
    )
```
